32 devices in a mesh: dp: 32 (over z, y, x, core).
Axes of the slice: x: 2, y: 2, z: 4, core: 2. Of those that a mesh axis runs over, the one named last changes fastest.
Arguments:
- tokens: bfloat16 [32768, 768], P('dp'), may hold values from -6 to 6
- lengths: int32 [64], P('dp'), may hold values from 16 to 512, as said below
- groups: int32 [64], replicated, may hold values from 0 to 63, as said below
- query_weight: bfloat16 [768, 768], replicated, may hold values from -0.21875 to 0.21875
- query_bias: float32 [768], replicated, may hold values from -1.2 to 1.2
- key_weight: bfloat16 [768, 768], replicated, may hold values from -0.21875 to 0.21875
- value_weight: bfloat16 [768, 768], replicated, may hold values from -0.21875 to 0.21875
- value_bias: float32 [768], replicated, may hold values from -1.2 to 1.2
- output_weight: bfloat16 [768, 768], replicated, may hold values from -1.25 to 1.25
- output_bias: float32 [768], replicated, may hold values from -1.2 to 1.2
- first_gain: float32 [768], replicated, may hold values from 0.5 to 1.5
- first_shift: float32 [768], replicated, may hold values from -1.2 to 1.2
- inner_weight: bfloat16 [768, 3072], replicated, may hold values from -0.21875 to 0.21875
- inner_bias: float32 [3072], replicated, may hold values from -1.2 to 1.2
- outer_weight: bfloat16 [3072, 768], replicated, may hold values from -0.109375 to 0.109375
- outer_bias: float32 [768], replicated, may hold values from -1.2 to 1.2
- second_gain: float32 [768], replicated, may hold values from 0.5 to 1.5
- second_shift: float32 [768], replicated, may hold values from -1.2 to 1.2
Outputs:
- loss: float32 [], replicated
- layer_output: bfloat16 [32768, 768], P('dp')
- token_grad: float32 [32768, 768], P('dp')
- query_weight_grad: float32 [768, 768], P('dp')
- query_bias_grad: float32 [768], P('dp')
- key_weight_grad: float32 [768, 768], P('dp')
- value_weight_grad: float32 [768, 768], P('dp')
- value_bias_grad: float32 [768], P('dp')
- output_weight_grad: float32 [768, 768], P('dp')
- output_bias_grad: float32 [768], P('dp')
- first_gain_grad: float32 [768], P('dp')
- first_shift_grad: float32 [768], P('dp')
- inner_weight_grad: float32 [768, 3072], P('dp')
- inner_bias_grad: float32 [3072], P('dp')
- outer_weight_grad: float32 [3072, 768], P('dp')
- outer_bias_grad: float32 [768], P('dp')
- second_gain_grad: float32 [768], P('dp')
- second_shift_grad: float32 [768], P('dp')
The draws below stay inside these ranges and needn't reach their ends.
Inputs may be any that keep to these rules, and one draw needn't show every extreme that they name: The 2 sentences of one device come from one length bucket: bucket b holds lengths from b * 128 + 1 (at least 16) to (b + 1) * 128; in every draw one sentence has exactly 512 tokens. `groups`: sentences with equal numbers form a group of 1 to 6 sentences; some group has exactly 6.
All inputs are finite; a program needn't handle non-finite values.
Results may differ from the reference program's by a relative error of at most 0.014.
Values may be sent and summed in bfloat16 or wider, within the bound.
A program may use at most 192 MiB of HBM per device.

```python
import jax
import jax.numpy as jnp
from jax import lax

D = 768
HEADS = 12
HD = 64
FF = 3072
LMAX = 512
MIN_LEN = 16
SEQ_DEV = 2
SEQS = 64
TOKENS = 32768


def draw_lengths(key, part):
    key = jax.random.fold_in(key, 11)
    bucket_key, length_key, long_key, device_key = jax.random.split(key, 4)
    devices = SEQS // SEQ_DEV
    width_of = LMAX // 4
    chosen_device = jax.random.randint(device_key, (), 0, devices)
    buckets = jax.random.randint(bucket_key, (devices,), 0, 4)
    buckets = jnp.where(jnp.arange(devices) == chosen_device, 3, buckets)
    per_row = jnp.repeat(buckets, SEQ_DEV)
    floor_len = jnp.maximum(per_row * width_of + 1, MIN_LEN)
    ceiling = jnp.maximum(floor_len, (per_row + 1) * width_of)
    drawn = jax.random.randint(length_key, (SEQS,), floor_len, ceiling + 1)
    chosen = chosen_device * SEQ_DEV + jax.random.randint(long_key, (), 0, SEQ_DEV)
    return jnp.where(jnp.arange(SEQS) == chosen, LMAX, drawn).astype(jnp.int32)


def draw_groups(key, part):
    key = jax.random.fold_in(key, 23)
    flag_key, order_key = jax.random.split(key, 2)
    row_ids = jnp.arange(SEQS, dtype=jnp.int32)
    coins = jax.random.randint(flag_key, (SEQS,), 0, 3) == 0
    starts = jnp.logical_or(row_ids % 6 == 0, coins)
    starts = jnp.where(row_ids < 6, row_ids == 0, starts)
    labels = jnp.cumsum(starts.astype(jnp.int32)) - 1
    shuffle = jax.random.permutation(order_key, SEQS)
    shuffled = labels[shuffle].astype(jnp.int32)
    last_place = jax.ops.segment_max(row_ids, shuffled, num_segments=SEQS)
    return last_place[shuffled].astype(jnp.int32)


def shard_levels(rng, dims, shards, smallest, largest):
    gain = 1.0
    for position, blocks in shards:
        heights = jax.random.uniform(jax.random.fold_in(jax.random.fold_in(rng, 6), position), (blocks,), jnp.float32, smallest / len(shards), largest / len(shards))
        gain = gain * jnp.repeat(jnp.exp(heights), dims[position] // blocks).reshape((-1,) + (1,) * (len(dims) - 1 - position))
    return gain


def centred(key, dims, scale, most, cuts=(), kind=jnp.bfloat16):
    level = shard_levels(key, dims, cuts, -0.22, 0.18) if cuts else 1.0
    entries = jax.random.normal(key, dims, jnp.float32) * scale * level
    return jnp.minimum(jnp.maximum(entries, -most), most).astype(kind)


def setup_inputs(seed: int = 0) -> dict:
    splits = jax.random.split(jax.random.key(seed), 19)
    return {
        "tokens": centred(splits[0], (TOKENS, D), 1.0, 6.0, ((0, 32),)),
        "lengths": draw_lengths(jax.random.fold_in(splits[18], 71), 0),
        "groups": draw_groups(jax.random.fold_in(splits[18], 71), 0),
        "query_weight": centred(splits[3], (D, D), D ** -0.5, 0.21875),
        "query_bias": centred(splits[4], (D,), 0.2, 1.2, (), jnp.float32),
        "key_weight": centred(splits[5], (D, D), D ** -0.5, 0.21875),
        "value_weight": centred(splits[6], (D, D), D ** -0.5, 0.21875),
        "value_bias": centred(splits[7], (D,), 0.2, 1.2, (), jnp.float32),
        "output_weight": centred(splits[8], (D, D), (D // 32) ** -0.5, 1.25),
        "output_bias": centred(splits[9], (D,), 0.2, 1.2, (), jnp.float32),
        "first_gain": jnp.clip(1.0 + 0.1 * jax.random.normal(splits[10], (D,), jnp.float32), 0.5, 1.5),
        "first_shift": centred(splits[11], (D,), 0.2, 1.2, (), jnp.float32),
        "inner_weight": centred(splits[12], (D, FF), D ** -0.5, 0.21875),
        "inner_bias": centred(splits[13], (FF,), 0.2, 1.2, (), jnp.float32),
        "outer_weight": centred(splits[14], (FF, D), FF ** -0.5, 0.109375),
        "outer_bias": centred(splits[15], (D,), 0.2, 1.2, (), jnp.float32),
        "second_gain": jnp.clip(1.0 + 0.1 * jax.random.normal(splits[16], (D,), jnp.float32), 0.5, 1.5),
        "second_shift": centred(splits[17], (D,), 0.2, 1.2, (), jnp.float32),
    }


cosine_scale = 20.0
layer_epsilon = 1e-06
unit_epsilon = 1e-06

@jax.custom_vjp
def low(v):
    return lax.optimization_barrier(v.astype(jnp.bfloat16)).astype(jnp.float32)

@jax.custom_vjp
def low_back(v):
    return v

def low_keep(v):
    return (low(v), None)

def low_pass(kept, grad):
    return (grad,)

def back_keep(v):
    return (v, None)

def back_low(kept, grad):
    return (low(grad),)
low.defvjp(low_keep, low_pass)
low_back.defvjp(back_keep, back_low)

def highest_mix(operand, weight):
    return jnp.einsum('bld,de->ble', operand, weight, precision=lax.Precision.HIGHEST)

def normalize(residual, scaling, offset):
    center = residual - lax.optimization_barrier(jnp.mean(residual, axis=-1, keepdims=True))
    spread = lax.optimization_barrier(jnp.mean(center * center, axis=-1, keepdims=True))
    return center * lax.rsqrt(spread + layer_epsilon) * scaling + offset

def encode(params, block_tokens, block_lengths):
    query_weight, query_bias, key_weight, value_weight, value_bias, output_weight, output_bias, first_gain, first_shift, inner_weight, inner_bias, outer_weight, outer_bias, second_gain, second_shift = params
    seq_count = block_tokens.shape[0]
    split_shape = (seq_count, LMAX, HEADS, HD)
    queries = low(low_back((highest_mix(block_tokens, query_weight) + query_bias) * 0.125)).reshape(split_shape)
    key_rows = low(low_back(highest_mix(block_tokens, key_weight))).reshape(split_shape)
    value_rows = low(low_back(highest_mix(block_tokens, value_weight) + value_bias)).reshape(split_shape)
    scores = low_back(jnp.einsum('bqhd,bkhd->bhqk', queries, key_rows, precision=lax.Precision.HIGHEST))
    key_live = jnp.arange(LMAX)[None, :] < block_lengths[:, None]
    scores = jnp.where(key_live[:, None, None, :], scores, -1e+30)
    probs_low = low(jax.nn.softmax(scores, axis=-1))
    mixture = jnp.einsum('bhqk,bkhd->bqhd', probs_low, value_rows, precision=lax.Precision.HIGHEST)
    mixture = low(low_back(mixture.reshape(seq_count, LMAX, D)))
    attended = low_back(highest_mix(mixture, output_weight) + output_bias)
    hidden = normalize(block_tokens + attended, first_gain, first_shift)
    inner_pre = low_back(highest_mix(low(hidden), inner_weight) + inner_bias)
    activated = low(jax.nn.gelu(inner_pre, approximate=False))
    branch = low_back(highest_mix(activated, outer_weight) + outer_bias)
    output = normalize(hidden + branch, second_gain, second_shift)
    weights_live = key_live.astype(jnp.float32)[:, :, None]
    pooled = lax.optimization_barrier(jnp.sum(output * weights_live, axis=1)) / block_lengths[:, None].astype(jnp.float32)
    return (output, low(pooled))

def contrast(pooled, groups):
    unit_rows = pooled * lax.rsqrt(lax.optimization_barrier(jnp.sum(pooled * pooled, axis=-1, keepdims=True)) + unit_epsilon)
    similar = cosine_scale * jnp.dot(unit_rows, unit_rows.T, precision=lax.Precision.HIGHEST)
    row_ids = jnp.arange(SEQS)
    itself = row_ids[:, None] == row_ids[None, :]
    logits = jnp.where(itself, -1e+30, similar)
    totals = jax.nn.logsumexp(logits, axis=-1)
    matched = jnp.logical_and(groups[:, None] == groups[None, :], jnp.logical_not(itself)).astype(jnp.float32)
    weights = matched / jnp.maximum(lax.optimization_barrier(jnp.sum(matched, axis=-1, keepdims=True)), 1.0)
    return jnp.sum(lax.optimization_barrier(jnp.sum(weights, axis=-1)) * totals - lax.optimization_barrier(jnp.sum(weights * similar, axis=-1)))

def forward(params, tokens, lengths, groups):
    per_step = 8
    stacked = tokens.reshape(SEQS // per_step, per_step, LMAX, D)
    parted = lengths.reshape(SEQS // per_step, per_step)
    checked = jax.checkpoint(encode)

    def advance(state_in, step_inputs):
        output, pooled = checked(params, step_inputs[0], step_inputs[1])
        return (state_in, (output, pooled))
    unused, (outputs, pooled) = lax.scan(advance, jnp.zeros((), jnp.float32), (stacked, parted))
    loss_value = contrast(pooled.reshape(SEQS, D), groups)
    return (loss_value, outputs.reshape(TOKENS, D))

def reference(tokens, lengths, groups, query_weight, query_bias, key_weight, value_weight, value_bias, output_weight, output_bias, first_gain, first_shift, inner_weight, inner_bias, outer_weight, outer_bias, second_gain, second_shift):
    params = tuple((member.astype(jnp.float32) for member in (query_weight, query_bias, key_weight, value_weight, value_bias, output_weight, output_bias, first_gain, first_shift, inner_weight, inner_bias, outer_weight, outer_bias, second_gain, second_shift)))

    def objective(weights_in, tokens_in):
        return forward(weights_in, tokens_in, lengths, groups)
    loss_value, pullback, outputs = jax.vjp(objective, params, tokens.astype(jnp.float32), has_aux=True)
    weight_grads, token_grad = pullback(jnp.ones((), jnp.float32))
    return (loss_value, outputs.astype(jnp.bfloat16), token_grad, weight_grads[0], weight_grads[1], weight_grads[2], weight_grads[3], weight_grads[4], weight_grads[5], weight_grads[6], weight_grads[7], weight_grads[8], weight_grads[9], weight_grads[10], weight_grads[11], weight_grads[12], weight_grads[13], weight_grads[14])
```

```python
import functools
import math

import jax
import jax.numpy as jnp
from jax import lax
from jax.experimental import pallas as pl
from jax.experimental.pallas import tpu as pltpu
from jax.sharding import PartitionSpec as P

HEADS = 12
HD = 64
cosine_scale = 20.0
layer_epsilon = 1e-06
unit_epsilon = 1e-06
low = jnp.bfloat16
full = jnp.float32
MIB = 1 << 20


def dot(left, right, left_axis=1, right_axis=0):
    return lax.dot_general(
        left, right, (((left_axis,), (right_axis,)), ((), ())), preferred_element_type=full
    )


def gelu_pair(value):
    size = jnp.abs(value)
    ratio = pl.reciprocal(1.0 + (0.3275911 / math.sqrt(2.0)) * size, approx=True)
    bell = jnp.exp(value * value * -0.5)
    series = 0.5 * 1.061405429
    for factor in (-1.453152027, 1.421413741, -0.284496736, 0.254829592):
        series = series * ratio + 0.5 * factor
    half_tail = series * ratio * bell
    cumulative = jnp.where(value >= 0.0, 1.0 - half_tail, half_tail)
    return value * cumulative, cumulative + value * bell * (1.0 / math.sqrt(2.0 * math.pi))


def spread_lanes(column, lanes=128):
    return jnp.broadcast_to(column, (column.shape[0], lanes))


def forward_kernel(
    lengths,
    tokens,
    vectors,
    inner_bias,
    query_weight,
    key_weight,
    value_weight,
    output_weight,
    inner_weight,
    outer_weight,
    layer_output,
    pooled,
    live_mean,
    queries_t,
    keys_t,
    values,
    mixture_t,
    probs,
    inverse_totals,
    first_normed,
    first_inverse,
    hidden_low,
    second_normed,
    second_inverse,
    activated,
    slopes,
    tokens_t,
    w_query,
    w_key,
    w_value,
    w_output,
    w_inner,
    w_outer,
    key_rows,
    values_t,
    mask_block,
    raised,
    total_second,
    hidden_full,
    sems,
    raised_sems,
):
    sentence = pl.program_id(0)
    slots, width = tokens.shape
    parts = activated.shape[0]
    part = activated.shape[2]
    length = lengths[sentence]
    weights = (
        (query_weight, w_query),
        (key_weight, w_key),
        (value_weight, w_value),
        (output_weight, w_output),
        (inner_weight, w_inner),
        (outer_weight, w_outer),
    )
    copies = [
        pltpu.make_async_copy(source, target, sems.at[place])
        for place, (source, target) in enumerate(weights)
    ]

    @pl.when(sentence == 0)
    def _():
        for copy in copies:
            copy.start()

    slot_ids = lax.broadcasted_iota(jnp.int32, (slots, 128), 0)
    lane_ids = lax.broadcasted_iota(jnp.int32, (slots, 128), 1)
    mask_block[...] = jnp.where(
        jnp.logical_and(slot_ids >= length, lane_ids == 0), -1e30, 0.0
    ).astype(low)

    def ready(place):
        @pl.when(sentence == 0)
        def _():
            copies[place].wait()

    block = tokens[...]
    tokens_t[...] = block.T
    ready(0)
    queries_t[...] = ((dot(block, w_query[...]) + vectors[0:1, :]) * 0.125).astype(low).T
    ready(1)
    rows = dot(block, w_key[...]).astype(low)
    key_rows[...] = rows
    keys_t[...] = rows.T
    ready(2)
    rows = (dot(block, w_value[...]) + vectors[1:2, :]).astype(low)
    values[...] = rows
    values_t[...] = rows.T

    pick_row = jnp.where(
        lax.broadcasted_iota(jnp.int32, (128, slots), 0) == 0, 1.0, 0.0
    ).astype(low)
    empty = jnp.zeros((HD, slots), low)
    depth = raised.shape[0]

    def raised_copy(head):
        return pltpu.make_async_copy(
            raised.at[lax.rem(head, depth)],
            probs.at[sentence * HEADS + head],
            raised_sems.at[lax.rem(head, depth)],
        )

    def head_pair(pair, carry):
        start = pl.multiple_of(pair * 128, 128)
        left = jnp.concatenate([key_rows[:, pl.ds(start, 128)], mask_block[...]], axis=1)
        pair_queries = queries_t[pl.ds(start, 128), :]
        for half in range(2):
            head = pair * 2 + half
            if half == 0:
                right = jnp.concatenate([pair_queries[:HD], empty, pick_row], axis=0)
            else:
                right = jnp.concatenate([empty, pair_queries[HD:], pick_row], axis=0)

            @pl.when(pair >= depth // 2)
            def _():
                raised_copy(head).wait()

            scores = dot(left, right)
            summit = jnp.max(scores, axis=0, keepdims=True)
            totals = jnp.zeros((8, slots), full)
            slot = lax.rem(head, depth)
            step = 64
            for place in range(0, slots, step):
                piece = jnp.exp(scores[place : place + step, :] - summit)
                totals = totals + jnp.sum(piece.reshape(step // 8, 8, slots), axis=0)
                raised[slot, place : place + step, :] = piece.astype(low)
            inverse = 1.0 / jnp.sum(totals, axis=0, keepdims=True)
            raised_copy(head).start()
            inverse_totals[head] = jnp.broadcast_to(inverse, (8, slots))
            row = pl.multiple_of(start + half * HD, HD)
            mixed = dot(values_t[pl.ds(row, HD), :], raised[slot]) * inverse
            mixture_t[pl.ds(row, HD), :] = mixed.astype(low)
        return carry

    lax.fori_loop(0, HEADS // 2, head_pair, 0)

    ready(3)
    attended = dot(mixture_t[...], w_output[...], 0, 0)
    step = 32
    for place in range(0, slots, step):
        rows = slice(place, place + step)
        residual = block[rows].astype(full) + attended[rows] + vectors[2:3, :]
        center = residual - jnp.mean(residual, axis=1, keepdims=True)
        inverse = lax.rsqrt(jnp.mean(center * center, axis=1, keepdims=True) + layer_epsilon)
        normed = center * inverse
        hidden = normed * vectors[3:4, :] + vectors[4:5, :]
        first_normed[rows, :] = normed
        first_inverse[rows, :] = spread_lanes(inverse)
        hidden_low[rows, :] = hidden.astype(low)
        hidden_full[rows, :] = hidden

    ready(4)
    ready(5)
    total_second[...] = jnp.zeros_like(total_second)

    def feed(index, carry):
        start = pl.multiple_of(index * part, part)
        inner = dot(hidden_low[...], w_inner[:, pl.ds(start, part)])
        offset = inner_bias[:, pl.ds(start, part)]
        step = 32
        for place in range(0, slots, step):
            value, slope = gelu_pair(inner[place : place + step] + offset)
            activated[index, place : place + step, :] = value.astype(low)
            slopes[index, place : place + step, :] = slope.astype(low)
        total_second[...] += dot(activated[index], w_outer[pl.ds(start, part), :])
        return carry

    lax.fori_loop(0, parts, feed, 0)

    live_sum = jnp.zeros((8, width), full)
    count = length.astype(full)
    step = 32
    for place in range(0, slots, step):
        rows = slice(place, place + step)
        residual = hidden_full[rows, :] + total_second[rows, :] + vectors[5:6, :]
        center = residual - jnp.mean(residual, axis=1, keepdims=True)
        inverse = lax.rsqrt(jnp.mean(center * center, axis=1, keepdims=True) + layer_epsilon)
        normed = center * inverse
        second_normed[rows, :] = normed
        layer_output[rows, :] = (normed * vectors[6:7, :] + vectors[7:8, :]).astype(low)
        live = lax.broadcasted_iota(jnp.int32, (step, width), 0) + place < length
        live_sum = live_sum + jnp.sum(
            jnp.where(live, normed, 0.0).reshape(step // 8, 8, width), axis=0
        )
        alive = lax.broadcasted_iota(jnp.int32, (step, 128), 0) + place < length
        second_inverse[rows, :] = jnp.where(alive, spread_lanes(inverse) / count, 0.0)
    mean_normed = jnp.sum(live_sum, axis=0, keepdims=True) / count
    live_mean[0] = jnp.broadcast_to(mean_normed, (8, width))
    vector = (mean_normed * vectors[6:7, :] + vectors[7:8, :]).astype(low).astype(full)
    pooled[0] = jnp.broadcast_to(vector, (8, width))

    for head in range(HEADS - depth, HEADS):
        raised_copy(head).wait()


def forward(lengths, tokens, vectors, inner_bias, weights):
    count = lengths.shape[0]
    rows, width = tokens.shape
    slots = rows // count
    inner = weights[4].shape[1]
    part = 768
    parts = inner // part
    hbm = pl.BlockSpec(memory_space=pl.ANY)
    vmem = pl.BlockSpec(memory_space=pltpu.VMEM)

    def by_rows(columns):
        return pl.BlockSpec((slots, columns), lambda s: (s, 0))

    by_columns = pl.BlockSpec((width, slots), lambda s: (0, s))
    by_sentence = pl.BlockSpec((1, 8, width), lambda s: (s, 0, 0))
    by_parts = pl.BlockSpec((parts, slots, part), lambda s: (0, s, 0))
    shape = jax.ShapeDtypeStruct
    return pl.pallas_call(
        forward_kernel,
        grid=(count,),
        in_specs=[pl.BlockSpec(memory_space=pltpu.SMEM), by_rows(width), vmem, vmem] + [hbm] * 6,
        out_specs=[
            by_rows(width),
            by_sentence,
            by_sentence,
            by_columns,
            by_columns,
            by_rows(width),
            by_columns,
            hbm,
            pl.BlockSpec((HEADS, 8, slots), lambda s: (s, 0, 0)),
            by_rows(width),
            by_rows(128),
            by_rows(width),
            by_rows(width),
            by_rows(128),
            by_parts,
            by_parts,
            by_columns,
        ],
        out_shape=[
            shape((rows, width), low),
            shape((count, 8, width), full),
            shape((count, 8, width), full),
            shape((width, rows), low),
            shape((width, rows), low),
            shape((rows, width), low),
            shape((width, rows), low),
            shape((count * HEADS, slots, slots), low),
            shape((count * HEADS, 8, slots), full),
            shape((rows, width), full),
            shape((rows, 128), full),
            shape((rows, width), low),
            shape((rows, width), full),
            shape((rows, 128), full),
            shape((parts, rows, part), low),
            shape((parts, rows, part), low),
            shape((width, rows), low),
        ],
        scratch_shapes=[pltpu.VMEM(w.shape, low) for w in weights]
        + [
            pltpu.VMEM((slots, width), low),
            pltpu.VMEM((width, slots), low),
            pltpu.VMEM((slots, 128), low),
            pltpu.VMEM((4, slots, slots), low),
            pltpu.VMEM((slots, width), full),
            pltpu.VMEM((slots, width), full),
            pltpu.SemaphoreType.DMA((6,)),
            pltpu.SemaphoreType.DMA((4,)),
        ],
        compiler_params=pltpu.CompilerParams(vmem_limit_bytes=62 * MIB),
        name="encode",
    )(lengths, tokens, vectors, inner_bias, *weights)


def partner_of(me, mask):
    bit = lax.rem(lax.div(me, mask), 2)
    return bit, me + mask * (1 - 2 * bit)


class Summation:
    def __init__(self, buffers, sems, place, links):
        self.send, self.held = buffers[0], buffers[1:]
        self.send_sems, self.recv_sems = sems
        self.place = place
        self.links = links
        self.third = self.held[0].shape[-2] // 3
        self.started = []

    def exchange(self, stage, part, source, target, link):
        copy = pltpu.make_async_remote_copy(
            src_ref=source,
            dst_ref=target,
            send_sem=self.send_sems.at[self.place, stage, part],
            recv_sem=self.recv_sems.at[self.place, stage, part],
            device_id=(self.links[link][1],),
            device_id_type=pl.DeviceIdType.MESH,
        )
        return copy

    def views(self, stage, away):
        h = self.third

        def side(link):
            bit = self.links[link][0]
            return 1 - bit if away else bit

        if stage == 0:
            return [self.send.at[:, :, :, :, side("core")]]
        if stage == 1:
            r = self.held[0]
            return [
                r.at[:, :, :, side("x"), pl.ds(0, h)],
                r.at[:, :, side("y"), :, pl.ds(h, h)],
                r.at[:, side("z0"), :, :, pl.ds(2 * h, h)],
            ]
        if stage == 2:
            r = self.held[1]
            return [r.at[0, :, :, side("y")], r.at[1, :, side("z0")], r.at[2, :, :, side("x")]]
        if stage == 3:
            r = self.held[2]
            return [r.at[0, :, side("z0")], r.at[1, :, side("x")], r.at[2, :, side("y")]]
        r = self.held[3]
        return [r.at[part, side("z1")] for part in range(3)]

    def copies(self, stage):
        routes = (
            ("core",),
            ("x", "y", "z0"),
            ("y", "z0", "x"),
            ("z0", "x", "y"),
            ("z1", "z1", "z1"),
        )[stage]
        sources = self.views(stage, True)
        target = self.held[stage]
        targets = [target] if stage == 0 else [target.at[part] for part in range(3)]
        return [
            self.exchange(stage, part, source, goal, link)
            for part, (source, goal, link) in enumerate(zip(sources, targets, routes))
        ]

    def start(self, stage=0):
        for copy in self.copies(stage):
            copy.start()

    def step(self, stage, out=None):
        for copy in self.copies(stage):
            copy.wait()
        kept = self.views(stage, False)
        if stage == 0:
            self.held[0][...] = self.held[0][...] + kept[0][...]
        elif stage < 4:
            for part in range(3):
                self.held[stage][part] = self.held[stage][part] + kept[part][...]
        else:
            h = self.third
            for part in range(3):
                out[part * h : part * h + h, :] = kept[part][...].astype(full) + self.held[4][
                    part
                ].astype(full)
        if stage < 4:
            self.start(stage + 1)


def contrast(points, groups):
    count = points.shape[0]
    inverse = lax.rsqrt(jnp.sum(points * points, axis=1, keepdims=True) + unit_epsilon)
    unit = points * inverse
    similar = cosine_scale * lax.dot_general(
        unit,
        unit,
        (((1,), (1,)), ((), ())),
        precision=lax.Precision.HIGHEST,
        preferred_element_type=full,
    )
    rows = lax.broadcasted_iota(jnp.int32, (count, count), 0)
    columns = lax.broadcasted_iota(jnp.int32, (count, count), 1)
    itself = rows == columns
    logits = jnp.where(itself, -1e30, similar)
    summit = jnp.max(logits, axis=1, keepdims=True)
    raised = jnp.exp(logits - summit)
    totals = jnp.sum(raised, axis=1, keepdims=True)
    chances = raised / totals
    log_total = summit + jnp.log(totals)
    across = jnp.broadcast_to(groups, (count, count))
    matched = jnp.where(
        jnp.logical_and(across == across.T, jnp.logical_not(itself)), 1.0, 0.0
    )
    weights = matched / jnp.maximum(jnp.sum(matched, axis=1, keepdims=True), 1.0)
    row_mass = jnp.sum(weights, axis=1, keepdims=True)
    loss_rows = row_mass * log_total - jnp.sum(weights * similar, axis=1, keepdims=True)
    loss = jnp.sum(loss_rows, axis=0, keepdims=True)
    coupling = row_mass * chances - weights
    unit_grad = cosine_scale * lax.dot_general(
        coupling + coupling.T,
        unit,
        (((1,), (0,)), ((), ())),
        precision=lax.Precision.HIGHEST,
        preferred_element_type=full,
    )
    grad = inverse * (unit_grad - unit * jnp.sum(unit * unit_grad, axis=1, keepdims=True))
    return loss, grad


def backward_kernel(
    devices,
    sentences,
    pooled,
    live_mean,
    vectors,
    groups,
    activated_in,
    slopes_in,
    second_normed_in,
    second_inverse_in,
    hidden_low_in,
    first_normed_in,
    first_inverse_in,
    mixture_t_in,
    queries_t_in,
    keys_t_in,
    values_in,
    tokens_t_in,
    probs_in,
    inverse_totals_in,
    query_weight,
    key_weight,
    value_weight,
    output_weight,
    inner_weight,
    outer_weight,
    loss_out,
    token_grad_out,
    outer_out,
    inner_out,
    square_out,
    sums_out,
    act,
    inner_grad,
    w_rows,
    w_columns,
    mixture_t,
    normed,
    grads,
    branch,
    hidden_low,
    second_inverse,
    first_inverse,
    inverse_totals,
    score_grads,
    own,
    gathered,
    points,
    outer_send,
    outer_0,
    outer_1,
    outer_2,
    outer_3,
    outer_4,
    inner_send,
    inner_0,
    inner_1,
    inner_2,
    inner_3,
    inner_4,
    square_0,
    square_1,
    square_2,
    square_3,
    square_4,
    sum_held,
    sum_recv,
    load_sems,
    prob_sems,
    gather_send,
    gather_recv,
    set_send,
    set_recv,
    sum_send,
    sum_sems,
):
    me = lax.axis_index("dp")
    rows, width = normed.shape
    slots = rows // sentences
    parts = act.shape[0]
    heads = width // HD
    links = {
        "core": partner_of(me, 1),
        "x": partner_of(me, 2),
        "y": partner_of(me, 4),
        "z0": partner_of(me, 8),
        "z1": partner_of(me, 16),
    }
    load_count = iter(range(64))

    def load(source, target):
        return pltpu.make_async_copy(source, target, load_sems.at[next(load_count)])

    get_normed = load(second_normed_in, normed)
    get_second = load(second_inverse_in, second_inverse)
    get_act = load(activated_in, act)
    get_outer = load(outer_weight, w_rows)
    get_slopes = load(slopes_in, inner_grad)
    get_hidden = load(hidden_low_in, hidden_low)
    get_inner = load(inner_weight, w_columns)
    get_first = load(first_inverse_in, first_inverse)
    get_mixture = load(mixture_t_in, mixture_t)
    get_totals = load(inverse_totals_in, inverse_totals)
    early = (
        get_normed,
        get_second,
        get_act,
        get_outer,
        get_slopes,
        get_hidden,
        get_inner,
        get_first,
        get_mixture,
        get_totals,
    )
    for copy in early:
        copy.start()

    barrier = pltpu.get_barrier_semaphore()

    def greet(step, carry):
        other = lax.rem(me + step, devices)
        pl.semaphore_signal(
            barrier, inc=1, device_id=(other,), device_id_type=pl.DeviceIdType.MESH
        )
        return carry

    lax.fori_loop(1, devices, greet, 0)
    for sentence in range(sentences):
        own[sentence : sentence + 1, :] = pooled[sentence, 0:1, :]
    gathered[me] = own[...]
    pl.semaphore_wait(barrier, devices - 1)

    def gather_copy(step):
        return pltpu.make_async_remote_copy(
            src_ref=own,
            dst_ref=gathered.at[me],
            send_sem=gather_send.at[step],
            recv_sem=gather_recv.at[step],
            device_id=(lax.rem(me + step, devices),),
            device_id_type=pl.DeviceIdType.MESH,
        )

    def gather_start(step, carry):
        gather_copy(step).start()
        return carry

    def gather_wait(step, carry):
        gather_copy(step).wait()
        return carry

    lax.fori_loop(1, devices, gather_start, 0)
    lax.fori_loop(1, devices, gather_wait, 0)
    for device in range(devices):
        points[device * sentences : (device + 1) * sentences, :] = gathered[device]
    loss, pooled_grad = contrast(points[...], groups[...])
    loss_out[...] = jnp.broadcast_to(loss, loss_out.shape)
    row_ids = lax.broadcasted_iota(jnp.int32, (devices * sentences, width), 0)
    own_grads = [
        jnp.sum(
            jnp.where(row_ids == me * sentences + sentence, pooled_grad, 0.0),
            axis=0,
            keepdims=True,
        )
        for sentence in range(sentences)
    ]
    vector_sums = sum_held.at[0]
    vector_sums[...] = jnp.zeros_like(vector_sums)
    vector_sums[1:2, :] = sum(
        own_grads[sentence] * live_mean[sentence, 0:1, :] for sentence in range(sentences)
    )
    vector_sums[2:3, :] = sum(own_grads)

    outer_set = Summation(
        (outer_send, outer_0, outer_1, outer_2, outer_3, outer_4), (set_send, set_recv), 0, links
    )
    inner_set = Summation(
        (inner_send, inner_0, inner_1, inner_2, inner_3, inner_4), (set_send, set_recv), 1, links
    )
    piece_rows, piece_columns = outer_send.shape[-2] // 2, width // 2
    square_sends = [
        outer_send.at[
            :,
            :,
            :,
            :,
            :,
            pl.ds(place % 2 * piece_rows, piece_rows),
            pl.ds(place // 2 * piece_columns, piece_columns),
        ]
        for place in range(4)
    ]
    square_sets = [
        Summation(
            (square_sends[place],)
            + tuple(
                ref.at[place] for ref in (square_0, square_1, square_2, square_3, square_4)
            ),
            (set_send, set_recv),
            2 + place,
            links,
        )
        for place in range(4)
    ]

    def widen(column, lanes=width):
        return jnp.concatenate([column] * (lanes // 128), axis=1)

    get_normed.wait()
    get_second.wait()
    bias_sum = jnp.zeros((8, width), full)
    step = 32
    for sentence in range(sentences):
        scaled = own_grads[sentence] * vectors[6:7, :]
        shifted = scaled - jnp.mean(scaled, axis=1, keepdims=True)

        def second_back(index, total):
            at = pl.ds(pl.multiple_of(sentence * slots + index * step, step), step)
            unit = normed[at, :]
            mass = jnp.mean(unit * scaled, axis=1, keepdims=True)
            grad = widen(second_inverse[at, :]) * (shifted - unit * mass)
            grads[at, :] = grad
            rounded = grad.astype(low)
            branch[at, :] = rounded
            return total + jnp.sum(
                rounded.astype(full).reshape(step // 8, 8, width), axis=0
            )

        bias_sum = lax.fori_loop(0, slots // step, second_back, bias_sum)
    vector_sums[0:1, :] = jnp.sum(bias_sum, axis=0, keepdims=True)
    get_normed_2 = load(first_normed_in, normed)
    get_normed_2.start()

    get_act.wait()

    def cores_of(index):
        return [(y, x, core) for y in range(2) for x in range(2) for core in range(2)][index]

    def outer_block(index, carry):
        result = dot(act[index], branch[...], 0, 0).astype(low)
        high, below = lax.div(index, 2), lax.rem(index, 2)
        piece = outer_send.shape[-2]
        for place in range(8):
            y, x, core = cores_of(place)
            outer_send[high, below, y, x, core] = result[place * piece : (place + 1) * piece, :]
        return carry

    lax.fori_loop(0, parts, outer_block, 0)
    outer_set.start()

    get_values = load(values_in, act.at[0])
    get_values.start()

    def prob_slot(order):
        place = lax.rem(order, 4)
        return act.at[
            2 + lax.div(place, 2),
            pl.ds(pl.multiple_of(lax.rem(place, 2) * slots, slots), slots),
            0:slots,
        ]

    def prob_copy(order):
        half = lax.rem(order, 2)
        sentence = lax.rem(lax.div(order, 2), sentences)
        pair = lax.div(order, 2 * sentences)
        return pltpu.make_async_copy(
            probs_in.at[sentence * heads + pair * 2 + half],
            prob_slot(order),
            prob_sems.at[lax.rem(order, 4)],
        )

    for order in range(3):
        prob_copy(order).start()

    get_outer.wait()
    get_slopes.wait()

    def inner_block(index, carry):
        start = pl.multiple_of(index * width, width)
        weight = w_rows[pl.ds(start, width), :]
        total = jnp.zeros((8, width), full)
        for piece in range(2):
            span = rows // 2
            result = dot(branch[piece * span : (piece + 1) * span, :], weight, 1, 1)
            for place in range(0, span, step):
                at = pl.ds(piece * span + place, step)
                value = (
                    result[place : place + step] * inner_grad[index, at, :].astype(full)
                ).astype(low)
                inner_grad[index, at, :] = value
                total = total + jnp.sum(
                    value.astype(full).reshape(step // 8, 8, width), axis=0
                )
        vector_sums[pl.ds(8 + index, 1), :] = jnp.sum(total, axis=0, keepdims=True)
        return carry

    lax.fori_loop(0, parts, inner_block, 0)
    square_loads = [
        load(source, w_rows.at[pl.ds(place * width, width)])
        for place, source in enumerate((output_weight, query_weight, key_weight, value_weight))
    ]
    for copy in square_loads:
        copy.start()

    outer_set.step(0)

    get_hidden.wait()
    own_rows = width // devices
    for block in range(2):
        left = hidden_low[:, block * (width // 2) : (block + 1) * (width // 2)].T

        def inner_weight_block(index, carry):
            upper = dot(left, inner_grad[index])
            lower = dot(left, inner_grad[index + 2])
            start = pl.multiple_of(index * width, width)
            for place in range(16):
                y, x, core = cores_of(place % 8)
                at = slice(place * own_rows, (place + 1) * own_rows)
                inner_send[block, place // 8, y, x, core, :, pl.ds(start, width)] = (
                    jnp.concatenate([upper[at], lower[at]], axis=0).astype(low)
                )
            return carry

        lax.fori_loop(0, 2, inner_weight_block, 0)
    inner_set.start()

    get_inner.wait()
    get_normed_2.wait()
    get_first.wait()
    span = 256

    def hidden_block(index, sums):
        gain_sum, shift_sum, bias_sum = sums
        base = pl.multiple_of(index * span, span)
        total = dot(inner_grad[0, pl.ds(base, span), :], w_columns[:, 0:width], 1, 1)
        for part in range(1, parts):
            total = total + dot(
                inner_grad[part, pl.ds(base, span), :],
                w_columns[:, part * width : (part + 1) * width],
                1,
                1,
            )
        for place in range(0, span, step):
            at = pl.ds(base + place, step)
            upstream = grads[at, :] + total[place : place + step]
            unit = normed[at, :]
            gain_sum = gain_sum + jnp.sum((upstream * unit).reshape(step // 8, 8, width), axis=0)
            shift_sum = shift_sum + jnp.sum(upstream.reshape(step // 8, 8, width), axis=0)
            scaled = upstream * vectors[3:4, :]
            center = scaled - jnp.mean(scaled, axis=1, keepdims=True)
            grad = widen(first_inverse[at, :]) * (
                center - unit * jnp.mean(scaled * unit, axis=1, keepdims=True)
            )
            grads[at, :] = grad
            rounded = grad.astype(low)
            branch[at, :] = rounded
            bias_sum = bias_sum + jnp.sum(
                rounded.astype(full).reshape(step // 8, 8, width), axis=0
            )
        return gain_sum, shift_sum, bias_sum

    zero = jnp.zeros((8, width), full)
    gain_sum, shift_sum, bias_sum = lax.fori_loop(
        0, rows // span, hidden_block, (zero, zero, zero)
    )
    vector_sums[3:4, :] = jnp.sum(gain_sum, axis=0, keepdims=True)
    vector_sums[4:5, :] = jnp.sum(shift_sum, axis=0, keepdims=True)
    vector_sums[5:6, :] = jnp.sum(bias_sum, axis=0, keepdims=True)

    get_queries = load(queries_t_in, w_columns.at[:, 0:rows])
    get_keys = load(keys_t_in, w_columns.at[:, rows : 2 * rows])
    get_queries.start()
    get_keys.start()
    get_tokens = [
        load(
            tokens_t_in.at[:, sentence * slots : (sentence + 1) * slots],
            inner_grad.at[2 + sentence, 0:width, 0:slots],
        )
        for sentence in range(sentences)
    ]
    for copy in get_tokens:
        copy.start()
    outer_set.step(1)
    inner_set.step(0)

    def square_pieces(place, result):
        half = width // 2
        for device in range(devices):
            y, x, core = cores_of(device % 8)
            z = device // 8
            at = slice(device * own_rows, (device + 1) * own_rows)
            square_sends[place][z // 2, z % 2, y, x, core] = jnp.concatenate(
                [result[at, :half], result[at, half:]], axis=0
            ).astype(low)

    get_mixture.wait()
    square_pieces(0, dot(mixture_t[...], branch[...]))
    square_sets[0].start()

    square_loads[0].wait()
    get_totals.wait()
    for sentence in range(sentences):
        spans = slice(sentence * slots, (sentence + 1) * slots)
        result = dot(w_rows[0:width, :], branch[spans, :], 1, 1)
        for head in range(heads):
            at = slice(head * HD, (head + 1) * HD)
            place = sentence * heads + head
            value = result[at] * inverse_totals[place, 0:1, :]
            mass = jnp.sum(value * mixture_t[at, spans].astype(full), axis=0, keepdims=True)
            inverse_totals[place] = jnp.broadcast_to(mass, (8, slots))
            inner_grad[sentence, at, 0:slots] = value.astype(low)
    outer_set.step(2)

    get_queries.wait()
    get_keys.wait()
    get_values.wait()
    empty = jnp.zeros((HD, slots), low)
    orders = heads * sentences
    group_pairs = 2

    def attend_back(step_index, carry):
        pair = lax.div(step_index, sentences)
        sentence = lax.rem(step_index, sentences)
        start = pl.multiple_of(pair * 128, 128)
        spans = pl.ds(pl.multiple_of(sentence * slots, slots), slots)
        left = act[0, spans, pl.ds(start, 128)]
        for half in range(2):
            order = step_index * 2 + half
            row = pl.multiple_of(start + half * HD, HD)
            place = sentence * heads + pair * 2 + half
            prob_copy(order).wait()

            @pl.when(order + 3 < orders)
            def _():
                prob_copy(order + 3).start()

            slot = lax.rem(order, 4)
            prob = prob_slot(order)
            upstream = inner_grad[sentence, pl.ds(row, HD), 0:slots]
            right = jnp.concatenate(
                [upstream, empty] if half == 0 else [empty, upstream], axis=0
            )
            toward = dot(left, right)
            mass = inverse_totals[place, 0:1, :]
            for piece in range(0, slots, 64):
                score_grads[half, piece : piece + 64, :] = (
                    prob[piece : piece + 64, :].astype(full) * (toward[piece : piece + 64] - mass)
                ).astype(low)
            value_grad = dot(upstream, prob[...], 1, 1)
            key_spans = pl.ds(pl.multiple_of(rows + sentence * slots, slots), slots)
            query = w_columns[pl.ds(row, HD), spans]
            key = w_columns[pl.ds(row, HD), key_spans]
            score = score_grads[half]
            key_grad = dot(query, score, 1, 1)
            query_grad = dot(key, score)
            mixture_t[pl.ds(row, HD), spans] = value_grad.astype(low)
            w_columns[pl.ds(row, HD), spans] = query_grad.astype(low)
            w_columns[pl.ds(row, HD), key_spans] = key_grad.astype(low)
        return carry

    def projection_grads(group):
        at = slice(group * 256, (group + 1) * 256)
        results = []
        for name in range(3):
            total = None
            for sentence in range(sentences):
                left = inner_grad[2 + sentence, 0:width, 0:slots]
                if name < 2:
                    base = name * rows + sentence * slots
                    right = w_columns[at, base : base + slots]
                else:
                    right = mixture_t[at, sentence * slots : (sentence + 1) * slots]
                term = dot(left, right, 1, 1)
                total = term if total is None else total + term
            results.append(total * 0.125 if name == 0 else total)
        square_pieces(1 + group, jnp.concatenate(results, axis=1))

    def both(first, second):
        first()
        second()

    ticks = {
        0: {1: lambda: inner_set.step(1), 3: lambda: square_sets[0].step(0)},
        1: {0: lambda: outer_set.step(3), 1: lambda: inner_set.step(2), 3: lambda: square_sets[0].step(1)},
        2: {
            0: lambda: both(
                lambda: outer_set.step(4, outer_out), lambda: square_sets[1].step(0)
            ),
            1: lambda: inner_set.step(3),
            2: lambda: square_sets[0].step(2),
            3: lambda: square_sets[1].step(1),
        },
    }
    for group in range(3):
        steps = group_pairs * sentences

        def group_step(index, carry, group=group):
            attend_back(group * steps + index, 0)
            for when, action in ticks[group].items():
                pl.when(index == when)(action)
            return carry

        lax.fori_loop(0, steps, group_step, 0)
        if group == 0:
            for copy in get_tokens:
                copy.wait()
        projection_grads(group)
        square_sets[1 + group].start()

    ones = jnp.ones((8, rows), low)
    vector_sums[6:7, :] = 0.125 * dot(ones, w_columns[:, 0:rows], 1, 1)[0:1, :]
    vector_sums[7:8, :] = dot(ones, mixture_t[...], 1, 1)[0:1, :]

    def sum_copy(stage):
        return pltpu.make_async_remote_copy(
            src_ref=sum_held.at[stage],
            dst_ref=sum_recv.at[stage],
            send_sem=sum_send.at[stage],
            recv_sem=sum_sems.at[stage],
            device_id=(links[("core", "x", "y", "z0", "z1")[stage]][1],),
            device_id_type=pl.DeviceIdType.MESH,
        )

    def sum_step(stage):
        sum_copy(stage).wait()
        total = sum_held[stage] + sum_recv[stage]
        if stage < 4:
            sum_held[stage + 1] = total
            sum_copy(stage + 1).start()
        else:
            sums_out[...] = total

    sum_copy(0).start()
    inner_set.step(4, inner_out)
    square_sets[0].step(3)
    square_sets[1].step(2)
    square_sets[2].step(0)

    for copy in square_loads[1:]:
        copy.wait()

    def token_block(sentence):
        spans = slice(sentence * slots, (sentence + 1) * slots)
        lefts = (
            w_columns[:, spans],
            w_columns[:, rows + sentence * slots : rows + (sentence + 1) * slots],
            mixture_t[:, spans],
        )
        total = 0.125 * dot(lefts[0], w_rows[width : 2 * width, :], 0, 1)
        total = total + dot(lefts[1], w_rows[2 * width : 3 * width, :], 0, 1)
        total = total + dot(lefts[2], w_rows[3 * width : 4 * width, :], 0, 1)
        grads[spans, :] = grads[spans, :] + total
        return pltpu.make_async_copy(
            grads.at[spans], token_grad_out.at[spans], load_sems.at[60 + sentence]
        )

    square_sets[3].step(0)
    sum_step(0)
    outs = []
    for sentence in range(sentences):
        copy = token_block(sentence)
        copy.start()
        outs.append(copy)
        if sentence == 0:
            square_sets[2].step(1)
            square_sets[1].step(3)
            square_sets[0].step(4, square_out.at[0])
            square_sets[3].step(1)
            sum_step(1)
    square_sets[2].step(2)
    square_sets[1].step(4, square_out.at[1])
    square_sets[3].step(2)
    sum_step(2)
    square_sets[2].step(3)
    square_sets[3].step(3)
    sum_step(3)
    square_sets[2].step(4, square_out.at[2])
    square_sets[3].step(4, square_out.at[3])
    sum_step(4)
    for copy in outs:
        copy.wait()


def finish_kernel(
    devices,
    loss,
    outer,
    inner,
    square,
    sums,
    loss_out,
    query_out,
    query_bias,
    key_out,
    value_out,
    value_bias,
    output_out,
    output_bias,
    first_gain,
    first_shift,
    inner_out,
    inner_bias,
    outer_out,
    outer_bias,
    second_gain,
    second_shift,
):
    me = lax.axis_index("dp")
    width = outer.shape[1]
    own = query_out.shape[0]
    loss_out[...] = loss[0:1, 0:1]
    outer_out[...] = outer[...]
    half = inner.shape[1]
    inner_out[:, 0:half] = inner[0:own, :]
    inner_out[:, half : 2 * half] = inner[own : 2 * own, :]
    output_out[:, 0 : width // 2] = square[0, 0:own, :]
    output_out[:, width // 2 : width] = square[0, own : 2 * own, :]
    for group in range(3):
        at = slice(group * 256, (group + 1) * 256)
        first, second = square[1 + group, 0:own, :], square[1 + group, own : 2 * own, :]
        query_out[:, at] = first[:, 0:256]
        key_out[:, group * 256 : group * 256 + 128] = first[:, 256:384]
        key_out[:, group * 256 + 128 : group * 256 + 256] = second[:, 0:128]
        value_out[:, at] = second[:, 128:384]
    source = lax.broadcasted_iota(jnp.int32, (width, 128), 0)
    lane = lax.broadcasted_iota(jnp.int32, (width, 128), 1)

    def pick(values, start):
        chosen = jnp.where(source == lane + start, 1.0, 0.0)
        return lax.dot_general(
            values,
            chosen,
            (((1,), (0,)), ((), ())),
            precision=lax.Precision.HIGHEST,
            preferred_element_type=full,
        )

    picked = pick(sums[0:8, :], me * own)
    for place, ref in enumerate(
        (
            outer_bias,
            second_gain,
            second_shift,
            first_gain,
            first_shift,
            output_bias,
            query_bias,
            value_bias,
        )
    ):
        ref[...] = picked[place : place + 1, 0 : ref.shape[1]]
    wide = inner_bias.shape[1]
    per_row = width // wide
    row_ids = lax.broadcasted_iota(jnp.int32, (8, width), 0)
    chosen = jnp.sum(
        jnp.where(row_ids == lax.div(me, per_row), sums[8:16, :], 0.0), axis=0, keepdims=True
    )
    inner_bias[...] = pick(jnp.broadcast_to(chosen, (8, width)), lax.rem(me, per_row) * wide)[
        0:1, 0:wide
    ]


def linked_device(
    devices,
    tokens,
    lengths,
    groups,
    query_weight,
    query_bias,
    key_weight,
    value_weight,
    value_bias,
    output_weight,
    output_bias,
    first_gain,
    first_shift,
    inner_weight,
    inner_bias,
    outer_weight,
    outer_bias,
    second_gain,
    second_shift,
):
    sentences = lengths.shape[0]
    rows, width = tokens.shape
    slots = rows // sentences
    inner = inner_weight.shape[1]
    vectors = jnp.stack(
        (
            query_bias,
            value_bias,
            output_bias,
            first_gain,
            first_shift,
            outer_bias,
            second_gain,
            second_shift,
        )
    )
    weights = (query_weight, key_weight, value_weight, output_weight, inner_weight, outer_weight)
    (
        layer_output,
        pooled,
        live_mean,
        queries_t,
        keys_t,
        values,
        mixture_t,
        probs,
        inverse_totals,
        first_normed,
        first_inverse,
        hidden_low,
        second_normed,
        second_inverse,
        activated,
        slopes,
        tokens_t,
    ) = forward(lengths, tokens, vectors, inner_bias[None], weights)
    hbm = pl.BlockSpec(memory_space=pl.ANY)
    vmem = pl.BlockSpec(memory_space=pltpu.VMEM)
    shape = jax.ShapeDtypeStruct
    piece_outer = (inner // devices, width)
    piece_inner = (2 * width // devices, inner // 2)
    piece_square = (2 * width // devices, width // 2)

    def levels(piece, lead=()):
        third = (piece[0] // 3, piece[1])
        shapes = [(2,) * 5 + piece, (2,) * 4 + piece]
        shapes += [(3,) + (2,) * k + third for k in (3, 2, 1, 0)]
        return [pltpu.VMEM(lead + s, low) for s in shapes]

    loss, token_grad, outer, inner_sum, square, sums = pl.pallas_call(
        functools.partial(backward_kernel, devices, sentences),
        in_specs=[vmem] * 4 + [hbm] * 20,
        out_specs=[vmem, hbm, vmem, vmem, vmem, vmem],
        out_shape=[
            shape((8, 128), full),
            shape((rows, width), full),
            shape(piece_outer, full),
            shape(piece_inner, full),
            shape((4,) + piece_square, full),
            shape((16, width), full),
        ],
        scratch_shapes=[
            pltpu.VMEM(activated.shape, low),
            pltpu.VMEM(activated.shape, low),
            pltpu.VMEM((inner, width), low),
            pltpu.VMEM((width, inner), low),
            pltpu.VMEM((width, rows), low),
            pltpu.VMEM((rows, width), full),
            pltpu.VMEM((rows, width), full),
            pltpu.VMEM((rows, width), low),
            pltpu.VMEM((rows, width), low),
            pltpu.VMEM((rows, 128), full),
            pltpu.VMEM((rows, 128), full),
            pltpu.VMEM(inverse_totals.shape, full),
            pltpu.VMEM((2, slots, slots), low),
            pltpu.VMEM((sentences, width), full),
            pltpu.VMEM((devices, sentences, width), full),
            pltpu.VMEM((devices * sentences, width), full),
        ]
        + levels(piece_outer)
        + levels(piece_inner)
        + levels(piece_square, (4,))[1:]
        + [
            pltpu.VMEM((5, 16, width), full),
            pltpu.VMEM((5, 16, width), full),
            pltpu.SemaphoreType.DMA((64,)),
            pltpu.SemaphoreType.DMA((4,)),
            pltpu.SemaphoreType.DMA((devices,)),
            pltpu.SemaphoreType.DMA((devices,)),
            pltpu.SemaphoreType.DMA((6, 5, 3)),
            pltpu.SemaphoreType.DMA((6, 5, 3)),
            pltpu.SemaphoreType.DMA((5,)),
            pltpu.SemaphoreType.DMA((5,)),
        ],
        compiler_params=pltpu.CompilerParams(
            collective_id=0, has_side_effects=True, vmem_limit_bytes=63 * MIB
        ),
        name="decode",
    )(
        pooled,
        live_mean,
        vectors,
        groups.astype(full)[None],
        activated,
        slopes,
        second_normed,
        second_inverse,
        hidden_low,
        first_normed,
        first_inverse,
        mixture_t,
        queries_t,
        keys_t,
        values,
        tokens_t,
        probs,
        inverse_totals,
        *weights,
    )
    own = width // devices
    finals = pl.pallas_call(
        functools.partial(finish_kernel, devices),
        out_shape=[
            shape((1, 1), full),
            shape((own, width), full),
            shape((1, own), full),
            shape((own, width), full),
            shape((own, width), full),
            shape((1, own), full),
            shape((own, width), full),
            shape((1, own), full),
            shape((1, own), full),
            shape((1, own), full),
            shape((own, inner), full),
            shape((1, inner // devices), full),
            shape((inner // devices, width), full),
            shape((1, own), full),
            shape((1, own), full),
            shape((1, own), full),
        ],
        in_specs=[vmem] * 5,
        out_specs=[vmem] * 16,
        compiler_params=pltpu.CompilerParams(vmem_limit_bytes=32 * MIB),
        name="finish",
    )(loss, outer, inner_sum, square, sums)
    finals = [f.reshape(f.shape[1:]) if f.shape[0] == 1 else f for f in finals]
    return (finals[0].reshape(()), layer_output, token_grad, *finals[1:])


highest = lax.Precision.HIGHEST


def project(operand, weight):
    return jnp.dot(operand, weight, preferred_element_type=jnp.float32)


def transpose_left(left_rows, right_rows):
    return lax.dot_general(
        left_rows, right_rows, (((0,), (0,)), ((), ())), preferred_element_type=jnp.float32
    )


def transpose_right(operand, weight):
    return lax.dot_general(
        operand, weight, (((1,), (1,)), ((), ())), preferred_element_type=jnp.float32
    )


def standardize(residual):
    center = residual - jnp.mean(residual, axis=-1, keepdims=True)
    inverse = lax.rsqrt(jnp.mean(center * center, axis=-1, keepdims=True) + layer_epsilon)
    return (center * inverse, inverse)


def standardize_back(upstream, normed, inverse, scaling):
    scaled = upstream * scaling
    return inverse * (
        scaled
        - jnp.mean(scaled, axis=-1, keepdims=True)
        - normed * jnp.mean(scaled * normed, axis=-1, keepdims=True)
    )


def gelu_slope(inner_pre):
    cumulative = 0.5 * (1.0 + lax.erf(inner_pre * (1.0 / math.sqrt(2.0))))
    density = jnp.exp(-0.5 * inner_pre * inner_pre) * (1.0 / math.sqrt(2.0 * math.pi))
    return cumulative + inner_pre * density


def masked_scores(queries, key_rows, key_live):
    scores = jnp.einsum("qhd,khd->hqk", queries, key_rows, preferred_element_type=jnp.float32)
    return jnp.where(key_live[None, None, :], scores, -1e30)


def attend(pieces):
    queries, key_rows, value_rows, key_live = pieces
    scores = masked_scores(queries, key_rows, key_live)
    summit = jnp.max(scores, axis=-1, keepdims=True)
    raised = jnp.exp(scores - summit)
    totals = jnp.sum(raised, axis=-1, keepdims=True)
    weights = (raised / totals).astype(jnp.bfloat16)
    mixture = jnp.einsum("hqk,khd->qhd", weights, value_rows, preferred_element_type=jnp.float32)
    return (mixture.astype(jnp.bfloat16), (summit + jnp.log(totals))[..., 0])


def attend_back(pieces):
    queries, key_rows, value_rows, key_live, log_total, upstream = pieces
    scores = masked_scores(queries, key_rows, key_live)
    chances = jnp.exp(scores - log_total[..., None])
    toward = jnp.einsum("qhd,khd->hqk", upstream, value_rows, preferred_element_type=jnp.float32)
    score_grad = (chances * (toward - jnp.sum(chances * toward, axis=-1, keepdims=True))).astype(
        jnp.bfloat16
    )
    value_grad = jnp.einsum(
        "hqk,qhd->khd", chances.astype(jnp.bfloat16), upstream, preferred_element_type=jnp.float32
    )
    query_grad = jnp.einsum(
        "hqk,khd->qhd", score_grad, key_rows, preferred_element_type=jnp.float32
    )
    key_grad = jnp.einsum("hqk,qhd->khd", score_grad, queries, preferred_element_type=jnp.float32)
    return (
        query_grad.astype(jnp.bfloat16),
        key_grad.astype(jnp.bfloat16),
        value_grad.astype(jnp.bfloat16),
    )


def contrast_rows(row_unit, unit_rows, row_groups, groups, row_start):
    similar = cosine_scale * lax.dot_general(
        row_unit, unit_rows, (((1,), (1,)), ((), ())), precision=highest
    )
    row_ids = row_start + jnp.arange(row_unit.shape[0])
    column_ids = jnp.arange(unit_rows.shape[0])
    itself = row_ids[:, None] == column_ids[None, :]
    logits = jnp.where(itself, -1e30, similar)
    summit = jnp.max(logits, axis=-1, keepdims=True)
    raised = jnp.exp(logits - summit)
    totals = jnp.sum(raised, axis=-1, keepdims=True)
    chances = raised / totals
    log_total = summit + jnp.log(totals)
    matched = jnp.logical_and(
        row_groups[:, None] == groups[None, :], jnp.logical_not(itself)
    ).astype(jnp.float32)
    weights = matched / jnp.maximum(jnp.sum(matched, axis=-1, keepdims=True), 1.0)
    row_mass = jnp.sum(weights, axis=-1, keepdims=True)
    loss_rows = row_mass[:, 0] * log_total[:, 0] - jnp.sum(weights * similar, axis=-1)
    return (jnp.sum(loss_rows), row_mass * chances - weights)


def per_device(
    tokens,
    lengths,
    groups,
    query_weight,
    query_bias,
    key_weight,
    value_weight,
    value_bias,
    output_weight,
    output_bias,
    first_gain,
    first_shift,
    inner_weight,
    inner_bias,
    outer_weight,
    outer_bias,
    second_gain,
    second_shift,
):
    seq_count = lengths.shape[0]
    slot_count = tokens.shape[0] // seq_count
    model_width = tokens.shape[1]
    heads_shape = (seq_count, slot_count, HEADS, HD)
    queries = ((project(tokens, query_weight) + query_bias) * 0.125).astype(jnp.bfloat16)
    key_rows = project(tokens, key_weight).astype(jnp.bfloat16)
    value_rows = (project(tokens, value_weight) + value_bias).astype(jnp.bfloat16)
    key_live = jnp.arange(slot_count)[None, :] < lengths[:, None]
    head_queries = queries.reshape(heads_shape)
    head_keys = key_rows.reshape(heads_shape)
    head_values = value_rows.reshape(heads_shape)
    mixture, log_total = lax.map(attend, (head_queries, head_keys, head_values, key_live))
    mixture = mixture.reshape(tokens.shape)
    first_normed, first_inverse = standardize(
        tokens.astype(jnp.float32) + project(mixture, output_weight) + output_bias
    )
    hidden = first_normed * first_gain + first_shift
    hidden_low = hidden.astype(jnp.bfloat16)
    inner_pre = project(hidden_low, inner_weight) + inner_bias
    activated = jax.nn.gelu(inner_pre, approximate=False).astype(jnp.bfloat16)
    second_normed, second_inverse = standardize(
        hidden + project(activated, outer_weight) + outer_bias
    )
    output = second_normed * second_gain + second_shift
    live_rows = key_live.astype(jnp.float32)[:, :, None]
    counts = lengths.astype(jnp.float32)[:, None]
    pooled = (
        jnp.sum(output.reshape(seq_count, slot_count, model_width) * live_rows, axis=1) / counts
    ).astype(jnp.bfloat16)
    everyone = lax.all_gather(pooled, "dp", axis=0, tiled=True).astype(jnp.float32)
    inverse_all = lax.rsqrt(jnp.sum(everyone * everyone, axis=-1, keepdims=True) + unit_epsilon)
    unit_rows = everyone * inverse_all
    first_row = lax.axis_index("dp") * seq_count
    own_unit = lax.dynamic_slice_in_dim(unit_rows, first_row, seq_count, 0)
    own_inverse = lax.dynamic_slice_in_dim(inverse_all, first_row, seq_count, 0)
    own_groups = lax.dynamic_slice_in_dim(groups, first_row, seq_count, 0)
    part_loss, coupling = contrast_rows(own_unit, unit_rows, own_groups, groups, first_row)
    loss_value = lax.psum(part_loss, "dp")
    spread = cosine_scale * lax.dot_general(
        coupling, own_unit, (((0,), (0,)), ((), ())), precision=highest
    )
    unit_grad = cosine_scale * jnp.dot(coupling, unit_rows, precision=highest) + lax.psum_scatter(
        spread, "dp", scatter_dimension=0, tiled=True
    )
    pooled_grad = own_inverse * (
        unit_grad - own_unit * jnp.sum(own_unit * unit_grad, axis=-1, keepdims=True)
    )
    grad_output = (pooled_grad[:, None, :] / counts[:, :, None] * live_rows).reshape(tokens.shape)
    second_gain_grad = jnp.sum(grad_output * second_normed, axis=0)
    second_shift_grad = jnp.sum(grad_output, axis=0)
    grad_second = standardize_back(grad_output, second_normed, second_inverse, second_gain)
    branch_grad = grad_second.astype(jnp.bfloat16)
    outer_bias_grad = jnp.sum(branch_grad, axis=0, dtype=jnp.float32)
    outer_weight_grad = transpose_left(activated, branch_grad)
    inner_grad = (transpose_right(branch_grad, outer_weight) * gelu_slope(inner_pre)).astype(
        jnp.bfloat16
    )
    inner_bias_grad = jnp.sum(inner_grad, axis=0, dtype=jnp.float32)
    inner_weight_grad = transpose_left(hidden_low, inner_grad)
    hidden_grad = grad_second + transpose_right(inner_grad, inner_weight)
    first_gain_grad = jnp.sum(hidden_grad * first_normed, axis=0)
    first_shift_grad = jnp.sum(hidden_grad, axis=0)
    grad_first = standardize_back(hidden_grad, first_normed, first_inverse, first_gain)
    attended_grad = grad_first.astype(jnp.bfloat16)
    output_bias_grad = jnp.sum(attended_grad, axis=0, dtype=jnp.float32)
    output_weight_grad = transpose_left(mixture, attended_grad)
    mixture_grad = transpose_right(attended_grad, output_weight).astype(jnp.bfloat16)
    query_grad, key_grad, value_grad = lax.map(
        attend_back,
        (
            head_queries,
            head_keys,
            head_values,
            key_live,
            log_total,
            mixture_grad.reshape(heads_shape),
        ),
    )
    query_grad = query_grad.reshape(tokens.shape)
    key_grad = key_grad.reshape(tokens.shape)
    value_grad = value_grad.reshape(tokens.shape)
    query_weight_grad = 0.125 * transpose_left(tokens, query_grad)
    query_bias_grad = 0.125 * jnp.sum(query_grad, axis=0, dtype=jnp.float32)
    key_weight_grad = transpose_left(tokens, key_grad)
    value_weight_grad = transpose_left(tokens, value_grad)
    value_bias_grad = jnp.sum(value_grad, axis=0, dtype=jnp.float32)
    token_grad = (
        grad_first
        + 0.125 * transpose_right(query_grad, query_weight)
        + transpose_right(key_grad, key_weight)
        + transpose_right(value_grad, value_weight)
    )
    summed = tuple(
        (
            lax.psum_scatter(query_weight_grad, "dp", scatter_dimension=0, tiled=True),
            lax.psum_scatter(query_bias_grad, "dp", scatter_dimension=0, tiled=True),
            lax.psum_scatter(key_weight_grad, "dp", scatter_dimension=0, tiled=True),
            lax.psum_scatter(value_weight_grad, "dp", scatter_dimension=0, tiled=True),
            lax.psum_scatter(value_bias_grad, "dp", scatter_dimension=0, tiled=True),
            lax.psum_scatter(output_weight_grad, "dp", scatter_dimension=0, tiled=True),
            lax.psum_scatter(output_bias_grad, "dp", scatter_dimension=0, tiled=True),
            lax.psum_scatter(first_gain_grad, "dp", scatter_dimension=0, tiled=True),
            lax.psum_scatter(first_shift_grad, "dp", scatter_dimension=0, tiled=True),
            lax.psum_scatter(inner_weight_grad, "dp", scatter_dimension=0, tiled=True),
            lax.psum_scatter(inner_bias_grad, "dp", scatter_dimension=0, tiled=True),
            lax.psum_scatter(outer_weight_grad, "dp", scatter_dimension=0, tiled=True),
            lax.psum_scatter(outer_bias_grad, "dp", scatter_dimension=0, tiled=True),
            lax.psum_scatter(second_gain_grad, "dp", scatter_dimension=0, tiled=True),
            lax.psum_scatter(second_shift_grad, "dp", scatter_dimension=0, tiled=True),
        )
    )
    return (loss_value, output.astype(jnp.bfloat16), token_grad) + summed


def solution(mesh):
    placed = (
        P("dp", None),
        P("dp"),
        P(),
        P(),
        P(),
        P(),
        P(),
        P(),
        P(),
        P(),
        P(),
        P(),
        P(),
        P(),
        P(),
        P(),
        P(),
        P(),
    )
    devices = mesh.shape["dp"]
    body = functools.partial(linked_device, devices) if devices == 32 else per_device
    return jax.shard_map(
        body,
        mesh=mesh,
        in_specs=placed,
        out_specs=(
            P(),
            P("dp", None),
            P("dp", None),
            P("dp", None),
            P("dp"),
            P("dp", None),
            P("dp", None),
            P("dp"),
            P("dp", None),
            P("dp"),
            P("dp"),
            P("dp"),
            P("dp", None),
            P("dp"),
            P("dp", None),
            P("dp"),
            P("dp"),
            P("dp"),
        ),
        check_vma=False,
    )
```

```python
import functools
import math

import jax
import jax.numpy as jnp
from jax import lax
from jax.experimental import pallas as pl
from jax.experimental.pallas import tpu as pltpu
from jax.sharding import PartitionSpec as P

HEADS = 12
HD = 64
cosine_scale = 20.0
layer_epsilon = 1e-06
unit_epsilon = 1e-06
low = jnp.bfloat16
full = jnp.float32
MIB = 1 << 20


def dot(left, right, left_axis=1, right_axis=0):
    return lax.dot_general(
        left, right, (((left_axis,), (right_axis,)), ((), ())), preferred_element_type=full
    )


def gelu_pair(value):
    size = jnp.abs(value)
    ratio = pl.reciprocal(1.0 + (0.3275911 / math.sqrt(2.0)) * size, approx=True)
    bell = jnp.exp(value * value * -0.5)
    series = 0.5 * 1.061405429
    for factor in (-1.453152027, 1.421413741, -0.284496736, 0.254829592):
        series = series * ratio + 0.5 * factor
    half_tail = series * ratio * bell
    cumulative = jnp.where(value >= 0.0, 1.0 - half_tail, half_tail)
    return value * cumulative, cumulative + value * bell * (1.0 / math.sqrt(2.0 * math.pi))


def widen(column, lanes):
    return jnp.concatenate([column] * (lanes // 128), axis=1)


def standardized(residual):
    center = residual - jnp.mean(residual, axis=1, keepdims=True)
    inverse = lax.rsqrt(jnp.mean(center * center, axis=1, keepdims=True) + layer_epsilon)
    return center * inverse, inverse


def forward_kernel(
    sentences,
    lengths,
    query_bias,
    value_bias,
    output_bias,
    first_gain,
    first_shift,
    inner_bias,
    outer_bias,
    second_gain,
    second_shift,
    tokens_in,
    query_weight,
    key_weight,
    value_weight,
    output_weight,
    inner_weight,
    outer_weight,
    layer_output_out,
    pooled,
    live_mean,
    queries_t_out,
    keys_t_out,
    values_out,
    mixture_t_out,
    tokens_t_out,
    probs_out,
    inverse_totals_out,
    first_normed_out,
    first_inverse_out,
    hidden_t_out,
    second_normed_out,
    second_inverse_out,
    activated_t_out,
    slopes_out,
    tokens,
    w_query,
    w_key,
    w_value,
    w_output,
    w_inner,
    w_outer,
    layer_output,
    queries_t,
    keys_t,
    values,
    mixture_t,
    tokens_t,
    inverse_totals,
    first_normed,
    first_inverse,
    hidden_low,
    hidden_t,
    second_normed,
    second_inverse,
    activated,
    activated_t,
    slopes,
    mask_block,
    in_sems,
    out_sems,
    prob_sems,
    feed_sems,
):
    rows, width = tokens.shape
    slots = rows // sentences
    inner = w_inner.shape[1]
    wide = slopes.shape[2]
    loads = [
        pltpu.make_async_copy(source, target, in_sems.at[place])
        for place, (source, target) in enumerate(
            (
                (tokens_in, tokens),
                (query_weight, w_query),
                (key_weight, w_key),
                (value_weight, w_value),
                (output_weight, w_output),
                (inner_weight, w_inner),
                (outer_weight, w_outer),
            )
        )
    ]
    for copy in loads:
        copy.start()
    stores = []

    def store(source, target):
        copy = pltpu.make_async_copy(source, target, out_sems.at[len(stores)])
        copy.start()
        stores.append(copy)

    def line(ref):
        return ref[...].reshape(1, ref.shape[0])

    key_rows = activated.at[:, 0:width]
    values_t = activated.at[0:width, width : width + rows]

    def prob_slot(pair, unit):
        start = pl.multiple_of((lax.rem(pair, 3) * 2 + unit // 2) * slots, slots)
        lane = unit % 2 * slots
        return activated_t.at[pl.ds(start, slots), lane : lane + slots]

    slot_ids = lax.broadcasted_iota(jnp.int32, (slots, 128), 0)
    lane_ids = lax.broadcasted_iota(jnp.int32, (slots, 128), 1)
    for sentence in range(sentences):
        mask_block[sentence] = jnp.where(
            jnp.logical_and(slot_ids >= lengths[sentence], lane_ids == 0), -1e30, 0.0
        ).astype(low)

    for copy in loads[:4]:
        copy.wait()
    span = 512
    pieces = [slice(start, start + span) for start in range(0, rows, span)]
    bias = line(query_bias)
    for at in pieces:
        queries_t[:, at] = ((dot(tokens[at, :], w_query[...]) + bias) * 0.125).astype(low).T
    for at in pieces:
        result = dot(tokens[at, :], w_key[...]).astype(low)
        key_rows[at, :] = result
        keys_t[:, at] = result.T
    bias = line(value_bias)
    for at in pieces:
        result = (dot(tokens[at, :], w_value[...]) + bias).astype(low)
        values[at, :] = result
        values_t[:, at] = result.T
    for at in pieces:
        tokens_t[:, at] = tokens[at, :].T
    store(queries_t, queries_t_out)
    store(keys_t, keys_t_out)
    store(values, values_out)
    store(tokens_t, tokens_t_out)

    pick_row = jnp.where(
        lax.broadcasted_iota(jnp.int32, (128, slots), 0) == 0, 1.0, 0.0
    ).astype(low)
    empty = jnp.zeros((HD, slots), low)

    units = [(sentence, half) for sentence in range(sentences) for half in range(2)]

    def prob_copies(pair):
        return [
            pltpu.make_async_copy(
                prob_slot(pair, unit),
                probs_out.at[sentence * HEADS + pair * 2 + half],
                prob_sems.at[lax.rem(pair, 3), unit],
            )
            for unit, (sentence, half) in enumerate(units)
        ]

    def head_pair(exact, pair, carry):
        start = pl.multiple_of(pair * 128, 128)

        @pl.when(pair >= 3)
        def _():
            for copy in prob_copies(pair):
                copy.wait()

        def spans(unit):
            sentence = units[unit][0]
            return slice(sentence * slots, (sentence + 1) * slots)

        def get_scores(unit):
            sentence, half = units[unit]
            left = jnp.concatenate(
                [key_rows[spans(unit), pl.ds(start, 128)], mask_block[sentence]], axis=1
            )
            own = queries_t[pl.ds(pl.multiple_of(start + half * HD, HD), HD), spans(unit)]
            parts = [own, empty] if half == 0 else [empty, own]
            return dot(left, jnp.concatenate(parts + [pick_row], axis=0))

        def get_probs(unit, scores):
            sentence, half = units[unit]
            if exact:
                summit = jnp.max(scores, axis=0, keepdims=True)
            totals = jnp.zeros((8, slots), full)
            slot = prob_slot(pair, unit)
            step = 64
            parts = []
            for place in range(0, slots, step):
                piece = scores[place : place + step, :]
                piece = jnp.exp(piece - summit if exact else piece)
                totals = totals + jnp.sum(piece.reshape(step // 8, 8, slots), axis=0)
                piece = piece.astype(low)
                slot[place : place + step, :] = piece
                parts.append(piece)
            inverse = 1.0 / jnp.sum(totals, axis=0, keepdims=True)
            inverse_totals[sentence * HEADS + pair * 2 + half] = inverse
            return jnp.concatenate(parts, axis=0), inverse

        def mix(unit, raised, inverse):
            row = pl.multiple_of(start + units[unit][1] * HD, HD)
            mixed = dot(values_t[pl.ds(row, HD), spans(unit)], raised) * inverse
            mixture_t[pl.ds(row, HD), spans(unit)] = mixed.astype(low)

        count = len(units)
        scored, raised = {}, {}
        for turn in range(count + 2):
            if turn < count:
                scored[turn] = get_scores(turn)
            if 0 <= turn - 1 < count:
                raised[turn - 1] = get_probs(turn - 1, scored.pop(turn - 1))
            if turn >= 2:
                mix(turn - 2, *raised.pop(turn - 2))
        for copy in prob_copies(pair):
            copy.start()
        return carry

    head_ids = lax.broadcasted_iota(jnp.int32, (16, width), 0)
    column_ids = lax.broadcasted_iota(jnp.int32, (16, width), 1)
    selector = jnp.where(head_ids == lax.div(column_ids, HD), 1.0, 0.0).astype(low)

    def largest(ref):
        return jnp.max(dot(selector, ref[...] * ref[...]), axis=1, keepdims=True)

    bound = jnp.max(largest(queries_t) * largest(keys_t))

    @pl.when(bound < 1600.0)
    def _():
        lax.fori_loop(0, HEADS // 2, functools.partial(head_pair, False), 0)

    @pl.when(jnp.logical_not(bound < 1600.0))
    def _():
        lax.fori_loop(0, HEADS // 2, functools.partial(head_pair, True), 0)

    store(mixture_t, mixture_t_out)
    store(inverse_totals, inverse_totals_out)

    loads[4].wait()
    bias, gain, shift = line(output_bias), line(first_gain), line(first_shift)
    span, step = 256, 32
    for start in range(0, rows, span):
        attended = dot(mixture_t[:, start : start + span], w_output[...], 0, 0)
        for place in range(0, span, step):
            at = slice(start + place, start + place + step)
            normed, inverse = standardized(
                tokens[at, :].astype(full) + attended[place : place + step] + bias
            )
            first_normed[at, :] = normed
            first_inverse[at, :] = jnp.broadcast_to(inverse, (step, 128))
            hidden_low[at, :] = (normed * gain + shift).astype(low)
        at = slice(start, start + span)
        hidden_t[:, at] = hidden_low[at, :].T
    store(first_normed, first_normed_out)
    store(first_inverse, first_inverse_out)
    store(hidden_t, hidden_t_out)

    loads[5].wait()
    for pair in range(HEADS // 2 - 3, HEADS // 2):
        for copy in prob_copies(pair):
            copy.wait()

    def feed_copies(index):
        start = pl.multiple_of(index * wide, wide)
        return (
            pltpu.make_async_copy(
                activated_t.at[pl.ds(start, wide)],
                activated_t_out.at[pl.ds(start, wide)],
                feed_sems.at[index, 0],
            ),
            pltpu.make_async_copy(
                slopes.at[index], slopes_out.at[index], feed_sems.at[index, 1]
            ),
        )

    def feed(index, carry):
        start = pl.multiple_of(index * wide, wide)
        weight = w_inner[:, pl.ds(start, wide)]
        offset = inner_bias[:, pl.ds(start, wide)]
        block, step = 128, 16

        def gelu_block(place, pre):
            at = slice(place, place + block)
            parts = []
            for piece in range(0, block, step):
                value, slope = gelu_pair(pre[piece : piece + step] + offset)
                slopes[index, place + piece : place + piece + step, :] = slope.astype(low)
                parts.append(value.astype(low))
            value = jnp.concatenate(parts, axis=0)
            activated[at, pl.ds(start, wide)] = value
            activated_t[pl.ds(start, wide), at] = value.T

        before = None
        for place in range(0, rows, block):
            pre = dot(hidden_low[place : place + block, :], weight)
            if before is not None:
                gelu_block(place - block, before)
            before = pre
        gelu_block(rows - block, before)
        for copy in feed_copies(index):
            copy.start()
        return carry

    lax.fori_loop(0, inner // wide, feed, 0)

    loads[6].wait()
    bias, gain_2, shift_2 = line(outer_bias), line(second_gain), line(second_shift)
    live_sums = [jnp.zeros((8, width), full) for _ in range(sentences)]
    for start in range(0, rows, span):
        branch = dot(activated[start : start + span, :], w_outer[...])
        sentence = start // slots
        length = lengths[sentence]
        for place in range(0, span, step):
            at = slice(start + place, start + place + step)
            hidden = first_normed[at, :] * gain + shift
            normed, inverse = standardized(hidden + branch[place : place + step] + bias)
            second_normed[at, :] = normed
            layer_output[at, :] = (normed * gain_2 + shift_2).astype(low)
            slot_row = lax.broadcasted_iota(jnp.int32, (step, 128), 0) + (
                start + place - sentence * slots
            )
            live = jnp.where(slot_row < length, 1.0, 0.0)
            live_sums[sentence] = live_sums[sentence] + jnp.sum(
                (normed * widen(live, width)).reshape(step // 8, 8, width), axis=0
            )
            second_inverse[at, :] = inverse * live * (1.0 / length.astype(full))
        at = slice(start, start + span)
        store(second_normed.at[at], second_normed_out.at[at])
        store(layer_output.at[at], layer_output_out.at[at])
        store(second_inverse.at[at], second_inverse_out.at[at])
    for sentence in range(sentences):
        mean_normed = jnp.sum(live_sums[sentence], axis=0, keepdims=True) / lengths[
            sentence
        ].astype(full)
        live_mean[sentence] = jnp.broadcast_to(mean_normed, (8, width))
        vector = (mean_normed * gain_2 + shift_2).astype(low).astype(full)
        pooled[sentence] = jnp.broadcast_to(vector, (8, width))
    for index in range(inner // wide):
        for copy in feed_copies(index):
            copy.wait()
    for copy in stores:
        copy.wait()


def forward(lengths, tokens, vectors, inner_bias, weights):
    sentences = lengths.shape[0]
    rows, width = tokens.shape
    slots = rows // sentences
    inner = weights[4].shape[1]
    wide = 1024
    hbm = pl.BlockSpec(memory_space=pl.ANY)
    vmem = pl.BlockSpec(memory_space=pltpu.VMEM)
    shape = jax.ShapeDtypeStruct
    kept = [
        ((rows, width), low),
        ((width, rows), low),
        ((width, rows), low),
        ((rows, width), low),
        ((width, rows), low),
        ((width, rows), low),
        ((sentences * HEADS, 1, slots), full),
        ((rows, width), full),
        ((rows, 128), full),
        ((rows, width), low),
        ((width, rows), low),
        ((rows, width), full),
        ((rows, 128), full),
        ((rows, inner), low),
        ((inner, rows), low),
        ((inner // wide, rows, wide), low),
    ]
    outs = [shape(*k) for k in kept]
    per_sentence = shape((sentences, 8, width), full)
    probs = shape((sentences * HEADS, slots, slots), low)
    return pl.pallas_call(
        functools.partial(forward_kernel, sentences),
        in_specs=[pl.BlockSpec(memory_space=pltpu.SMEM)] + [vmem] * 9 + [hbm] * 7,
        out_specs=[hbm, vmem, vmem] + [hbm] * 14,
        out_shape=[outs[0], per_sentence, per_sentence]
        + outs[1:6]
        + [probs]
        + outs[6:9]
        + outs[10:13]
        + outs[14:],
        scratch_shapes=[pltpu.VMEM((rows, width), low)]
        + [pltpu.VMEM(w.shape, low) for w in weights]
        + [pltpu.VMEM(*k) for k in kept]
        + [
            pltpu.VMEM((sentences, slots, 128), low),
            pltpu.SemaphoreType.DMA((7,)),
            pltpu.SemaphoreType.DMA((32,)),
            pltpu.SemaphoreType.DMA((3, 2 * sentences)),
            pltpu.SemaphoreType.DMA((inner // wide, 2)),
        ],
        compiler_params=pltpu.CompilerParams(vmem_limit_bytes=63 * MIB),
        name="encode",
    )(lengths, *vectors[:5], inner_bias, *vectors[5:], tokens, *weights)


SETS = ("A0", "A1", "A2", "B0", "B1", "B2", "C0", "C1", "C2", "C3")

SCHEDULE = {
    "a2": (("A0", 0),),
    "g0": (("A1", 0),),
    "w0": (("A2", 0),),
    "g1": (("A0", 1),),
    "w1": (("A1", 1), ("B0", 0),),
    "g2": (("A2", 1),),
    "w2": (("A0", 2), ("B1", 0),),
    "h0": (("A1", 2), ("B0", 1), ("B2", 0),),
    "h1": (("A0", 3), ("A2", 2), ("B1", 1),),
    "m": (("A1", 3), ("B0", 2),),
    "p0": (("B2", 1), ("C0", 0),),
    "p1": (("A2", 3), ("B1", 2),),
    "p2": (("B0", 3), ("B2", 2),),
    "p3": (("C0", 1), ("C1", 0),),
    "c1": (("B1", 3),),
    "p5": (("B2", 3), ("C0", 2), ("C2", 0),),
    "c2": (("C1", 1),),
    "t1": (("C0", 3), ("C1", 2), ("C2", 1), ("C3", 0),),
    "end": (("C2", 2), ("C1", 3), ("C3", 1), ("C2", 3), ("C3", 2), ("C3", 3),),
}


class Summation:
    def __init__(self, name, send, held, out, sems, me, links):
        self.send, self.held, self.out = send, held, out
        self.place = SETS.index(name)
        self.odd = self.place % 2
        self.send_sems, self.recv_sems = sems
        self.me, self.links = me, links
        self.third = held[0].shape[-2] // 3

    def side(self, link, away):
        bit = self.links[link][0]
        return 1 - bit if away else bit

    def halves(self, stage, away):
        h = self.third

        def side(link):
            return self.side(link, away)

        if stage == 0:
            return [(self.send.at[:, :, :, :, side("core")], "core")]
        r = self.held[stage - 1]
        if stage == 1:
            return [
                (r.at[:, :, :, side("x"), pl.ds(0, h)], "x"),
                (r.at[:, :, side("y"), :, pl.ds(h, h)], "y"),
                (r.at[:, side("z0"), :, :, pl.ds(2 * h, h)], "z0"),
            ]
        last = (r.at[2, :, side("y")], "y") if self.odd else (r.at[2, :, :, side("x")], "x")
        return [(r.at[0, :, :, side("y")], "y"), (r.at[1, :, :, side("x")], "x"), last]

    def quarter(self, part, far, near):
        link = ("z0", "z0", "x" if self.odd else "y")[part]
        source = self.held[2].at[part, self.side("z1", far), self.side(link, near)]
        return source, self.me + far * self.links["z1"][1] + near * self.links[link][1]

    def copies(self, stage):
        moves = []
        if stage < 3:
            target = self.held[stage]
            for part, (source, link) in enumerate(self.halves(stage, 1)):
                goal = target if stage == 0 else target.at[part]
                moves.append((source, goal, self.me + self.links[link][1]))
        else:
            for part in range(3):
                for slot, (far, near) in enumerate(((0, 1), (1, 0), (1, 1))):
                    source, device = self.quarter(part, far, near)
                    moves.append((source, self.held[3].at[part, slot], device))
        return [self.copy(stage, *move) for move in moves]

    def copy(self, stage, source, goal, device):
        return pltpu.make_async_remote_copy(
            src_ref=source,
            dst_ref=goal,
            send_sem=self.send_sems.at[self.place, stage],
            recv_sem=self.recv_sems.at[self.place, stage],
            device_id=(device,),
            device_id_type=pl.DeviceIdType.MESH,
        )

    def start(self, stage=0):
        for copy in self.copies(stage):
            copy.start()

    def step(self, stage):
        held = self.held[stage]
        whole = self.copy(stage, held, held, self.me + self.links["core"][1])
        whole.wait_send()
        whole.wait_recv()
        if stage < 3:
            for part, (kept, _) in enumerate(self.halves(stage, 0)):
                if stage == 0:
                    held[...] = held[...] + kept[...]
                else:
                    held[part] = held[part] + kept[...]
            self.start(stage + 1)
        else:
            h = self.third
            for part in range(3):
                total = self.quarter(part, 0, 0)[0][...].astype(full)
                for slot in range(3):
                    total = total + self.held[3][part, slot].astype(full)
                self.out[part * h : part * h + h, :] = total


def contrast(points, groups):
    count = points.shape[0]
    inverse = lax.rsqrt(jnp.sum(points * points, axis=1, keepdims=True) + unit_epsilon)
    unit = points * inverse
    similar = cosine_scale * lax.dot_general(
        unit,
        unit,
        (((1,), (1,)), ((), ())),
        precision=lax.Precision.HIGHEST,
        preferred_element_type=full,
    )
    rows = lax.broadcasted_iota(jnp.int32, (count, count), 0)
    columns = lax.broadcasted_iota(jnp.int32, (count, count), 1)
    itself = rows == columns
    logits = jnp.where(itself, -1e30, similar)
    summit = jnp.max(logits, axis=1, keepdims=True)
    raised = jnp.exp(logits - summit)
    totals = jnp.sum(raised, axis=1, keepdims=True)
    chances = raised / totals
    log_total = summit + jnp.log(totals)
    across = jnp.broadcast_to(groups, (count, count))
    matched = jnp.where(
        jnp.logical_and(across == across.T, jnp.logical_not(itself)), 1.0, 0.0
    )
    weights = matched / jnp.maximum(jnp.sum(matched, axis=1, keepdims=True), 1.0)
    row_mass = jnp.sum(weights, axis=1, keepdims=True)
    loss_rows = row_mass * log_total - jnp.sum(weights * similar, axis=1, keepdims=True)
    loss = jnp.sum(loss_rows, axis=0, keepdims=True)
    coupling = row_mass * chances - weights
    unit_grad = cosine_scale * lax.dot_general(
        coupling + coupling.T,
        unit,
        (((1,), (0,)), ((), ())),
        precision=lax.Precision.HIGHEST,
        preferred_element_type=full,
    )
    grad = inverse * (unit_grad - unit * jnp.sum(unit * unit_grad, axis=1, keepdims=True))
    return loss, grad


def backward_kernel(
    devices,
    sentences,
    pooled,
    live_mean,
    first_gain,
    second_gain,
    groups,
    activated_t_in,
    slopes_in,
    second_normed_in,
    second_inverse_in,
    hidden_t_in,
    first_normed_in,
    first_inverse_in,
    mixture_t_in,
    queries_t_in,
    keys_t_in,
    values_in,
    tokens_t_in,
    probs_in,
    inverse_totals_in,
    query_weight,
    key_weight,
    value_weight,
    output_weight,
    inner_weight,
    outer_weight,
    packed_out,
    loss_out,
    outer_out,
    inner_out,
    square_out,
    sums_out,
    act_t,
    inner_grad,
    w_rows,
    w_columns,
    normed,
    grads,
    branch,
    hidden_t,
    inverses,
    inverse_totals,
    own,
    gathered,
    points,
    outer_send,
    outer_0,
    outer_1,
    outer_2,
    outer_3,
    inner_send,
    inner_0,
    inner_1,
    inner_2,
    inner_3,
    square_1,
    square_2,
    square_3,
    sum_held,
    sum_recv,
    load_sems,
    prob_sems,
    gather_sems,
    set_send,
    set_recv,
    sum_sems,
    credit,
):
    me = lax.axis_index("dp")
    rows, width = normed.shape
    slots = rows // sentences
    parts, _, wide = inner_grad.shape
    heads = width // HD
    own_rows = width // devices

    def link(mask):
        bit = lax.rem(lax.div(me, mask), 2)
        return bit, mask * (1 - 2 * bit)

    links = {"core": link(1), "x": link(2), "y": link(4), "z0": link(8), "z1": link(16)}
    load_count = iter(range(36))

    def load(source, target):
        copy = pltpu.make_async_copy(source, target, load_sems.at[next(load_count)])
        copy.start()
        return copy

    get_normed = load(second_normed_in, normed)
    get_second = load(second_inverse_in, inverses)
    get_act = load(activated_t_in, act_t)
    get_outer = load(outer_weight, w_rows)
    get_slopes = [load(slopes_in.at[part], inner_grad.at[part]) for part in range(parts)]
    get_hidden = load(hidden_t_in, hidden_t)
    get_inner = load(inner_weight, w_columns)
    get_totals = load(inverse_totals_in, inverse_totals)

    barrier = pltpu.get_barrier_semaphore()

    def greet(step, carry):
        other = lax.rem(me + step, devices)
        pl.semaphore_signal(
            barrier, inc=1, device_id=(other,), device_id_type=pl.DeviceIdType.MESH
        )
        return carry

    lax.fori_loop(1, devices, greet, 0)
    for sentence in range(sentences):
        own[sentence : sentence + 1, :] = pooled[sentence, 0:1, :]
    gathered[me] = own[...]
    pl.semaphore_wait(barrier, devices - 1)

    def gather_copy(step):
        return pltpu.make_async_remote_copy(
            src_ref=own,
            dst_ref=gathered.at[me],
            send_sem=gather_sems.at[0],
            recv_sem=gather_sems.at[1],
            device_id=(lax.rem(me + step, devices),),
            device_id_type=pl.DeviceIdType.MESH,
        )

    def gather_start(step, carry):
        gather_copy(step).start()
        return carry

    lax.fori_loop(1, devices, gather_start, 0)
    others = gathered.at[pl.ds(0, devices - 1)]
    whole = pltpu.make_async_remote_copy(
        src_ref=others,
        dst_ref=others,
        send_sem=gather_sems.at[0],
        recv_sem=gather_sems.at[1],
        device_id=(lax.rem(me + 1, devices),),
        device_id_type=pl.DeviceIdType.MESH,
    )
    whole.wait_send()
    whole.wait_recv()
    for device in range(devices):
        points[device * sentences : (device + 1) * sentences, :] = gathered[device]
    loss, pooled_grad = contrast(
        points[...], groups[...].astype(full).reshape(1, groups.shape[0])
    )
    loss_out[...] = jnp.broadcast_to(loss, loss_out.shape)
    row_ids = lax.broadcasted_iota(jnp.int32, (devices * sentences, width), 0)
    own_grads = [
        jnp.sum(
            jnp.where(row_ids == me * sentences + sentence, pooled_grad, 0.0),
            axis=0,
            keepdims=True,
        )
        for sentence in range(sentences)
    ]
    vector_sums = sum_held.at[0]
    vector_sums[...] = jnp.zeros_like(vector_sums)
    vector_sums[1:2, :] = sum(
        own_grads[sentence] * live_mean[sentence, 0:1, :] for sentence in range(sentences)
    )
    vector_sums[2:3, :] = sum(own_grads)

    sets = {}

    def add_set(name, send, held, out):
        sets[name] = Summation(name, send, held, out, (set_send, set_recv), me, links)

    def columns(ref, start, size):
        return ref.at[(slice(None),) * (len(ref.shape) - 1) + (pl.ds(start, size),)]

    third = width // 3
    for part in range(3):
        lanes = (part * third, third)
        add_set(
            f"A{part}",
            columns(outer_send, *lanes),
            [columns(r, *lanes) for r in (outer_0, outer_1, outer_2, outer_3)],
            columns(outer_out, *lanes),
        )
        half = wide // 2
        lanes = (part * half, half)
        add_set(
            f"B{part}",
            columns(inner_send, *lanes),
            [columns(r, *lanes) for r in (inner_0, inner_1, inner_2, inner_3)],
            columns(inner_out, *lanes),
        )
    piece_rows, piece_columns = outer_send.shape[-2] // 2, width // 2
    square_sends = [
        outer_send.at[
            :,
            :,
            :,
            :,
            :,
            pl.ds(place % 2 * piece_rows, piece_rows),
            pl.ds(place // 2 * piece_columns, piece_columns),
        ]
        for place in range(4)
    ]
    for place in range(4):
        first = outer_0.at[
            :,
            :,
            :,
            :,
            pl.ds(place % 2 * piece_rows, piece_rows),
            pl.ds(place // 2 * piece_columns, piece_columns),
        ]
        add_set(
            f"C{place}",
            square_sends[place],
            [first] + [r.at[place] for r in (square_1, square_2, square_3)],
            square_out.at[place],
        )
    second_done = []

    def tick(point):
        for name, stage in SCHEDULE.get(point, ()):
            sets[name].step(stage)
            if name[0] == "A" and stage == 1:
                second_done.append(name)
                if len(second_done) == 3:
                    pl.semaphore_signal(
                        credit,
                        inc=1,
                        device_id=(me + links["core"][1],),
                        device_id_type=pl.DeviceIdType.MESH,
                    )

    def piece_at(device):
        return device // 16, device // 8 % 2, device // 4 % 2, device // 2 % 2, device % 2

    get_normed.wait()
    get_second.wait()
    bias_sum = jnp.zeros((8, width), full)
    step = 32
    for sentence in range(sentences):
        scaled = own_grads[sentence] * second_gain[...].reshape(1, width)
        shifted = scaled - jnp.mean(scaled, axis=1, keepdims=True)

        def second_back(index, total):
            at = pl.ds(pl.multiple_of(sentence * slots + index * step, step), step)
            unit = normed[at, :]
            mass = jnp.mean(unit * scaled, axis=1, keepdims=True)
            grad = widen(inverses[at, :], width) * (shifted - unit * mass)
            grads[at, :] = grad
            rounded = grad.astype(low)
            branch[at, :] = rounded
            return total + jnp.sum(
                rounded.astype(full).reshape(step // 8, 8, width), axis=0
            )

        bias_sum = lax.fori_loop(0, slots // step, second_back, bias_sum)
    vector_sums[0:1, :] = jnp.sum(bias_sum, axis=0, keepdims=True)
    get_normed_2 = load(first_normed_in, normed)
    get_first = load(first_inverse_in, inverses)

    get_act.wait()
    piece = outer_send.shape[-2]
    for part in range(3):
        right = branch[:, part * third : (part + 1) * third]
        for block in range(4):
            result = dot(act_t[block * 8 * piece : (block + 1) * 8 * piece, :], right).astype(low)
            for place in range(8):
                sets[f"A{part}"].send[piece_at(block * 8 + place)] = result[
                    place * piece : (place + 1) * piece, :
                ]
        sets[f"A{part}"].start()
        tick(f"a{part}")

    get_values = load(values_in, act_t.at[0:rows, 0:width])
    steps = heads // 2 * sentences

    def prob_slot(index, half):
        start = pl.multiple_of(rows + lax.rem(index, 4) * slots, slots)
        return act_t.at[pl.ds(start, slots), half * slots : (half + 1) * slots]

    def prob_copies(index):
        first = lax.rem(index, sentences) * heads + lax.div(index, sentences) * 2
        return [
            pltpu.make_async_copy(
                probs_in.at[first + half],
                prob_slot(index, half),
                prob_sems.at[lax.rem(index, 4), half],
            )
            for half in range(2)
        ]

    for index in range(3):
        for copy in prob_copies(index):
            copy.start()

    get_outer.wait()
    get_hidden.wait()
    block, step = wide // 2, 32

    def slope_dot(index):
        return dot(branch[...], w_rows[index * block : (index + 1) * block, :], 1, 1)

    def slope_block(index, result):
        part, lanes = index // 2, slice(index % 2 * block, (index % 2 + 1) * block)
        total = jnp.zeros((8, block), full)
        for place in range(0, rows, step):
            at = slice(place, place + step)
            value = (result[at] * inner_grad[part, at, lanes].astype(full)).astype(low)
            inner_grad[part, at, lanes] = value
            total = total + jnp.sum(value.astype(full).reshape(step // 8, 8, block), axis=0)
        total = jnp.sum(total, axis=0, keepdims=True)
        for piece in range(0, block, 256):
            flat = index * block + piece
            row, lane = 8 + flat // width, flat % width
            vector_sums[row : row + 1, lane : lane + 256] = total[:, piece : piece + 256]

    before = slope_dot(0)
    for index in range(2 * parts):
        part = index // 2
        result = slope_dot(index + 1) if index + 1 < 2 * parts else None
        if index % 2 == 0:
            get_slopes[part].wait()
        slope_block(index, before)
        before = result
        if index % 2 == 0:
            continue
        tick(f"g{part}")
        for piece in range(2):
            result = dot(
                hidden_t[piece * (width // 2) : (piece + 1) * (width // 2), :], inner_grad[part]
            )
            for place in range(devices // 2):
                value = result[place * own_rows : (place + 1) * own_rows]
                sets[f"B{part}"].send[piece_at(piece * (devices // 2) + place)] = jnp.concatenate(
                    [value[:, : wide // 2], value[:, wide // 2 :]], axis=0
                ).astype(low)
        sets[f"B{part}"].start()
        tick(f"w{part}")
    mixture_t = hidden_t
    get_mixture = load(mixture_t_in, mixture_t)
    square_loads = [
        load(source, w_rows.at[pl.ds(place * width, width)])
        for place, source in enumerate((output_weight, query_weight, key_weight, value_weight))
    ]

    get_inner.wait()
    get_normed_2.wait()
    get_first.wait()
    span, step = rows // 2, 32
    gain = first_gain[...].reshape(1, width)

    def hidden_dot(start):
        total = None
        for part in range(parts):
            term = dot(
                inner_grad[part, start : start + span, :],
                w_columns[:, part * wide : (part + 1) * wide],
                1,
                1,
            )
            total = term if total is None else total + term
        return total

    def first_back(start, total, gain_sum, shift_sum, bias_sum):
        for place in range(0, span, step):
            at = slice(start + place, start + place + step)
            upstream = grads[at, :] + total[place : place + step]
            unit = normed[at, :]
            gain_sum = gain_sum + jnp.sum((upstream * unit).reshape(step // 8, 8, width), axis=0)
            shift_sum = shift_sum + jnp.sum(upstream.reshape(step // 8, 8, width), axis=0)
            scaled = upstream * gain
            center = scaled - jnp.mean(scaled, axis=1, keepdims=True)
            grad = widen(inverses[at, :], width) * (
                center - unit * jnp.mean(scaled * unit, axis=1, keepdims=True)
            )
            grads[at, :] = grad
            rounded = grad.astype(low)
            branch[at, :] = rounded
            bias_sum = bias_sum + jnp.sum(
                rounded.astype(full).reshape(step // 8, 8, width), axis=0
            )
        return gain_sum, shift_sum, bias_sum

    zero = jnp.zeros((8, width), full)
    state = (zero, zero, zero)
    before = hidden_dot(0)
    for start in range(span, rows + span, span):
        result = hidden_dot(start) if start < rows else None
        state = first_back(start - span, before, *state)
        before = result
        tick(f"h{start // span - 1}")
    for place, total in zip((3, 4, 5), state):
        vector_sums[place : place + 1, :] = jnp.sum(total, axis=0, keepdims=True)

    get_queries = load(queries_t_in, w_columns.at[:, 0:rows])
    get_keys = load(keys_t_in, w_columns.at[:, rows : 2 * rows])
    tokens_t = inner_grad.at[1, 0:width, :]
    get_tokens = load(tokens_t_in, tokens_t)

    def square_pieces(place, index, result):
        lanes = pl.ds(index * 128, 128)
        for device in range(devices):
            at = slice(device * own_rows, (device + 1) * own_rows)
            z1, z0, y, x, core = piece_at(device)
            square_sends[place].at[z1, z0, y, x, core][:, lanes] = jnp.concatenate(
                [result[at, 0:128], result[at, 128:256]], axis=0
            ).astype(low)

    get_mixture.wait()
    for index in range(3):
        square_pieces(0, index, dot(mixture_t[...], branch[:, index * 256 : (index + 1) * 256]))
    pl.semaphore_wait(credit, 1)
    sets["C0"].start()
    tick("o")

    square_loads[0].wait()
    get_totals.wait()
    upstream_t = inner_grad.at[0, 0:width, :]
    for sentence in range(sentences):
        spans = slice(sentence * slots, (sentence + 1) * slots)
        result = dot(w_rows[0:width, :], branch[spans, :], 1, 1)
        for head in range(heads):
            at = slice(head * HD, (head + 1) * HD)
            place = sentence * heads + head
            value = result[at] * inverse_totals[place, 0:1, :]
            mass = jnp.sum(value * mixture_t[at, spans].astype(full), axis=0, keepdims=True)
            inverse_totals[place] = mass
            upstream_t[at, spans] = value.astype(low)
    tick("m")

    get_queries.wait()
    get_keys.wait()
    get_values.wait()
    get_tokens.wait()
    empty = jnp.zeros((HD, slots), low)
    value_grads, key_grads = act_t.at[0:rows, 0:width], branch
    toward_refs = [normed.at[at : at + slots, 0:slots] for at in (0, slots)]
    score_refs = [inner_grad.at[2, at : at + slots, 0:slots] for at in (0, slots)]

    def projection_grads(group):
        at = slice(group * 256, (group + 1) * 256)
        left = tokens_t[...]
        square_pieces(1 + group, 0, dot(left, w_columns[at, 0:rows], 1, 1) * 0.125)
        square_pieces(1 + group, 1, dot(left, key_grads[:, at]))
        square_pieces(1 + group, 2, dot(left, value_grads[:, at]))
        sets[f"C{1 + group}"].start()

    def head_pair(index, carry):
        pair, sentence = lax.div(index, sentences), lax.rem(index, sentences)
        start = pl.multiple_of(pair * 128, 128)
        spans = pl.ds(pl.multiple_of(sentence * slots, slots), slots)
        key_spans = pl.ds(pl.multiple_of(rows + sentence * slots, slots), slots)
        for copy in prob_copies(index):
            copy.wait()

        @pl.when(index + 3 < steps)
        def _():
            for copy in prob_copies(index + 3):
                copy.start()

        def row(half):
            return pl.ds(pl.multiple_of(start + half * HD, HD), HD)

        def masked(half, value):
            return jnp.concatenate([value, empty] if half == 0 else [empty, value], axis=0)

        def toward(half):
            upstream = masked(half, upstream_t[row(half), spans])
            toward_refs[half][...] = dot(value_grads[spans, pl.ds(start, 128)], upstream)
            return dot(prob_slot(index, half)[...], upstream.T)

        def scores(half):
            mass = inverse_totals[sentence * heads + pair * 2 + half, 0:1, :]
            prob = prob_slot(index, half)
            result = toward_refs[half]
            for piece in range(0, slots, 64):
                at = slice(piece, piece + 64)
                score_refs[half][at, :] = (
                    prob[at, :].astype(full) * (result[at, :] - mass)
                ).astype(low)

        def finish(half):
            score = score_refs[half][...]
            query = w_columns[row(half), spans]
            key = w_columns[row(half), key_spans]
            key_grad = dot(score, masked(half, query).T)
            w_columns[row(half), spans] = dot(key, score).astype(low)
            return key_grad

        value_grad = toward(0)
        value_grad = value_grad + toward(1)
        scores(0)
        key_grad = finish(0)
        scores(1)
        key_grad = key_grad + finish(1)
        key_grads[spans, pl.ds(start, 128)] = key_grad.astype(low)
        value_grads[spans, pl.ds(start, 128)] = value_grad.astype(low)
        for when in range(heads // 2):
            group = when // 2

            def after(when=when, group=group):
                tick(f"p{when}")
                if when % 2:
                    projection_grads(group)
                    tick(f"c{group}")

            pl.when(index == (when + 1) * sentences - 1)(after)
        return carry

    lax.fori_loop(0, steps, head_pair, 0)

    ones = jnp.ones((8, rows), low)
    vector_sums[6:7, :] = 0.125 * dot(ones, w_columns[:, 0:rows], 1, 1)[0:1, :]
    vector_sums[7:8, :] = dot(ones, value_grads[...])[0:1, :]

    def sum_copies(stage):
        core, x, y, z0, z1 = (links[name][1] for name in ("core", "x", "y", "z0", "z1"))
        moves = ((core,), (x, y, x + y), (z0, z1, z0 + z1))[stage]
        base = (0, 1, 4)[stage]
        return [
            sum_copy(stage, sum_held.at[stage], sum_recv.at[base + index], move)
            for index, move in enumerate(moves)
        ]

    def sum_copy(stage, source, goal, move):
        return pltpu.make_async_remote_copy(
            src_ref=source,
            dst_ref=goal,
            send_sem=sum_sems.at[stage, 0],
            recv_sem=sum_sems.at[stage, 1],
            device_id=(me + move,),
            device_id_type=pl.DeviceIdType.MESH,
        )

    def sum_step(stage):
        base, count = ((0, 1), (1, 3), (4, 3))[stage]
        arrived = sum_recv.at[pl.ds(base, count)]
        whole = sum_copy(stage, arrived, arrived, links["core"][1])
        whole.wait_send()
        whole.wait_recv()
        total = sum_held[stage]
        for index in range(count):
            total = total + sum_recv[base + index]
        if stage < 2:
            sum_held[stage + 1] = total
            for copy in sum_copies(stage + 1):
                copy.start()
        else:
            sums_out[...] = total

    for copy in sum_copies(0):
        copy.start()

    for copy in square_loads[1:]:
        copy.wait()

    def token_dot(start):
        spans = slice(start, start + span)
        total = 0.125 * dot(w_columns[:, spans], w_rows[width : 2 * width, :], 0, 1)
        total = total + dot(key_grads[spans, :], w_rows[2 * width : 3 * width, :], 1, 1)
        return total + dot(value_grads[spans, :], w_rows[3 * width : 4 * width, :], 1, 1)

    outs = []
    for index, start in enumerate(range(0, rows, span)):
        at = slice(start, start + span)
        grads[at, :] = grads[at, :] + token_dot(start)
        copy = load(grads.at[at], packed_out.at[at])
        outs.append(copy)
        tick(f"t{index}")
        sum_step(index)
    tick("end")
    sum_step(2)
    base = rows
    half = width // 2
    for source in (
        outer_out,
        inner_out.at[:, 0:width],
        inner_out.at[:, width : 2 * width],
        sums_out,
        loss_out,
    ):
        size = source.shape[0]
        outs.append(load(source, packed_out.at[pl.ds(base, size)]))
        base += size
    for place in range(4):
        size = square_out.shape[1]
        outs.append(
            load(
                square_out.at[place],
                packed_out.at[pl.ds(base + place // 2 * size, size), pl.ds(place % 2 * half, half)],
            )
        )
    for copy in outs:
        copy.wait()


def finish_kernel(
    devices,
    packed,
    loss_out,
    token_grad_out,
    query_out,
    query_bias,
    key_out,
    value_out,
    value_bias,
    output_out,
    output_bias,
    first_gain,
    first_shift,
    inner_out,
    inner_bias,
    outer_out,
    outer_bias,
    second_gain,
    second_shift,
    square_held,
    sums_held,
    sems,
):
    me = lax.axis_index("dp")
    rows, width = token_grad_out.shape
    own = query_out.shape[0]
    copies = []

    def move(source, target):
        copy = pltpu.make_async_copy(source, target, sems.at[len(copies)])
        copy.start()
        copies.append(copy)
        return copy

    outer_at = rows
    inner_at = outer_at + outer_out.shape[0]
    sums_at = inner_at + 4 * own
    square_at = sums_at + 24
    get_sums = move(packed.at[pl.ds(sums_at, 24)], sums_held)
    get_square = move(packed.at[pl.ds(square_at, 4 * own)], square_held)
    for start in range(0, rows, rows // 4):
        at = pl.ds(start, rows // 4)
        move(packed.at[at], token_grad_out.at[at])
    move(packed.at[pl.ds(outer_at, outer_out.shape[0])], outer_out)
    part = inner_out.shape[1] // 6
    for index in range(6):
        lane = index // 2 * part
        for piece in range(0, part, 256):
            first = lane + piece
            start = inner_at + first // width * 2 * own + index % 2 * own
            move(
                packed.at[pl.ds(start, own), pl.ds(first % width, 256)],
                inner_out.at[:, pl.ds(index * part + piece, 256)],
            )
    source = lax.broadcasted_iota(jnp.int32, (width, 128), 0)
    lane = lax.broadcasted_iota(jnp.int32, (width, 128), 1)

    def pick(values, start):
        chosen = jnp.where(source == lane + start, 1.0, 0.0)
        return lax.dot_general(
            values,
            chosen,
            (((1,), (0,)), ((), ())),
            precision=lax.Precision.HIGHEST,
            preferred_element_type=full,
        )

    get_sums.wait()
    picked = pick(sums_held[0:8, :], me * own)
    for place, ref in enumerate(
        (
            outer_bias,
            second_gain,
            second_shift,
            first_gain,
            first_shift,
            output_bias,
            query_bias,
            value_bias,
        )
    ):
        ref[...] = picked[place : place + 1, 0 : ref.shape[1]]
    wide = inner_bias.shape[1]
    per_row = width // wide
    row_ids = lax.broadcasted_iota(jnp.int32, (8, width), 0)
    chosen = jnp.sum(
        jnp.where(row_ids == lax.div(me, per_row), sums_held[8:16, :], 0.0),
        axis=0,
        keepdims=True,
    )
    inner_bias[...] = pick(jnp.broadcast_to(chosen, (8, width)), lax.rem(me, per_row) * wide)[
        0:1, 0:wide
    ]
    get_square.wait()
    half = width // 2

    def square(place, lower):
        start = place // 2 * 2 * own + lower * own
        return square_held[start : start + own, place % 2 * half : (place % 2 + 1) * half]

    def place_columns(target, column, place, index):
        lanes = slice(index * 128, (index + 1) * 128)
        for lower in range(2):
            at = column + lower * 128
            target[:, at : at + 128] = square(place, lower)[:, lanes]

    for index in range(3):
        place_columns(output_out, index * 256, 0, index)
        for place, target in enumerate((query_out, key_out, value_out)):
            place_columns(target, index * 256, 1 + index, place)
    loss_out[...] = sums_held[16:17, 0:1]
    for copy in copies[2:]:
        copy.wait()


def linked_device(
    devices,
    tokens,
    lengths,
    groups,
    query_weight,
    query_bias,
    key_weight,
    value_weight,
    value_bias,
    output_weight,
    output_bias,
    first_gain,
    first_shift,
    inner_weight,
    inner_bias,
    outer_weight,
    outer_bias,
    second_gain,
    second_shift,
):
    sentences = lengths.shape[0]
    rows, width = tokens.shape
    slots = rows // sentences
    inner = inner_weight.shape[1]
    vectors = (
        query_bias,
        value_bias,
        output_bias,
        first_gain,
        first_shift,
        outer_bias,
        second_gain,
        second_shift,
    )
    weights = (query_weight, key_weight, value_weight, output_weight, inner_weight, outer_weight)
    (
        layer_output,
        pooled,
        live_mean,
        queries_t,
        keys_t,
        values,
        mixture_t,
        tokens_t,
        probs,
        inverse_totals,
        first_normed,
        first_inverse,
        hidden_t,
        second_normed,
        second_inverse,
        activated_t,
        slopes,
    ) = forward(lengths, tokens, vectors, inner_bias[None], weights)
    hbm = pl.BlockSpec(memory_space=pl.ANY)
    vmem = pl.BlockSpec(memory_space=pltpu.VMEM)
    shape = jax.ShapeDtypeStruct
    piece_outer = (inner // devices, width)
    piece_inner = (2 * width // devices, inner // 2)
    piece_square = (2 * width // devices, width // 2)

    def levels(piece, lead=()):
        third = (piece[0] // 3, piece[1])
        shapes = [(2,) * 5 + piece, (2,) * 4 + piece]
        shapes += [(3,) + (2,) * k + third for k in (3, 2)] + [(3, 3) + third]
        return [pltpu.VMEM(lead + s, low) for s in shapes]

    sets = len(SETS)
    extra = piece_outer[0] + 2 * piece_inner[0] + 16 + 8 + 2 * piece_square[0]
    packed = pl.pallas_call(
        functools.partial(backward_kernel, devices, sentences),
        in_specs=[vmem] * 5 + [hbm] * 20,
        out_specs=hbm,
        out_shape=shape((rows + extra, width), full),
        scratch_shapes=[
            pltpu.VMEM((8, width), full),
            pltpu.VMEM(piece_outer, full),
            pltpu.VMEM(piece_inner, full),
            pltpu.VMEM((4,) + piece_square, full),
            pltpu.VMEM((16, width), full),
            pltpu.VMEM(activated_t.shape, low),
            pltpu.VMEM(slopes.shape, low),
            pltpu.VMEM((inner, width), low),
            pltpu.VMEM((width, inner), low),
            pltpu.VMEM((rows, width), full),
            pltpu.VMEM((rows, width), full),
            pltpu.VMEM((rows, width), low),
            pltpu.VMEM((width, rows), low),
            pltpu.VMEM((rows, 128), full),
            pltpu.VMEM(inverse_totals.shape, full),
            pltpu.VMEM((sentences, width), full),
            pltpu.VMEM((devices, sentences, width), full),
            pltpu.VMEM((devices * sentences, width), full),
        ]
        + levels(piece_outer)
        + levels(piece_inner)
        + levels(piece_square, (4,))[2:]
        + [
            pltpu.VMEM((3, 16, width), full),
            pltpu.VMEM((7, 16, width), full),
            pltpu.SemaphoreType.DMA((36,)),
            pltpu.SemaphoreType.DMA((4, 2)),
            pltpu.SemaphoreType.DMA((2,)),
            pltpu.SemaphoreType.DMA((sets, 4)),
            pltpu.SemaphoreType.DMA((sets, 4)),
            pltpu.SemaphoreType.DMA((3, 2)),
            pltpu.SemaphoreType.REGULAR,
        ],
        compiler_params=pltpu.CompilerParams(
            collective_id=0, has_side_effects=True, vmem_limit_bytes=63 * MIB
        ),
        name="decode",
    )(
        pooled,
        live_mean,
        first_gain,
        second_gain,
        groups,
        activated_t,
        slopes,
        second_normed,
        second_inverse,
        hidden_t,
        first_normed,
        first_inverse,
        mixture_t,
        queries_t,
        keys_t,
        values,
        tokens_t,
        probs,
        inverse_totals,
        *weights,
    )
    own = width // devices
    finals = pl.pallas_call(
        functools.partial(finish_kernel, devices),
        out_shape=[
            shape((1, 1), full),
            shape((rows, width), full),
            shape((own, width), full),
            shape((1, own), full),
            shape((own, width), full),
            shape((own, width), full),
            shape((1, own), full),
            shape((own, width), full),
            shape((1, own), full),
            shape((1, own), full),
            shape((1, own), full),
            shape((own, inner), full),
            shape((1, inner // devices), full),
            shape((inner // devices, width), full),
            shape((1, own), full),
            shape((1, own), full),
            shape((1, own), full),
        ],
        in_specs=[hbm],
        out_specs=[vmem, hbm] + [vmem] * 15,
        scratch_shapes=[
            pltpu.VMEM((2 * piece_square[0], width), full),
            pltpu.VMEM((24, width), full),
            pltpu.SemaphoreType.DMA((20,)),
        ],
        compiler_params=pltpu.CompilerParams(vmem_limit_bytes=32 * MIB),
        name="finish",
    )(packed)
    finals = [f.reshape(f.shape[1:]) if f.shape[0] == 1 else f for f in finals]
    return (finals[0].reshape(()), layer_output, *finals[1:])


highest = lax.Precision.HIGHEST


def project(operand, weight):
    return jnp.dot(operand, weight, preferred_element_type=jnp.float32)


def transpose_left(left_rows, right_rows):
    return lax.dot_general(
        left_rows, right_rows, (((0,), (0,)), ((), ())), preferred_element_type=jnp.float32
    )


def transpose_right(operand, weight):
    return lax.dot_general(
        operand, weight, (((1,), (1,)), ((), ())), preferred_element_type=jnp.float32
    )


def standardize(residual):
    center = residual - jnp.mean(residual, axis=-1, keepdims=True)
    inverse = lax.rsqrt(jnp.mean(center * center, axis=-1, keepdims=True) + layer_epsilon)
    return (center * inverse, inverse)


def standardize_back(upstream, normed, inverse, scaling):
    scaled = upstream * scaling
    return inverse * (
        scaled
        - jnp.mean(scaled, axis=-1, keepdims=True)
        - normed * jnp.mean(scaled * normed, axis=-1, keepdims=True)
    )


def gelu_slope(inner_pre):
    cumulative = 0.5 * (1.0 + lax.erf(inner_pre * (1.0 / math.sqrt(2.0))))
    density = jnp.exp(-0.5 * inner_pre * inner_pre) * (1.0 / math.sqrt(2.0 * math.pi))
    return cumulative + inner_pre * density


def masked_scores(queries, key_rows, key_live):
    scores = jnp.einsum("qhd,khd->hqk", queries, key_rows, preferred_element_type=jnp.float32)
    return jnp.where(key_live[None, None, :], scores, -1e30)


def attend(pieces):
    queries, key_rows, value_rows, key_live = pieces
    scores = masked_scores(queries, key_rows, key_live)
    summit = jnp.max(scores, axis=-1, keepdims=True)
    raised = jnp.exp(scores - summit)
    totals = jnp.sum(raised, axis=-1, keepdims=True)
    weights = (raised / totals).astype(jnp.bfloat16)
    mixture = jnp.einsum("hqk,khd->qhd", weights, value_rows, preferred_element_type=jnp.float32)
    return (mixture.astype(jnp.bfloat16), (summit + jnp.log(totals))[..., 0])


def attend_back(pieces):
    queries, key_rows, value_rows, key_live, log_total, upstream = pieces
    scores = masked_scores(queries, key_rows, key_live)
    chances = jnp.exp(scores - log_total[..., None])
    toward = jnp.einsum("qhd,khd->hqk", upstream, value_rows, preferred_element_type=jnp.float32)
    score_grad = (chances * (toward - jnp.sum(chances * toward, axis=-1, keepdims=True))).astype(
        jnp.bfloat16
    )
    value_grad = jnp.einsum(
        "hqk,qhd->khd", chances.astype(jnp.bfloat16), upstream, preferred_element_type=jnp.float32
    )
    query_grad = jnp.einsum(
        "hqk,khd->qhd", score_grad, key_rows, preferred_element_type=jnp.float32
    )
    key_grad = jnp.einsum("hqk,qhd->khd", score_grad, queries, preferred_element_type=jnp.float32)
    return (
        query_grad.astype(jnp.bfloat16),
        key_grad.astype(jnp.bfloat16),
        value_grad.astype(jnp.bfloat16),
    )


def contrast_rows(row_unit, unit_rows, row_groups, groups, row_start):
    similar = cosine_scale * lax.dot_general(
        row_unit, unit_rows, (((1,), (1,)), ((), ())), precision=highest
    )
    row_ids = row_start + jnp.arange(row_unit.shape[0])
    column_ids = jnp.arange(unit_rows.shape[0])
    itself = row_ids[:, None] == column_ids[None, :]
    logits = jnp.where(itself, -1e30, similar)
    summit = jnp.max(logits, axis=-1, keepdims=True)
    raised = jnp.exp(logits - summit)
    totals = jnp.sum(raised, axis=-1, keepdims=True)
    chances = raised / totals
    log_total = summit + jnp.log(totals)
    matched = jnp.logical_and(
        row_groups[:, None] == groups[None, :], jnp.logical_not(itself)
    ).astype(jnp.float32)
    weights = matched / jnp.maximum(jnp.sum(matched, axis=-1, keepdims=True), 1.0)
    row_mass = jnp.sum(weights, axis=-1, keepdims=True)
    loss_rows = row_mass[:, 0] * log_total[:, 0] - jnp.sum(weights * similar, axis=-1)
    return (jnp.sum(loss_rows), row_mass * chances - weights)


def per_device(
    tokens,
    lengths,
    groups,
    query_weight,
    query_bias,
    key_weight,
    value_weight,
    value_bias,
    output_weight,
    output_bias,
    first_gain,
    first_shift,
    inner_weight,
    inner_bias,
    outer_weight,
    outer_bias,
    second_gain,
    second_shift,
):
    seq_count = lengths.shape[0]
    slot_count = tokens.shape[0] // seq_count
    model_width = tokens.shape[1]
    heads_shape = (seq_count, slot_count, HEADS, HD)
    queries = ((project(tokens, query_weight) + query_bias) * 0.125).astype(jnp.bfloat16)
    key_rows = project(tokens, key_weight).astype(jnp.bfloat16)
    value_rows = (project(tokens, value_weight) + value_bias).astype(jnp.bfloat16)
    key_live = jnp.arange(slot_count)[None, :] < lengths[:, None]
    head_queries = queries.reshape(heads_shape)
    head_keys = key_rows.reshape(heads_shape)
    head_values = value_rows.reshape(heads_shape)
    mixture, log_total = lax.map(attend, (head_queries, head_keys, head_values, key_live))
    mixture = mixture.reshape(tokens.shape)
    first_normed, first_inverse = standardize(
        tokens.astype(jnp.float32) + project(mixture, output_weight) + output_bias
    )
    hidden = first_normed * first_gain + first_shift
    hidden_low = hidden.astype(jnp.bfloat16)
    inner_pre = project(hidden_low, inner_weight) + inner_bias
    activated = jax.nn.gelu(inner_pre, approximate=False).astype(jnp.bfloat16)
    second_normed, second_inverse = standardize(
        hidden + project(activated, outer_weight) + outer_bias
    )
    output = second_normed * second_gain + second_shift
    live_rows = key_live.astype(jnp.float32)[:, :, None]
    counts = lengths.astype(jnp.float32)[:, None]
    pooled = (
        jnp.sum(output.reshape(seq_count, slot_count, model_width) * live_rows, axis=1) / counts
    ).astype(jnp.bfloat16)
    everyone = lax.all_gather(pooled, "dp", axis=0, tiled=True).astype(jnp.float32)
    inverse_all = lax.rsqrt(jnp.sum(everyone * everyone, axis=-1, keepdims=True) + unit_epsilon)
    unit_rows = everyone * inverse_all
    first_row = lax.axis_index("dp") * seq_count
    own_unit = lax.dynamic_slice_in_dim(unit_rows, first_row, seq_count, 0)
    own_inverse = lax.dynamic_slice_in_dim(inverse_all, first_row, seq_count, 0)
    own_groups = lax.dynamic_slice_in_dim(groups, first_row, seq_count, 0)
    part_loss, coupling = contrast_rows(own_unit, unit_rows, own_groups, groups, first_row)
    loss_value = lax.psum(part_loss, "dp")
    spread = cosine_scale * lax.dot_general(
        coupling, own_unit, (((0,), (0,)), ((), ())), precision=highest
    )
    unit_grad = cosine_scale * jnp.dot(coupling, unit_rows, precision=highest) + lax.psum_scatter(
        spread, "dp", scatter_dimension=0, tiled=True
    )
    pooled_grad = own_inverse * (
        unit_grad - own_unit * jnp.sum(own_unit * unit_grad, axis=-1, keepdims=True)
    )
    grad_output = (pooled_grad[:, None, :] / counts[:, :, None] * live_rows).reshape(tokens.shape)
    second_gain_grad = jnp.sum(grad_output * second_normed, axis=0)
    second_shift_grad = jnp.sum(grad_output, axis=0)
    grad_second = standardize_back(grad_output, second_normed, second_inverse, second_gain)
    branch_grad = grad_second.astype(jnp.bfloat16)
    outer_bias_grad = jnp.sum(branch_grad, axis=0, dtype=jnp.float32)
    outer_weight_grad = transpose_left(activated, branch_grad)
    inner_grad = (transpose_right(branch_grad, outer_weight) * gelu_slope(inner_pre)).astype(
        jnp.bfloat16
    )
    inner_bias_grad = jnp.sum(inner_grad, axis=0, dtype=jnp.float32)
    inner_weight_grad = transpose_left(hidden_low, inner_grad)
    hidden_grad = grad_second + transpose_right(inner_grad, inner_weight)
    first_gain_grad = jnp.sum(hidden_grad * first_normed, axis=0)
    first_shift_grad = jnp.sum(hidden_grad, axis=0)
    grad_first = standardize_back(hidden_grad, first_normed, first_inverse, first_gain)
    attended_grad = grad_first.astype(jnp.bfloat16)
    output_bias_grad = jnp.sum(attended_grad, axis=0, dtype=jnp.float32)
    output_weight_grad = transpose_left(mixture, attended_grad)
    mixture_grad = transpose_right(attended_grad, output_weight).astype(jnp.bfloat16)
    query_grad, key_grad, value_grad = lax.map(
        attend_back,
        (
            head_queries,
            head_keys,
            head_values,
            key_live,
            log_total,
            mixture_grad.reshape(heads_shape),
        ),
    )
    query_grad = query_grad.reshape(tokens.shape)
    key_grad = key_grad.reshape(tokens.shape)
    value_grad = value_grad.reshape(tokens.shape)
    query_weight_grad = 0.125 * transpose_left(tokens, query_grad)
    query_bias_grad = 0.125 * jnp.sum(query_grad, axis=0, dtype=jnp.float32)
    key_weight_grad = transpose_left(tokens, key_grad)
    value_weight_grad = transpose_left(tokens, value_grad)
    value_bias_grad = jnp.sum(value_grad, axis=0, dtype=jnp.float32)
    token_grad = (
        grad_first
        + 0.125 * transpose_right(query_grad, query_weight)
        + transpose_right(key_grad, key_weight)
        + transpose_right(value_grad, value_weight)
    )
    summed = tuple(
        (
            lax.psum_scatter(query_weight_grad, "dp", scatter_dimension=0, tiled=True),
            lax.psum_scatter(query_bias_grad, "dp", scatter_dimension=0, tiled=True),
            lax.psum_scatter(key_weight_grad, "dp", scatter_dimension=0, tiled=True),
            lax.psum_scatter(value_weight_grad, "dp", scatter_dimension=0, tiled=True),
            lax.psum_scatter(value_bias_grad, "dp", scatter_dimension=0, tiled=True),
            lax.psum_scatter(output_weight_grad, "dp", scatter_dimension=0, tiled=True),
            lax.psum_scatter(output_bias_grad, "dp", scatter_dimension=0, tiled=True),
            lax.psum_scatter(first_gain_grad, "dp", scatter_dimension=0, tiled=True),
            lax.psum_scatter(first_shift_grad, "dp", scatter_dimension=0, tiled=True),
            lax.psum_scatter(inner_weight_grad, "dp", scatter_dimension=0, tiled=True),
            lax.psum_scatter(inner_bias_grad, "dp", scatter_dimension=0, tiled=True),
            lax.psum_scatter(outer_weight_grad, "dp", scatter_dimension=0, tiled=True),
            lax.psum_scatter(outer_bias_grad, "dp", scatter_dimension=0, tiled=True),
            lax.psum_scatter(second_gain_grad, "dp", scatter_dimension=0, tiled=True),
            lax.psum_scatter(second_shift_grad, "dp", scatter_dimension=0, tiled=True),
        )
    )
    return (loss_value, output.astype(jnp.bfloat16), token_grad) + summed


def solution(mesh):
    placed = (
        P("dp", None),
        P("dp"),
        P(),
        P(),
        P(),
        P(),
        P(),
        P(),
        P(),
        P(),
        P(),
        P(),
        P(),
        P(),
        P(),
        P(),
        P(),
        P(),
    )
    devices = mesh.shape["dp"]
    body = functools.partial(linked_device, devices) if devices == 32 else per_device
    return jax.shard_map(
        body,
        mesh=mesh,
        in_specs=placed,
        out_specs=(
            P(),
            P("dp", None),
            P("dp", None),
            P("dp", None),
            P("dp"),
            P("dp", None),
            P("dp", None),
            P("dp"),
            P("dp", None),
            P("dp"),
            P("dp"),
            P("dp"),
            P("dp", None),
            P("dp"),
            P("dp", None),
            P("dp"),
            P("dp"),
            P("dp"),
        ),
        check_vma=False,
    )
```

```python
import functools
import math

import jax
import jax.numpy as jnp
from jax import lax
from jax.experimental import pallas as pl
from jax.experimental.pallas import tpu as pltpu
from jax.sharding import PartitionSpec as P

HEADS = 12
HD = 64
cosine_scale = 20.0
layer_epsilon = 1e-06
unit_epsilon = 1e-06
low = jnp.bfloat16
full = jnp.float32
MIB = 1 << 20


def dot(left, right, left_axis=1, right_axis=0):
    return lax.dot_general(
        left, right, (((left_axis,), (right_axis,)), ((), ())), preferred_element_type=full
    )


def gelu_pair(value):
    size = jnp.abs(value)
    ratio = pl.reciprocal(1.0 + (0.3275911 / math.sqrt(2.0)) * size, approx=True)
    bell = jnp.exp(value * value * -0.5)
    series = 0.5 * 1.061405429
    for factor in (-1.453152027, 1.421413741, -0.284496736, 0.254829592):
        series = series * ratio + 0.5 * factor
    half_tail = series * ratio * bell
    cumulative = jnp.where(value >= 0.0, 1.0 - half_tail, half_tail)
    return value * cumulative, cumulative + value * bell * (1.0 / math.sqrt(2.0 * math.pi))


def widen(column, lanes):
    return jnp.concatenate([column] * (lanes // 128), axis=1)


def standardized(residual):
    center = residual - jnp.mean(residual, axis=1, keepdims=True)
    inverse = lax.rsqrt(jnp.mean(center * center, axis=1, keepdims=True) + layer_epsilon)
    return center * inverse, inverse


def forward_kernel(
    sentences,
    lengths,
    query_bias,
    value_bias,
    output_bias,
    first_gain,
    first_shift,
    inner_bias,
    outer_bias,
    second_gain,
    second_shift,
    tokens_in,
    query_weight,
    key_weight,
    value_weight,
    output_weight,
    inner_weight,
    outer_weight,
    layer_output_out,
    pooled,
    live_mean,
    queries_t_out,
    keys_t_out,
    values_out,
    mixture_t_out,
    tokens_t_out,
    probs_out,
    inverse_totals_out,
    first_normed_out,
    first_inverse_out,
    hidden_t_out,
    second_normed_out,
    second_inverse_out,
    activated_t_out,
    slopes_out,
    tokens,
    w_query,
    w_key,
    w_value,
    w_output,
    w_inner,
    w_outer,
    layer_output,
    queries_t,
    keys_t,
    values,
    mixture_t,
    tokens_t,
    inverse_totals,
    first_normed,
    first_inverse,
    hidden_low,
    hidden_t,
    second_normed,
    second_inverse,
    activated,
    activated_t,
    slopes,
    mask_block,
    in_sems,
    out_sems,
    prob_sems,
    feed_sems,
):
    rows, width = tokens.shape
    slots = rows // sentences
    inner = w_inner.shape[1]
    wide = slopes.shape[2]
    loads = [
        pltpu.make_async_copy(source, target, in_sems.at[place])
        for place, (source, target) in enumerate(
            (
                (tokens_in, tokens),
                (query_weight, w_query),
                (key_weight, w_key),
                (value_weight, w_value),
                (output_weight, w_output),
                (inner_weight, w_inner),
                (outer_weight, w_outer),
            )
        )
    ]
    for copy in loads:
        copy.start()
    stores = []

    def store(source, target):
        copy = pltpu.make_async_copy(source, target, out_sems.at[len(stores)])
        copy.start()
        stores.append(copy)

    def line(ref):
        return ref[...].reshape(1, ref.shape[0])

    key_rows = activated.at[:, 0:width]
    values_t = activated.at[0:width, width : width + rows]

    def prob_slot(pair, unit):
        start = pl.multiple_of((lax.rem(pair, 3) * 2 + unit // 2) * slots, slots)
        lane = unit % 2 * slots
        return activated_t.at[pl.ds(start, slots), lane : lane + slots]

    slot_ids = lax.broadcasted_iota(jnp.int32, (slots, 128), 0)
    lane_ids = lax.broadcasted_iota(jnp.int32, (slots, 128), 1)
    for sentence in range(sentences):
        mask_block[sentence] = jnp.where(
            jnp.logical_and(slot_ids >= lengths[sentence], lane_ids == 0), -1e30, 0.0
        ).astype(low)

    for copy in loads[:4]:
        copy.wait()
    span = 512
    pieces = [slice(start, start + span) for start in range(0, rows, span)]
    bias = line(query_bias)
    for at in pieces:
        queries_t[:, at] = ((dot(tokens[at, :], w_query[...]) + bias) * 0.125).astype(low).T
    for at in pieces:
        result = dot(tokens[at, :], w_key[...]).astype(low)
        key_rows[at, :] = result
        keys_t[:, at] = result.T
    bias = line(value_bias)
    for at in pieces:
        result = (dot(tokens[at, :], w_value[...]) + bias).astype(low)
        values[at, :] = result
        values_t[:, at] = result.T
    for at in pieces:
        tokens_t[:, at] = tokens[at, :].T
    store(queries_t, queries_t_out)
    store(keys_t, keys_t_out)
    store(values, values_out)
    store(tokens_t, tokens_t_out)

    pick_row = jnp.where(
        lax.broadcasted_iota(jnp.int32, (128, slots), 0) == 0, 1.0, 0.0
    ).astype(low)
    empty = jnp.zeros((HD, slots), low)

    units = [(sentence, half) for sentence in range(sentences) for half in range(2)]

    def prob_copies(pair):
        return [
            pltpu.make_async_copy(
                prob_slot(pair, unit),
                probs_out.at[sentence * HEADS + pair * 2 + half],
                prob_sems.at[lax.rem(pair, 3), unit],
            )
            for unit, (sentence, half) in enumerate(units)
        ]

    def head_pair(exact, pair, carry):
        start = pl.multiple_of(pair * 128, 128)

        @pl.when(pair >= 3)
        def _():
            for copy in prob_copies(pair):
                copy.wait()

        def spans(unit):
            sentence = units[unit][0]
            return slice(sentence * slots, (sentence + 1) * slots)

        def get_scores(unit):
            sentence, half = units[unit]
            left = jnp.concatenate(
                [key_rows[spans(unit), pl.ds(start, 128)], mask_block[sentence]], axis=1
            )
            own = queries_t[pl.ds(pl.multiple_of(start + half * HD, HD), HD), spans(unit)]
            parts = [own, empty] if half == 0 else [empty, own]
            return dot(left, jnp.concatenate(parts + [pick_row], axis=0))

        def get_probs(unit, scores):
            sentence, half = units[unit]
            if exact:
                summit = jnp.max(scores, axis=0, keepdims=True)
            totals = jnp.zeros((8, slots), full)
            slot = prob_slot(pair, unit)
            step = 64
            parts = []
            for place in range(0, slots, step):
                piece = scores[place : place + step, :]
                piece = jnp.exp(piece - summit if exact else piece)
                totals = totals + jnp.sum(piece.reshape(step // 8, 8, slots), axis=0)
                piece = piece.astype(low)
                slot[place : place + step, :] = piece
                parts.append(piece)
            inverse = 1.0 / jnp.sum(totals, axis=0, keepdims=True)
            inverse_totals[sentence * HEADS + pair * 2 + half] = inverse
            return jnp.concatenate(parts, axis=0), inverse

        def mix(unit, raised, inverse):
            row = pl.multiple_of(start + units[unit][1] * HD, HD)
            mixed = dot(values_t[pl.ds(row, HD), spans(unit)], raised) * inverse
            mixture_t[pl.ds(row, HD), spans(unit)] = mixed.astype(low)

        count = len(units)
        scored, raised = {}, {}
        for turn in range(count + 2):
            if turn < count:
                scored[turn] = get_scores(turn)
            if 0 <= turn - 1 < count:
                raised[turn - 1] = get_probs(turn - 1, scored.pop(turn - 1))
            if turn >= 2:
                mix(turn - 2, *raised.pop(turn - 2))
        for copy in prob_copies(pair):
            copy.start()
        return carry

    head_ids = lax.broadcasted_iota(jnp.int32, (16, width), 0)
    column_ids = lax.broadcasted_iota(jnp.int32, (16, width), 1)
    selector = jnp.where(head_ids == lax.div(column_ids, HD), 1.0, 0.0).astype(low)

    def largest(ref):
        return jnp.max(dot(selector, ref[...] * ref[...]), axis=1, keepdims=True)

    bound = jnp.max(largest(queries_t) * largest(keys_t))

    @pl.when(bound < 1600.0)
    def _():
        lax.fori_loop(0, HEADS // 2, functools.partial(head_pair, False), 0)

    @pl.when(jnp.logical_not(bound < 1600.0))
    def _():
        lax.fori_loop(0, HEADS // 2, functools.partial(head_pair, True), 0)

    store(mixture_t, mixture_t_out)
    store(inverse_totals, inverse_totals_out)

    loads[4].wait()
    bias, gain, shift = line(output_bias), line(first_gain), line(first_shift)
    span, step = 256, 32
    for start in range(0, rows, span):
        attended = dot(mixture_t[:, start : start + span], w_output[...], 0, 0)
        for place in range(0, span, step):
            at = slice(start + place, start + place + step)
            normed, inverse = standardized(
                tokens[at, :].astype(full) + attended[place : place + step] + bias
            )
            first_normed[at, :] = normed
            first_inverse[at, :] = jnp.broadcast_to(inverse, (step, 128))
            hidden_low[at, :] = (normed * gain + shift).astype(low)
        at = slice(start, start + span)
        hidden_t[:, at] = hidden_low[at, :].T
    store(first_normed, first_normed_out)
    store(first_inverse, first_inverse_out)
    store(hidden_t, hidden_t_out)

    loads[5].wait()
    for pair in range(HEADS // 2 - 3, HEADS // 2):
        for copy in prob_copies(pair):
            copy.wait()

    def feed_copies(index):
        start = pl.multiple_of(index * wide, wide)
        return (
            pltpu.make_async_copy(
                activated_t.at[pl.ds(start, wide)],
                activated_t_out.at[pl.ds(start, wide)],
                feed_sems.at[index, 0],
            ),
            pltpu.make_async_copy(
                slopes.at[index], slopes_out.at[index], feed_sems.at[index, 1]
            ),
        )

    def feed(index, carry):
        start = pl.multiple_of(index * wide, wide)
        weight = w_inner[:, pl.ds(start, wide)]
        offset = inner_bias[:, pl.ds(start, wide)]
        block, step = 128, 16

        def gelu_block(place, pre):
            at = slice(place, place + block)
            parts = []
            for piece in range(0, block, step):
                value, slope = gelu_pair(pre[piece : piece + step] + offset)
                slopes[index, place + piece : place + piece + step, :] = slope.astype(low)
                parts.append(value.astype(low))
            value = jnp.concatenate(parts, axis=0)
            activated[at, pl.ds(start, wide)] = value
            activated_t[pl.ds(start, wide), at] = value.T

        before = None
        for place in range(0, rows, block):
            pre = dot(hidden_low[place : place + block, :], weight)
            if before is not None:
                gelu_block(place - block, before)
            before = pre
        gelu_block(rows - block, before)
        for copy in feed_copies(index):
            copy.start()
        return carry

    lax.fori_loop(0, inner // wide, feed, 0)

    loads[6].wait()
    bias, gain_2, shift_2 = line(outer_bias), line(second_gain), line(second_shift)
    live_sums = [jnp.zeros((8, width), full) for _ in range(sentences)]
    for start in range(0, rows, span):
        branch = dot(activated[start : start + span, :], w_outer[...])
        sentence = start // slots
        length = lengths[sentence]
        for place in range(0, span, step):
            at = slice(start + place, start + place + step)
            hidden = first_normed[at, :] * gain + shift
            normed, inverse = standardized(hidden + branch[place : place + step] + bias)
            second_normed[at, :] = normed
            layer_output[at, :] = (normed * gain_2 + shift_2).astype(low)
            slot_row = lax.broadcasted_iota(jnp.int32, (step, 128), 0) + (
                start + place - sentence * slots
            )
            live = jnp.where(slot_row < length, 1.0, 0.0)
            live_sums[sentence] = live_sums[sentence] + jnp.sum(
                (normed * widen(live, width)).reshape(step // 8, 8, width), axis=0
            )
            second_inverse[at, :] = inverse * live * (1.0 / length.astype(full))
        at = slice(start, start + span)
        store(second_normed.at[at], second_normed_out.at[at])
        store(layer_output.at[at], layer_output_out.at[at])
        store(second_inverse.at[at], second_inverse_out.at[at])
    for sentence in range(sentences):
        mean_normed = jnp.sum(live_sums[sentence], axis=0, keepdims=True) / lengths[
            sentence
        ].astype(full)
        live_mean[sentence] = jnp.broadcast_to(mean_normed, (8, width))
        vector = (mean_normed * gain_2 + shift_2).astype(low).astype(full)
        pooled[sentence] = jnp.broadcast_to(vector, (8, width))
    for index in range(inner // wide):
        for copy in feed_copies(index):
            copy.wait()
    for copy in stores:
        copy.wait()


def forward(lengths, tokens, vectors, inner_bias, weights):
    sentences = lengths.shape[0]
    rows, width = tokens.shape
    slots = rows // sentences
    inner = weights[4].shape[1]
    wide = 1024
    hbm = pl.BlockSpec(memory_space=pl.ANY)
    vmem = pl.BlockSpec(memory_space=pltpu.VMEM)
    shape = jax.ShapeDtypeStruct
    kept = [
        ((rows, width), low),
        ((width, rows), low),
        ((width, rows), low),
        ((rows, width), low),
        ((width, rows), low),
        ((width, rows), low),
        ((sentences * HEADS, 1, slots), full),
        ((rows, width), full),
        ((rows, 128), full),
        ((rows, width), low),
        ((width, rows), low),
        ((rows, width), full),
        ((rows, 128), full),
        ((rows, inner), low),
        ((inner, rows), low),
        ((inner // wide, rows, wide), low),
    ]
    outs = [shape(*k) for k in kept]
    per_sentence = shape((sentences, 8, width), full)
    probs = shape((sentences * HEADS, slots, slots), low)
    return pl.pallas_call(
        functools.partial(forward_kernel, sentences),
        in_specs=[pl.BlockSpec(memory_space=pltpu.SMEM)] + [vmem] * 9 + [hbm] * 7,
        out_specs=[hbm, vmem, vmem] + [hbm] * 14,
        out_shape=[outs[0], per_sentence, per_sentence]
        + outs[1:6]
        + [probs]
        + outs[6:9]
        + outs[10:13]
        + outs[14:],
        scratch_shapes=[pltpu.VMEM((rows, width), low)]
        + [pltpu.VMEM(w.shape, low) for w in weights]
        + [pltpu.VMEM(*k) for k in kept]
        + [
            pltpu.VMEM((sentences, slots, 128), low),
            pltpu.SemaphoreType.DMA((7,)),
            pltpu.SemaphoreType.DMA((32,)),
            pltpu.SemaphoreType.DMA((3, 2 * sentences)),
            pltpu.SemaphoreType.DMA((inner // wide, 2)),
        ],
        compiler_params=pltpu.CompilerParams(vmem_limit_bytes=63 * MIB),
        name="encode",
    )(lengths, *vectors[:5], inner_bias, *vectors[5:], tokens, *weights)


SETS = ("A0", "A1", "A2", "B0", "B1", "B2", "C0", "C1", "C2", "C3")

SCHEDULE = {
    "g0": (("A1", 0),),
    "w0": (("A0", 0), ("A2", 0),),
    "w1": (("B0", 0),),
    "e2": (("A1", 1),),
    "w2": (("A0", 1), ("B1", 0),),
    "h0": (("B2", 0), ("A2", 1),),
    "h1": (("A0", 2), ("A1", 2), ("B0", 1),),
    "m": (("B1", 1), ("C0", 0), ("B2", 1),),
    "s0": (("A2", 2), ("A0", 3),),
    "s2": (("B0", 2),),
    "c0": (("B1", 2), ("A1", 3),),
    "s5": (("B2", 2),),
    "s6": (("C0", 1), ("A2", 3), ("C1", 0),),
    "c1": (("B0", 3),),
    "s8": (("C0", 2),),
    "s9": (("C2", 0), ("C1", 1), ("B1", 3),),
    "c2": (("C2", 1),),
    "t0": (("B2", 3), ("C3", 0), ("C1", 2),),
    "t2": (("C2", 2),),
    "t3": (("C0", 3), ("C3", 1),),
    "t5": (("C1", 3),),
    "end": (("C3", 2), ("C2", 3), ("C3", 3),),
}


class Summation:
    def __init__(self, name, send, held, out, sems, me, links):
        self.send, self.held, self.out = send, held, out
        self.place = SETS.index(name)
        self.odd = self.place % 2
        self.send_sems, self.recv_sems = sems
        self.me, self.links = me, links
        self.third = held[0].shape[-2] // 3

    def side(self, link, away):
        bit = self.links[link][0]
        return 1 - bit if away else bit

    def halves(self, stage, away):
        h = self.third

        def side(link):
            return self.side(link, away)

        if stage == 0:
            return [(self.send.at[:, :, :, :, side("core")], "core")]
        r = self.held[stage - 1]
        if stage == 1:
            return [
                (r.at[:, :, :, side("x"), pl.ds(0, h)], "x"),
                (r.at[:, :, side("y"), :, pl.ds(h, h)], "y"),
                (r.at[:, side("z0"), :, :, pl.ds(2 * h, h)], "z0"),
            ]
        last = (r.at[2, :, side("y")], "y") if self.odd else (r.at[2, :, :, side("x")], "x")
        return [(r.at[0, :, :, side("y")], "y"), (r.at[1, :, :, side("x")], "x"), last]

    def quarter(self, parts, far, near):
        link = "z0" if parts == 0 else "x" if self.odd else "y"
        at = pl.ds(0, 2) if parts == 0 else pl.ds(2, 1)
        source = self.held[2].at[at, self.side("z1", far), self.side(link, near)]
        return at, source, self.me + far * self.links["z1"][1] + near * self.links[link][1]

    def copies(self, stage):
        moves = []
        if stage < 3:
            target = self.held[stage]
            for part, (source, link) in enumerate(self.halves(stage, 1)):
                goal = target if stage == 0 else target.at[part]
                moves.append((source, goal, self.me + self.links[link][1]))
        else:
            for parts in range(2):
                for slot, (far, near) in enumerate(((0, 1), (1, 0), (1, 1))):
                    at, source, device = self.quarter(parts, far, near)
                    moves.append((source, self.held[3].at[at, slot], device))
        return [self.copy(stage, *move) for move in moves]

    def copy(self, stage, source, goal, device):
        return pltpu.make_async_remote_copy(
            src_ref=source,
            dst_ref=goal,
            send_sem=self.send_sems.at[self.place, stage],
            recv_sem=self.recv_sems.at[self.place, stage],
            device_id=(device,),
            device_id_type=pl.DeviceIdType.MESH,
        )

    def start(self, stage=0):
        for copy in self.copies(stage):
            copy.start()

    def step(self, stage):
        held = self.held[stage]
        whole = self.copy(stage, held, held, self.me + self.links["core"][1])
        whole.wait_send()
        whole.wait_recv()
        if stage < 3:
            for part, (kept, _) in enumerate(self.halves(stage, 0)):
                if stage == 0:
                    held[...] = held[...] + kept[...]
                else:
                    held[part] = held[part] + kept[...]
            self.start(stage + 1)
        else:
            h = self.third
            for part in range(3):
                total = self.quarter(part // 2, 0, 0)[1][part % 2].astype(full)
                for slot in range(3):
                    total = total + self.held[3][part, slot].astype(full)
                self.out[part * h : part * h + h, :] = total


def contrast(points, groups):
    count = points.shape[0]
    inverse = lax.rsqrt(jnp.sum(points * points, axis=1, keepdims=True) + unit_epsilon)
    unit = points * inverse
    similar = cosine_scale * lax.dot_general(
        unit,
        unit,
        (((1,), (1,)), ((), ())),
        precision=lax.Precision.HIGHEST,
        preferred_element_type=full,
    )
    rows = lax.broadcasted_iota(jnp.int32, (count, count), 0)
    columns = lax.broadcasted_iota(jnp.int32, (count, count), 1)
    itself = rows == columns
    logits = jnp.where(itself, -1e30, similar)
    summit = jnp.max(logits, axis=1, keepdims=True)
    raised = jnp.exp(logits - summit)
    totals = jnp.sum(raised, axis=1, keepdims=True)
    chances = raised / totals
    log_total = summit + jnp.log(totals)
    across = jnp.broadcast_to(groups, (count, count))
    matched = jnp.where(
        jnp.logical_and(across == across.T, jnp.logical_not(itself)), 1.0, 0.0
    )
    weights = matched / jnp.maximum(jnp.sum(matched, axis=1, keepdims=True), 1.0)
    row_mass = jnp.sum(weights, axis=1, keepdims=True)
    loss_rows = row_mass * log_total - jnp.sum(weights * similar, axis=1, keepdims=True)
    loss = jnp.sum(loss_rows, axis=0, keepdims=True)
    coupling = row_mass * chances - weights
    unit_grad = cosine_scale * lax.dot_general(
        coupling + coupling.T,
        unit,
        (((1,), (0,)), ((), ())),
        precision=lax.Precision.HIGHEST,
        preferred_element_type=full,
    )
    grad = inverse * (unit_grad - unit * jnp.sum(unit * unit_grad, axis=1, keepdims=True))
    return loss, grad


def backward_kernel(
    devices,
    sentences,
    pooled,
    live_mean,
    first_gain,
    second_gain,
    groups,
    activated_t_in,
    slopes_in,
    second_normed_in,
    second_inverse_in,
    hidden_t_in,
    first_normed_in,
    first_inverse_in,
    mixture_t_in,
    queries_t_in,
    keys_t_in,
    values_in,
    tokens_t_in,
    probs_in,
    inverse_totals_in,
    query_weight,
    key_weight,
    value_weight,
    output_weight,
    inner_weight,
    outer_weight,
    packed_out,
    loss_out,
    outer_out,
    inner_out,
    square_out,
    sums_out,
    act_t,
    inner_grad,
    w_rows,
    w_columns,
    normed,
    grads,
    branch,
    hidden_t,
    inverses,
    inverse_totals,
    own,
    gathered,
    outer_send,
    outer_0,
    outer_1,
    outer_2,
    outer_3,
    inner_send,
    inner_0,
    inner_1,
    inner_2,
    inner_3,
    square_1,
    square_2,
    square_3,
    sum_held,
    sum_recv,
    late_held,
    late_recv,
    load_sems,
    prob_sems,
    gather_sems,
    set_send,
    set_recv,
    sum_sems,
    credit,
):
    me = lax.axis_index("dp")
    rows, width = normed.shape
    slots = rows // sentences
    parts, _, wide = inner_grad.shape
    heads = width // HD
    own_rows = width // devices

    def link(mask):
        bit = lax.rem(lax.div(me, mask), 2)
        return bit, mask * (1 - 2 * bit)

    links = {"core": link(1), "x": link(2), "y": link(4), "z0": link(8), "z1": link(16)}
    load_count = iter(range(44))

    def load(source, target):
        copy = pltpu.make_async_copy(source, target, load_sems.at[next(load_count)])
        copy.start()
        return copy

    get_normed = load(second_normed_in, normed)
    get_second = load(second_inverse_in, inverses)
    get_act = load(activated_t_in, act_t)
    get_outer = load(outer_weight, w_rows)
    get_slopes = [load(slopes_in.at[part], inner_grad.at[part]) for part in range(parts)]
    get_hidden = load(hidden_t_in, hidden_t)
    get_inner = load(inner_weight, w_columns)
    get_totals = load(inverse_totals_in, inverse_totals)

    barrier = pltpu.get_barrier_semaphore()

    def greet(step, carry):
        other = lax.rem(me + step, devices)
        pl.semaphore_signal(
            barrier, inc=1, device_id=(other,), device_id_type=pl.DeviceIdType.MESH
        )
        return carry

    lax.fori_loop(1, devices, greet, 0)
    blocks = width // 128
    cut = [
        pooled[sentence, 0:1, block * 128 : (block + 1) * 128]
        for block in range(blocks)
        for sentence in range(sentences)
    ]
    cut.append(jnp.zeros((own.shape[0] - len(cut), 128), full))
    own[...] = jnp.concatenate(cut, axis=0).astype(low)
    gathered[me] = own[...]
    pl.semaphore_wait(barrier, devices - 1)

    def gather_copy(step):
        return pltpu.make_async_remote_copy(
            src_ref=own,
            dst_ref=gathered.at[me],
            send_sem=gather_sems.at[0],
            recv_sem=gather_sems.at[1],
            device_id=(lax.rem(me + step, devices),),
            device_id_type=pl.DeviceIdType.MESH,
        )

    def gather_start(step, carry):
        gather_copy(step).start()
        return carry

    lax.fori_loop(1, devices, gather_start, 0)
    others = gathered.at[pl.ds(0, devices - 1)]
    whole = pltpu.make_async_remote_copy(
        src_ref=others,
        dst_ref=others,
        send_sem=gather_sems.at[0],
        recv_sem=gather_sems.at[1],
        device_id=(lax.rem(me + 1, devices),),
        device_id_type=pl.DeviceIdType.MESH,
    )
    whole.wait_send()
    whole.wait_recv()
    everyone = gathered[...].reshape(devices * own.shape[0], 128)
    shape = (devices * sentences, devices * own.shape[0])
    row_ids = lax.broadcasted_iota(jnp.int32, shape, 0)
    source = lax.div(row_ids, sentences) * own.shape[0] + lax.rem(row_ids, sentences)
    column_ids = lax.broadcasted_iota(jnp.int32, shape, 1)
    points = jnp.concatenate(
        [
            dot(
                jnp.where(column_ids == source + block * sentences, 1.0, 0.0).astype(low), everyone
            )
            for block in range(blocks)
        ],
        axis=1,
    )
    loss, pooled_grad = contrast(
        points, groups[...].astype(full).reshape(1, groups.shape[0])
    )
    loss_out[...] = jnp.broadcast_to(loss, loss_out.shape)
    row_ids = lax.broadcasted_iota(jnp.int32, (devices * sentences, width), 0)
    own_grads = [
        jnp.sum(
            jnp.where(row_ids == me * sentences + sentence, pooled_grad, 0.0),
            axis=0,
            keepdims=True,
        )
        for sentence in range(sentences)
    ]
    vector_sums = sum_held.at[0]
    vector_sums[...] = jnp.zeros_like(vector_sums)
    vector_sums[1:2, :] = sum(
        own_grads[sentence] * live_mean[sentence, 0:1, :] for sentence in range(sentences)
    )
    vector_sums[2:3, :] = sum(own_grads)

    sets = {}

    def add_set(name, send, held, out):
        sets[name] = Summation(name, send, held, out, (set_send, set_recv), me, links)

    def columns(ref, start, size):
        return ref.at[(slice(None),) * (len(ref.shape) - 1) + (pl.ds(start, size),)]

    third = width // 3
    for part in range(3):
        lanes = (part * third, third)
        add_set(
            f"A{part}",
            columns(outer_send, *lanes),
            [columns(r, *lanes) for r in (outer_0, outer_1, outer_2, outer_3)],
            columns(outer_out, *lanes),
        )
        half = wide // 2
        lanes = (part * half, half)
        add_set(
            f"B{part}",
            columns(inner_send, *lanes),
            [columns(r, *lanes) for r in (inner_0, inner_1, inner_2, inner_3)],
            columns(inner_out, *lanes),
        )
    piece_rows, piece_columns = outer_send.shape[-2] // 2, width // 2
    square_sends = [
        outer_send.at[
            :,
            :,
            :,
            :,
            :,
            pl.ds(place % 2 * piece_rows, piece_rows),
            pl.ds(place // 2 * piece_columns, piece_columns),
        ]
        for place in range(4)
    ]
    for place in range(4):
        first = outer_0.at[
            :,
            :,
            :,
            :,
            pl.ds(place % 2 * piece_rows, piece_rows),
            pl.ds(place // 2 * piece_columns, piece_columns),
        ]
        add_set(
            f"C{place}",
            square_sends[place],
            [first] + [r.at[place] for r in (square_1, square_2, square_3)],
            square_out.at[place],
        )
    second_done, done = [], []

    def step_set(name, stage):
        sets[name].step(stage)
        if stage == 3:
            done.append(name)
        if name[0] == "A" and stage == 1:
            second_done.append(name)
            if len(second_done) == 3:
                pl.semaphore_signal(
                    credit,
                    inc=1,
                    device_id=(me + links["core"][1],),
                    device_id_type=pl.DeviceIdType.MESH,
                )

    def tick(point):
        for name, stage in SCHEDULE.get(point, ()):
            step_set(name, stage)

    def piece_at(device):
        return device // 16, device // 8 % 2, device // 4 % 2, device // 2 % 2, device % 2

    get_normed.wait()
    get_second.wait()
    bias_sum = jnp.zeros((8, width), full)
    step = 32
    for sentence in range(sentences):
        scaled = own_grads[sentence] * second_gain[...].reshape(1, width)
        shifted = scaled - jnp.mean(scaled, axis=1, keepdims=True)

        def second_back(index, total):
            at = pl.ds(pl.multiple_of(sentence * slots + index * step, step), step)
            unit = normed[at, :]
            mass = jnp.mean(unit * scaled, axis=1, keepdims=True)
            grad = widen(inverses[at, :], width) * (shifted - unit * mass)
            grads[at, :] = grad
            rounded = grad.astype(low)
            branch[at, :] = rounded
            return total + jnp.sum(
                rounded.astype(full).reshape(step // 8, 8, width), axis=0
            )

        bias_sum = lax.fori_loop(0, slots // step, second_back, bias_sum)
    vector_sums[0:1, :] = jnp.sum(bias_sum, axis=0, keepdims=True)
    get_normed_2 = load(first_normed_in, normed)
    get_first = load(first_inverse_in, inverses)

    get_act.wait()
    piece = outer_send.shape[-2]
    for part in range(3):
        right = branch[:, part * third : (part + 1) * third]
        for block in range(4):
            result = dot(act_t[block * 8 * piece : (block + 1) * 8 * piece, :], right).astype(low)
            for place in range(8):
                sets[f"A{part}"].send[piece_at(block * 8 + place)] = result[
                    place * piece : (place + 1) * piece, :
                ]
        sets[f"A{part}"].start()
        tick(f"a{part}")

    get_values = load(values_in, act_t.at[0:rows, 0:width])
    steps = heads // 2 * sentences

    def prob_slot(index, half):
        start = pl.multiple_of(rows + lax.rem(index, 4) * slots, slots)
        return act_t.at[pl.ds(start, slots), half * slots : (half + 1) * slots]

    def prob_copies(index):
        first = lax.rem(index, sentences) * heads + lax.div(index, sentences) * 2
        return [
            pltpu.make_async_copy(
                probs_in.at[first + half],
                prob_slot(index, half),
                prob_sems.at[lax.rem(index, 4), half],
            )
            for half in range(2)
        ]

    for index in range(3):
        for copy in prob_copies(index):
            copy.start()

    get_outer.wait()
    get_hidden.wait()
    block, step = wide // 2, 32

    def slope_dot(index):
        return dot(branch[...], w_rows[index * block : (index + 1) * block, :], 1, 1)

    def slope_block(index, result):
        part, lanes = index // 2, slice(index % 2 * block, (index % 2 + 1) * block)
        total = jnp.zeros((8, block), full)
        for place in range(0, rows, step):
            at = slice(place, place + step)
            value = (result[at] * inner_grad[part, at, lanes].astype(full)).astype(low)
            inner_grad[part, at, lanes] = value
            total = total + jnp.sum(value.astype(full).reshape(step // 8, 8, block), axis=0)
        total = jnp.sum(total, axis=0, keepdims=True)
        for piece in range(0, block, 256):
            flat = index * block + piece
            row, lane = 8 + flat // width, flat % width
            vector_sums[row : row + 1, lane : lane + 256] = total[:, piece : piece + 256]

    before = slope_dot(0)
    for index in range(2 * parts):
        part = index // 2
        result = slope_dot(index + 1) if index + 1 < 2 * parts else None
        if index % 2 == 0:
            get_slopes[part].wait()
        slope_block(index, before)
        before = result
        if index % 2 == 0:
            tick(f"e{part}")
            continue
        tick(f"g{part}")
        for piece in range(2):
            result = dot(
                hidden_t[piece * (width // 2) : (piece + 1) * (width // 2), :], inner_grad[part]
            )
            for place in range(devices // 2):
                value = result[place * own_rows : (place + 1) * own_rows]
                sets[f"B{part}"].send[piece_at(piece * (devices // 2) + place)] = jnp.concatenate(
                    [value[:, : wide // 2], value[:, wide // 2 :]], axis=0
                ).astype(low)
        sets[f"B{part}"].start()
        tick(f"w{part}")
    mixture_t = hidden_t
    get_mixture = load(mixture_t_in, mixture_t)
    square_loads = [
        load(source, w_rows.at[pl.ds(place * width, width)])
        for place, source in enumerate((output_weight, query_weight, key_weight, value_weight))
    ]

    get_inner.wait()
    get_normed_2.wait()
    get_first.wait()
    span, step = rows // 2, 32
    gain = first_gain[...].reshape(1, width)

    def hidden_dot(start):
        total = None
        for part in range(parts):
            term = dot(
                inner_grad[part, start : start + span, :],
                w_columns[:, part * wide : (part + 1) * wide],
                1,
                1,
            )
            total = term if total is None else total + term
        return total

    def first_back(start, total, gain_sum, shift_sum, bias_sum):
        for place in range(0, span, step):
            at = slice(start + place, start + place + step)
            upstream = grads[at, :] + total[place : place + step]
            unit = normed[at, :]
            gain_sum = gain_sum + jnp.sum((upstream * unit).reshape(step // 8, 8, width), axis=0)
            shift_sum = shift_sum + jnp.sum(upstream.reshape(step // 8, 8, width), axis=0)
            scaled = upstream * gain
            center = scaled - jnp.mean(scaled, axis=1, keepdims=True)
            grad = widen(inverses[at, :], width) * (
                center - unit * jnp.mean(scaled * unit, axis=1, keepdims=True)
            )
            grads[at, :] = grad
            rounded = grad.astype(low)
            branch[at, :] = rounded
            bias_sum = bias_sum + jnp.sum(
                rounded.astype(full).reshape(step // 8, 8, width), axis=0
            )
        return gain_sum, shift_sum, bias_sum

    zero = jnp.zeros((8, width), full)
    state = (zero, zero, zero)
    before = hidden_dot(0)
    tick("h0")
    result = hidden_dot(span)
    state = first_back(0, before, *state)
    tick("h1")
    state = first_back(span, result, *state)
    tick("h2")
    for place, total in zip((3, 4, 5), state):
        vector_sums[place : place + 1, :] = jnp.sum(total, axis=0, keepdims=True)

    get_queries = load(queries_t_in, w_columns.at[:, 0:rows])
    get_keys = load(keys_t_in, w_columns.at[:, rows : 2 * rows])
    tokens_t = inner_grad.at[1, 0:width, :]
    get_tokens = load(tokens_t_in, tokens_t)

    def square_pieces(place, index, result):
        lanes = pl.ds(index * 128, 128)
        for device in range(devices):
            at = slice(device * own_rows, (device + 1) * own_rows)
            z1, z0, y, x, core = piece_at(device)
            square_sends[place].at[z1, z0, y, x, core][:, lanes] = jnp.concatenate(
                [result[at, 0:128], result[at, 128:256]], axis=0
            ).astype(low)

    get_mixture.wait()
    for index in range(3):
        square_pieces(0, index, dot(mixture_t[...], branch[:, index * 256 : (index + 1) * 256]))
    pl.semaphore_wait(credit, 1)
    sets["C0"].start()
    tick("o")

    def start_sums(group, stage):
        for copy in sum_copies(group, stage)[1:]:
            copy.start()

    def sum_copies(group, stage):
        held, arrived, sems = group
        core, x, y, z0, z1 = (links[name][1] for name in ("core", "x", "y", "z0", "z1"))
        moves = ((core,), (x, y, x + y), (z0, z1, z0 + z1))[stage]
        base = (0, 1, 4)[stage]

        def copy(source, goal, move):
            return pltpu.make_async_remote_copy(
                src_ref=source,
                dst_ref=goal,
                send_sem=sems.at[stage, 0],
                recv_sem=sems.at[stage, 1],
                device_id=(me + move,),
                device_id_type=pl.DeviceIdType.MESH,
            )

        whole = arrived.at[pl.ds(base, len(moves))]
        return [copy(whole, whole, core)] + [
            copy(held.at[stage], arrived.at[base + index], move)
            for index, move in enumerate(moves)
        ]

    def sum_step(group, stage):
        held, arrived, _ = group
        copies = sum_copies(group, stage)
        copies[0].wait_send()
        copies[0].wait_recv()
        total = held[stage]
        for index in range(len(copies) - 1):
            total = total + arrived[(0, 1, 4)[stage] + index]
        if stage < 2:
            held[stage + 1] = total
            start_sums(group, stage + 1)
        elif group is early_sums:
            sums_out[...] = total
        else:
            sums_out[6:7, :] = total

    early_sums = (sum_held, sum_recv, sum_sems.at[0])
    late_sums = (late_held, late_recv, sum_sems.at[1])

    square_loads[0].wait()
    bias_row = vector_sums[5:6, :]
    upper = bias_row.astype(low)
    lower = (bias_row - upper.astype(full)).astype(low)
    split = jnp.concatenate([upper, lower, jnp.zeros((14, width), low)], axis=0)
    split = dot(split, w_rows[0:width, :], 1, 1)
    vector_sums[7:8, :] = split[0:1, :] + split[1:2, :]
    start_sums(early_sums, 0)
    get_totals.wait()
    upstream_t = inner_grad.at[0, 0:width, :]
    for sentence in range(sentences):
        spans = slice(sentence * slots, (sentence + 1) * slots)
        result = dot(w_rows[0:width, :], branch[spans, :], 1, 1)
        for head in range(heads):
            at = slice(head * HD, (head + 1) * HD)
            place = sentence * heads + head
            value = result[at] * inverse_totals[place, 0:1, :]
            mass = jnp.sum(value * mixture_t[at, spans].astype(full), axis=0, keepdims=True)
            inverse_totals[place] = mass
            upstream_t[at, spans] = value.astype(low)
    tick("m")

    get_queries.wait()
    get_keys.wait()
    get_values.wait()
    get_tokens.wait()
    empty = jnp.zeros((HD, slots), low)
    value_grads, key_grads = act_t.at[0:rows, 0:width], branch
    toward_refs = [normed.at[at : at + slots, 0:slots] for at in (0, slots)]
    score_refs = [inner_grad.at[2, at : at + slots, 0:slots] for at in (0, slots)]

    def projection_grads(group):
        at = slice(group * 256, (group + 1) * 256)
        left = tokens_t[...]
        square_pieces(1 + group, 0, dot(left, w_columns[at, 0:rows], 1, 1) * 0.125)
        square_pieces(1 + group, 1, dot(left, key_grads[:, at]))
        square_pieces(1 + group, 2, dot(left, value_grads[:, at]))
        sets[f"C{1 + group}"].start()

    def head_pair(index, carry):
        pair, sentence = lax.div(index, sentences), lax.rem(index, sentences)
        start = pl.multiple_of(pair * 128, 128)
        spans = pl.ds(pl.multiple_of(sentence * slots, slots), slots)
        key_spans = pl.ds(pl.multiple_of(rows + sentence * slots, slots), slots)
        for copy in prob_copies(index):
            copy.wait()

        @pl.when(index + 3 < steps)
        def _():
            for copy in prob_copies(index + 3):
                copy.start()

        def row(half):
            return pl.ds(pl.multiple_of(start + half * HD, HD), HD)

        def masked(half, value):
            return jnp.concatenate([value, empty] if half == 0 else [empty, value], axis=0)

        def toward(half):
            upstream = masked(half, upstream_t[row(half), spans])
            toward_refs[half][...] = dot(value_grads[spans, pl.ds(start, 128)], upstream)
            return dot(prob_slot(index, half)[...], upstream.T)

        def scores(half):
            mass = inverse_totals[sentence * heads + pair * 2 + half, 0:1, :]
            prob = prob_slot(index, half)
            result = toward_refs[half]
            for piece in range(0, slots, 64):
                at = slice(piece, piece + 64)
                score_refs[half][at, :] = (
                    prob[at, :].astype(full) * (result[at, :] - mass)
                ).astype(low)

        def finish(half):
            score = score_refs[half][...]
            query = w_columns[row(half), spans]
            key = w_columns[row(half), key_spans]
            key_grad = dot(score, masked(half, query).T)
            w_columns[row(half), spans] = dot(key, score).astype(low)
            return key_grad

        value_grad = toward(0)
        value_grad = value_grad + toward(1)
        scores(0)
        key_grad = finish(0)
        scores(1)
        key_grad = key_grad + finish(1)
        key_grads[spans, pl.ds(start, 128)] = key_grad.astype(low)
        value_grads[spans, pl.ds(start, 128)] = value_grad.astype(low)
        per_group = steps // 3
        for when in range(steps):
            last = when % per_group == per_group - 1
            vector_stage = {5: 0, 11: 1}.get(when)
            if not last and vector_stage is None and f"s{when}" not in SCHEDULE:
                continue

            def after(when=when, last=last, vector_stage=vector_stage):
                tick(f"s{when}")
                if vector_stage is not None:
                    sum_step(early_sums, vector_stage)
                if last:
                    projection_grads(when // per_group)
                    tick(f"c{when // per_group}")

            pl.when(index == when)(after)
        return carry

    lax.fori_loop(0, steps, head_pair, 0)

    late_held[0] = 0.125 * dot(jnp.ones((8, rows), low), w_columns[:, 0:rows], 1, 1)[0:1, :]
    start_sums(late_sums, 0)

    for copy in square_loads[1:]:
        copy.wait()

    outs = []
    finished = []

    def pack(source, start, lane=0):
        size, lanes = source.shape
        outs.append(
            load(source, packed_out.at[pl.ds(rows + start, size), pl.ds(lane, lanes)])
        )

    def pack_finished():
        for name in sets:
            if name in done and name not in finished:
                finished.append(name)
                place = int(name[1])
                if name[0] == "A":
                    pack(columns(outer_out, place * third, third), 0, place * third)
                elif name[0] == "B":
                    half = wide // 2
                    for piece in range(0, half, 256):
                        lane = place * half + piece
                        pack(
                            columns(inner_out, lane, 256),
                            outer_out.shape[0] + lane // width * inner_out.shape[0],
                            lane % width,
                        )
                else:
                    size = square_out.shape[1]
                    pack(square_out.at[place], square_at + place // 2 * size, place % 2 * (width // 2))

    sums_at = outer_out.shape[0] + 2 * inner_out.shape[0]
    square_at = sums_at + sums_out.shape[0] + loss_out.shape[0]
    pack(loss_out, sums_at + sums_out.shape[0])
    turn = 0
    for index, start in enumerate(range(0, rows, span)):
        at = slice(start, start + span)
        total = grads[at, :] + 0.125 * dot(w_columns[:, at], w_rows[width : 2 * width, :], 0, 1)
        for place, terms in ((2, key_grads), (3, value_grads)):
            tick(f"t{turn}")
            if turn == 3:
                sum_step(early_sums, 2)
            if turn in (1, 4):
                sum_step(late_sums, turn // 3)
            turn += 1
            total = total + dot(
                terms[at, :], w_rows[place * width : (place + 1) * width, :], 1, 1
            )
        grads[at, :] = total
        outs.append(load(grads.at[at], packed_out.at[at]))
        tick(f"t{turn}")
        turn += 1
        pack_finished()
    for name, stage in SCHEDULE["end"]:
        if (name, stage) == SCHEDULE["end"][-1]:
            sum_step(late_sums, 2)
            pack(sums_out, sums_at)
        step_set(name, stage)
        pack_finished()
    for copy in outs:
        copy.wait()


def finish_kernel(
    devices,
    packed,
    loss_out,
    token_grad_out,
    query_out,
    query_bias,
    key_out,
    value_out,
    value_bias,
    output_out,
    output_bias,
    first_gain,
    first_shift,
    inner_out,
    inner_bias,
    outer_out,
    outer_bias,
    second_gain,
    second_shift,
    square_held,
    sums_held,
    sems,
):
    me = lax.axis_index("dp")
    rows, width = token_grad_out.shape
    own = query_out.shape[0]
    copies = []

    def move(source, target):
        copy = pltpu.make_async_copy(source, target, sems.at[len(copies)])
        copy.start()
        copies.append(copy)
        return copy

    outer_at = rows
    inner_at = outer_at + outer_out.shape[0]
    sums_at = inner_at + 4 * own
    square_at = sums_at + 24
    get_sums = move(packed.at[pl.ds(sums_at, 24)], sums_held)
    get_square = move(packed.at[pl.ds(square_at, 4 * own)], square_held)
    for start in range(0, rows, rows // 4):
        at = pl.ds(start, rows // 4)
        move(packed.at[at], token_grad_out.at[at])
    move(packed.at[pl.ds(outer_at, outer_out.shape[0])], outer_out)
    part = inner_out.shape[1] // 6
    for index in range(6):
        lane = index // 2 * part
        for piece in range(0, part, 256):
            first = lane + piece
            start = inner_at + first // width * 2 * own + index % 2 * own
            move(
                packed.at[pl.ds(start, own), pl.ds(first % width, 256)],
                inner_out.at[:, pl.ds(index * part + piece, 256)],
            )
    source = lax.broadcasted_iota(jnp.int32, (width, 128), 0)
    lane = lax.broadcasted_iota(jnp.int32, (width, 128), 1)

    def pick(values, start):
        chosen = jnp.where(source == lane + start, 1.0, 0.0)
        return lax.dot_general(
            values,
            chosen,
            (((1,), (0,)), ((), ())),
            precision=lax.Precision.HIGHEST,
            preferred_element_type=full,
        )

    get_sums.wait()
    picked = pick(sums_held[0:8, :], me * own)
    for place, ref in enumerate(
        (
            outer_bias,
            second_gain,
            second_shift,
            first_gain,
            first_shift,
            output_bias,
            query_bias,
            value_bias,
        )
    ):
        ref[...] = picked[place : place + 1, 0 : ref.shape[1]]
    wide = inner_bias.shape[1]
    per_row = width // wide
    row_ids = lax.broadcasted_iota(jnp.int32, (8, width), 0)
    chosen = jnp.sum(
        jnp.where(row_ids == lax.div(me, per_row), sums_held[8:16, :], 0.0),
        axis=0,
        keepdims=True,
    )
    inner_bias[...] = pick(jnp.broadcast_to(chosen, (8, width)), lax.rem(me, per_row) * wide)[
        0:1, 0:wide
    ]
    get_square.wait()
    half = width // 2

    def square(place, lower):
        start = place // 2 * 2 * own + lower * own
        return square_held[start : start + own, place % 2 * half : (place % 2 + 1) * half]

    def place_columns(target, column, place, index):
        lanes = slice(index * 128, (index + 1) * 128)
        for lower in range(2):
            at = column + lower * 128
            target[:, at : at + 128] = square(place, lower)[:, lanes]

    for index in range(3):
        place_columns(output_out, index * 256, 0, index)
        for place, target in enumerate((query_out, key_out, value_out)):
            place_columns(target, index * 256, 1 + index, place)
    loss_out[...] = sums_held[16:17, 0:1]
    for copy in copies[2:]:
        copy.wait()


def linked_device(
    devices,
    tokens,
    lengths,
    groups,
    query_weight,
    query_bias,
    key_weight,
    value_weight,
    value_bias,
    output_weight,
    output_bias,
    first_gain,
    first_shift,
    inner_weight,
    inner_bias,
    outer_weight,
    outer_bias,
    second_gain,
    second_shift,
):
    sentences = lengths.shape[0]
    rows, width = tokens.shape
    slots = rows // sentences
    inner = inner_weight.shape[1]
    vectors = (
        query_bias,
        value_bias,
        output_bias,
        first_gain,
        first_shift,
        outer_bias,
        second_gain,
        second_shift,
    )
    weights = (query_weight, key_weight, value_weight, output_weight, inner_weight, outer_weight)
    (
        layer_output,
        pooled,
        live_mean,
        queries_t,
        keys_t,
        values,
        mixture_t,
        tokens_t,
        probs,
        inverse_totals,
        first_normed,
        first_inverse,
        hidden_t,
        second_normed,
        second_inverse,
        activated_t,
        slopes,
    ) = forward(lengths, tokens, vectors, inner_bias[None], weights)
    hbm = pl.BlockSpec(memory_space=pl.ANY)
    vmem = pl.BlockSpec(memory_space=pltpu.VMEM)
    shape = jax.ShapeDtypeStruct
    piece_outer = (inner // devices, width)
    piece_inner = (2 * width // devices, inner // 2)
    piece_square = (2 * width // devices, width // 2)

    def levels(piece, lead=()):
        third = (piece[0] // 3, piece[1])
        shapes = [(2,) * 5 + piece, (2,) * 4 + piece]
        shapes += [(3,) + (2,) * k + third for k in (3, 2)] + [(3, 3) + third]
        return [pltpu.VMEM(lead + s, low) for s in shapes]

    sets = len(SETS)
    extra = piece_outer[0] + 2 * piece_inner[0] + 16 + 8 + 2 * piece_square[0]
    packed = pl.pallas_call(
        functools.partial(backward_kernel, devices, sentences),
        in_specs=[vmem] * 5 + [hbm] * 20,
        out_specs=hbm,
        out_shape=shape((rows + extra, width), full),
        scratch_shapes=[
            pltpu.VMEM((8, width), full),
            pltpu.VMEM(piece_outer, full),
            pltpu.VMEM(piece_inner, full),
            pltpu.VMEM((4,) + piece_square, full),
            pltpu.VMEM((16, width), full),
            pltpu.VMEM(activated_t.shape, low),
            pltpu.VMEM(slopes.shape, low),
            pltpu.VMEM((inner, width), low),
            pltpu.VMEM((width, inner), low),
            pltpu.VMEM((rows, width), full),
            pltpu.VMEM((rows, width), full),
            pltpu.VMEM((rows, width), low),
            pltpu.VMEM((width, rows), low),
            pltpu.VMEM((rows, 128), full),
            pltpu.VMEM(inverse_totals.shape, full),
            pltpu.VMEM((16, 128), low),
            pltpu.VMEM((devices, 16, 128), low),
        ]
        + levels(piece_outer)
        + levels(piece_inner)
        + levels(piece_square, (4,))[2:]
        + [
            pltpu.VMEM((3, 16, width), full),
            pltpu.VMEM((7, 16, width), full),
            pltpu.VMEM((3, 1, width), full),
            pltpu.VMEM((7, 1, width), full),
            pltpu.SemaphoreType.DMA((44,)),
            pltpu.SemaphoreType.DMA((4, 2)),
            pltpu.SemaphoreType.DMA((2,)),
            pltpu.SemaphoreType.DMA((sets, 4)),
            pltpu.SemaphoreType.DMA((sets, 4)),
            pltpu.SemaphoreType.DMA((2, 3, 2)),
            pltpu.SemaphoreType.REGULAR,
        ],
        compiler_params=pltpu.CompilerParams(
            collective_id=0, has_side_effects=True, vmem_limit_bytes=63 * MIB
        ),
        name="decode",
    )(
        pooled,
        live_mean,
        first_gain,
        second_gain,
        groups,
        activated_t,
        slopes,
        second_normed,
        second_inverse,
        hidden_t,
        first_normed,
        first_inverse,
        mixture_t,
        queries_t,
        keys_t,
        values,
        tokens_t,
        probs,
        inverse_totals,
        *weights,
    )
    own = width // devices
    finals = pl.pallas_call(
        functools.partial(finish_kernel, devices),
        out_shape=[
            shape((1, 1), full),
            shape((rows, width), full),
            shape((own, width), full),
            shape((1, own), full),
            shape((own, width), full),
            shape((own, width), full),
            shape((1, own), full),
            shape((own, width), full),
            shape((1, own), full),
            shape((1, own), full),
            shape((1, own), full),
            shape((own, inner), full),
            shape((1, inner // devices), full),
            shape((inner // devices, width), full),
            shape((1, own), full),
            shape((1, own), full),
            shape((1, own), full),
        ],
        in_specs=[hbm],
        out_specs=[vmem, hbm] + [vmem] * 15,
        scratch_shapes=[
            pltpu.VMEM((2 * piece_square[0], width), full),
            pltpu.VMEM((24, width), full),
            pltpu.SemaphoreType.DMA((20,)),
        ],
        compiler_params=pltpu.CompilerParams(vmem_limit_bytes=32 * MIB),
        name="finish",
    )(packed)
    finals = [f.reshape(f.shape[1:]) if f.shape[0] == 1 else f for f in finals]
    return (finals[0].reshape(()), layer_output, *finals[1:])


highest = lax.Precision.HIGHEST


def project(operand, weight):
    return jnp.dot(operand, weight, preferred_element_type=jnp.float32)


def transpose_left(left_rows, right_rows):
    return lax.dot_general(
        left_rows, right_rows, (((0,), (0,)), ((), ())), preferred_element_type=jnp.float32
    )


def transpose_right(operand, weight):
    return lax.dot_general(
        operand, weight, (((1,), (1,)), ((), ())), preferred_element_type=jnp.float32
    )


def standardize(residual):
    center = residual - jnp.mean(residual, axis=-1, keepdims=True)
    inverse = lax.rsqrt(jnp.mean(center * center, axis=-1, keepdims=True) + layer_epsilon)
    return (center * inverse, inverse)


def standardize_back(upstream, normed, inverse, scaling):
    scaled = upstream * scaling
    return inverse * (
        scaled
        - jnp.mean(scaled, axis=-1, keepdims=True)
        - normed * jnp.mean(scaled * normed, axis=-1, keepdims=True)
    )


def gelu_slope(inner_pre):
    cumulative = 0.5 * (1.0 + lax.erf(inner_pre * (1.0 / math.sqrt(2.0))))
    density = jnp.exp(-0.5 * inner_pre * inner_pre) * (1.0 / math.sqrt(2.0 * math.pi))
    return cumulative + inner_pre * density


def masked_scores(queries, key_rows, key_live):
    scores = jnp.einsum("qhd,khd->hqk", queries, key_rows, preferred_element_type=jnp.float32)
    return jnp.where(key_live[None, None, :], scores, -1e30)


def attend(pieces):
    queries, key_rows, value_rows, key_live = pieces
    scores = masked_scores(queries, key_rows, key_live)
    summit = jnp.max(scores, axis=-1, keepdims=True)
    raised = jnp.exp(scores - summit)
    totals = jnp.sum(raised, axis=-1, keepdims=True)
    weights = (raised / totals).astype(jnp.bfloat16)
    mixture = jnp.einsum("hqk,khd->qhd", weights, value_rows, preferred_element_type=jnp.float32)
    return (mixture.astype(jnp.bfloat16), (summit + jnp.log(totals))[..., 0])


def attend_back(pieces):
    queries, key_rows, value_rows, key_live, log_total, upstream = pieces
    scores = masked_scores(queries, key_rows, key_live)
    chances = jnp.exp(scores - log_total[..., None])
    toward = jnp.einsum("qhd,khd->hqk", upstream, value_rows, preferred_element_type=jnp.float32)
    score_grad = (chances * (toward - jnp.sum(chances * toward, axis=-1, keepdims=True))).astype(
        jnp.bfloat16
    )
    value_grad = jnp.einsum(
        "hqk,qhd->khd", chances.astype(jnp.bfloat16), upstream, preferred_element_type=jnp.float32
    )
    query_grad = jnp.einsum(
        "hqk,khd->qhd", score_grad, key_rows, preferred_element_type=jnp.float32
    )
    key_grad = jnp.einsum("hqk,qhd->khd", score_grad, queries, preferred_element_type=jnp.float32)
    return (
        query_grad.astype(jnp.bfloat16),
        key_grad.astype(jnp.bfloat16),
        value_grad.astype(jnp.bfloat16),
    )


def contrast_rows(row_unit, unit_rows, row_groups, groups, row_start):
    similar = cosine_scale * lax.dot_general(
        row_unit, unit_rows, (((1,), (1,)), ((), ())), precision=highest
    )
    row_ids = row_start + jnp.arange(row_unit.shape[0])
    column_ids = jnp.arange(unit_rows.shape[0])
    itself = row_ids[:, None] == column_ids[None, :]
    logits = jnp.where(itself, -1e30, similar)
    summit = jnp.max(logits, axis=-1, keepdims=True)
    raised = jnp.exp(logits - summit)
    totals = jnp.sum(raised, axis=-1, keepdims=True)
    chances = raised / totals
    log_total = summit + jnp.log(totals)
    matched = jnp.logical_and(
        row_groups[:, None] == groups[None, :], jnp.logical_not(itself)
    ).astype(jnp.float32)
    weights = matched / jnp.maximum(jnp.sum(matched, axis=-1, keepdims=True), 1.0)
    row_mass = jnp.sum(weights, axis=-1, keepdims=True)
    loss_rows = row_mass[:, 0] * log_total[:, 0] - jnp.sum(weights * similar, axis=-1)
    return (jnp.sum(loss_rows), row_mass * chances - weights)


def per_device(
    tokens,
    lengths,
    groups,
    query_weight,
    query_bias,
    key_weight,
    value_weight,
    value_bias,
    output_weight,
    output_bias,
    first_gain,
    first_shift,
    inner_weight,
    inner_bias,
    outer_weight,
    outer_bias,
    second_gain,
    second_shift,
):
    seq_count = lengths.shape[0]
    slot_count = tokens.shape[0] // seq_count
    model_width = tokens.shape[1]
    heads_shape = (seq_count, slot_count, HEADS, HD)
    queries = ((project(tokens, query_weight) + query_bias) * 0.125).astype(jnp.bfloat16)
    key_rows = project(tokens, key_weight).astype(jnp.bfloat16)
    value_rows = (project(tokens, value_weight) + value_bias).astype(jnp.bfloat16)
    key_live = jnp.arange(slot_count)[None, :] < lengths[:, None]
    head_queries = queries.reshape(heads_shape)
    head_keys = key_rows.reshape(heads_shape)
    head_values = value_rows.reshape(heads_shape)
    mixture, log_total = lax.map(attend, (head_queries, head_keys, head_values, key_live))
    mixture = mixture.reshape(tokens.shape)
    first_normed, first_inverse = standardize(
        tokens.astype(jnp.float32) + project(mixture, output_weight) + output_bias
    )
    hidden = first_normed * first_gain + first_shift
    hidden_low = hidden.astype(jnp.bfloat16)
    inner_pre = project(hidden_low, inner_weight) + inner_bias
    activated = jax.nn.gelu(inner_pre, approximate=False).astype(jnp.bfloat16)
    second_normed, second_inverse = standardize(
        hidden + project(activated, outer_weight) + outer_bias
    )
    output = second_normed * second_gain + second_shift
    live_rows = key_live.astype(jnp.float32)[:, :, None]
    counts = lengths.astype(jnp.float32)[:, None]
    pooled = (
        jnp.sum(output.reshape(seq_count, slot_count, model_width) * live_rows, axis=1) / counts
    ).astype(jnp.bfloat16)
    everyone = lax.all_gather(pooled, "dp", axis=0, tiled=True).astype(jnp.float32)
    inverse_all = lax.rsqrt(jnp.sum(everyone * everyone, axis=-1, keepdims=True) + unit_epsilon)
    unit_rows = everyone * inverse_all
    first_row = lax.axis_index("dp") * seq_count
    own_unit = lax.dynamic_slice_in_dim(unit_rows, first_row, seq_count, 0)
    own_inverse = lax.dynamic_slice_in_dim(inverse_all, first_row, seq_count, 0)
    own_groups = lax.dynamic_slice_in_dim(groups, first_row, seq_count, 0)
    part_loss, coupling = contrast_rows(own_unit, unit_rows, own_groups, groups, first_row)
    loss_value = lax.psum(part_loss, "dp")
    spread = cosine_scale * lax.dot_general(
        coupling, own_unit, (((0,), (0,)), ((), ())), precision=highest
    )
    unit_grad = cosine_scale * jnp.dot(coupling, unit_rows, precision=highest) + lax.psum_scatter(
        spread, "dp", scatter_dimension=0, tiled=True
    )
    pooled_grad = own_inverse * (
        unit_grad - own_unit * jnp.sum(own_unit * unit_grad, axis=-1, keepdims=True)
    )
    grad_output = (pooled_grad[:, None, :] / counts[:, :, None] * live_rows).reshape(tokens.shape)
    second_gain_grad = jnp.sum(grad_output * second_normed, axis=0)
    second_shift_grad = jnp.sum(grad_output, axis=0)
    grad_second = standardize_back(grad_output, second_normed, second_inverse, second_gain)
    branch_grad = grad_second.astype(jnp.bfloat16)
    outer_bias_grad = jnp.sum(branch_grad, axis=0, dtype=jnp.float32)
    outer_weight_grad = transpose_left(activated, branch_grad)
    inner_grad = (transpose_right(branch_grad, outer_weight) * gelu_slope(inner_pre)).astype(
        jnp.bfloat16
    )
    inner_bias_grad = jnp.sum(inner_grad, axis=0, dtype=jnp.float32)
    inner_weight_grad = transpose_left(hidden_low, inner_grad)
    hidden_grad = grad_second + transpose_right(inner_grad, inner_weight)
    first_gain_grad = jnp.sum(hidden_grad * first_normed, axis=0)
    first_shift_grad = jnp.sum(hidden_grad, axis=0)
    grad_first = standardize_back(hidden_grad, first_normed, first_inverse, first_gain)
    attended_grad = grad_first.astype(jnp.bfloat16)
    output_bias_grad = jnp.sum(attended_grad, axis=0, dtype=jnp.float32)
    output_weight_grad = transpose_left(mixture, attended_grad)
    mixture_grad = transpose_right(attended_grad, output_weight).astype(jnp.bfloat16)
    query_grad, key_grad, value_grad = lax.map(
        attend_back,
        (
            head_queries,
            head_keys,
            head_values,
            key_live,
            log_total,
            mixture_grad.reshape(heads_shape),
        ),
    )
    query_grad = query_grad.reshape(tokens.shape)
    key_grad = key_grad.reshape(tokens.shape)
    value_grad = value_grad.reshape(tokens.shape)
    query_weight_grad = 0.125 * transpose_left(tokens, query_grad)
    query_bias_grad = 0.125 * jnp.sum(query_grad, axis=0, dtype=jnp.float32)
    key_weight_grad = transpose_left(tokens, key_grad)
    value_weight_grad = transpose_left(tokens, value_grad)
    value_bias_grad = jnp.sum(value_grad, axis=0, dtype=jnp.float32)
    token_grad = (
        grad_first
        + 0.125 * transpose_right(query_grad, query_weight)
        + transpose_right(key_grad, key_weight)
        + transpose_right(value_grad, value_weight)
    )
    summed = tuple(
        (
            lax.psum_scatter(query_weight_grad, "dp", scatter_dimension=0, tiled=True),
            lax.psum_scatter(query_bias_grad, "dp", scatter_dimension=0, tiled=True),
            lax.psum_scatter(key_weight_grad, "dp", scatter_dimension=0, tiled=True),
            lax.psum_scatter(value_weight_grad, "dp", scatter_dimension=0, tiled=True),
            lax.psum_scatter(value_bias_grad, "dp", scatter_dimension=0, tiled=True),
            lax.psum_scatter(output_weight_grad, "dp", scatter_dimension=0, tiled=True),
            lax.psum_scatter(output_bias_grad, "dp", scatter_dimension=0, tiled=True),
            lax.psum_scatter(first_gain_grad, "dp", scatter_dimension=0, tiled=True),
            lax.psum_scatter(first_shift_grad, "dp", scatter_dimension=0, tiled=True),
            lax.psum_scatter(inner_weight_grad, "dp", scatter_dimension=0, tiled=True),
            lax.psum_scatter(inner_bias_grad, "dp", scatter_dimension=0, tiled=True),
            lax.psum_scatter(outer_weight_grad, "dp", scatter_dimension=0, tiled=True),
            lax.psum_scatter(outer_bias_grad, "dp", scatter_dimension=0, tiled=True),
            lax.psum_scatter(second_gain_grad, "dp", scatter_dimension=0, tiled=True),
            lax.psum_scatter(second_shift_grad, "dp", scatter_dimension=0, tiled=True),
        )
    )
    return (loss_value, output.astype(jnp.bfloat16), token_grad) + summed


def solution(mesh):
    placed = (
        P("dp", None),
        P("dp"),
        P(),
        P(),
        P(),
        P(),
        P(),
        P(),
        P(),
        P(),
        P(),
        P(),
        P(),
        P(),
        P(),
        P(),
        P(),
        P(),
    )
    devices = mesh.shape["dp"]
    body = functools.partial(linked_device, devices) if devices == 32 else per_device
    return jax.shard_map(
        body,
        mesh=mesh,
        in_specs=placed,
        out_specs=(
            P(),
            P("dp", None),
            P("dp", None),
            P("dp", None),
            P("dp"),
            P("dp", None),
            P("dp", None),
            P("dp"),
            P("dp", None),
            P("dp"),
            P("dp"),
            P("dp"),
            P("dp", None),
            P("dp"),
            P("dp", None),
            P("dp"),
            P("dp"),
            P("dp"),
        ),
        check_vma=False,
    )
```

```python
import functools
import math

import jax
import jax.numpy as jnp
from jax import lax
from jax.experimental import pallas as pl
from jax.experimental.pallas import tpu as pltpu
from jax.sharding import PartitionSpec as P

HEADS = 12
HD = 64
cosine_scale = 20.0
layer_epsilon = 1e-06
unit_epsilon = 1e-06
low = jnp.bfloat16
full = jnp.float32
MIB = 1 << 20


def dot(left, right, left_axis=1, right_axis=0):
    return lax.dot_general(
        left, right, (((left_axis,), (right_axis,)), ((), ())), preferred_element_type=full
    )


def gelu_pair(value):
    square = value * value
    series = 1.42509398e-06
    for factor in (-3.66948363e-05, -8.78201378e-05, 3.63922768e-02, 7.97869715e-01):
        series = series * square + factor
    cumulative = 0.5 * jnp.tanh(value * series) + 0.5
    bell = jnp.exp(square * -0.5)
    return value * cumulative, cumulative + value * bell * (1.0 / math.sqrt(2.0 * math.pi))


def widen(column, lanes):
    return jnp.concatenate([column] * (lanes // 128), axis=1)


def standardized(residual):
    center = residual - jnp.mean(residual, axis=1, keepdims=True)
    inverse = lax.rsqrt(jnp.mean(center * center, axis=1, keepdims=True) + layer_epsilon)
    return center * inverse, inverse


def forward_kernel(
    sentences,
    lengths,
    query_bias,
    value_bias,
    output_bias,
    first_gain,
    first_shift,
    inner_bias,
    outer_bias,
    second_gain,
    second_shift,
    tokens_in,
    query_weight,
    key_weight,
    value_weight,
    output_weight,
    inner_weight,
    outer_weight,
    layer_output_out,
    pooled,
    live_mean,
    queries_t_out,
    keys_t_out,
    values_out,
    mixture_t_out,
    tokens_t_out,
    probs_out,
    inverse_totals_out,
    first_normed_out,
    first_inverse_out,
    hidden_t_out,
    second_normed_out,
    second_inverse_out,
    activated_t_out,
    slopes_out,
    tokens,
    w_query,
    w_key,
    w_value,
    w_output,
    w_inner,
    w_outer,
    layer_output,
    queries_t,
    keys_t,
    values,
    mixture_t,
    tokens_t,
    inverse_totals,
    first_normed,
    first_inverse,
    hidden_low,
    hidden_t,
    second_normed,
    second_inverse,
    activated,
    activated_t,
    slopes,
    mask_block,
    in_sems,
    out_sems,
    prob_sems,
    feed_sems,
):
    rows, width = tokens.shape
    slots = rows // sentences
    inner = w_inner.shape[1]
    wide = slopes.shape[2]
    loads = [
        pltpu.make_async_copy(source, target, in_sems.at[place])
        for place, (source, target) in enumerate(
            (
                (tokens_in, tokens),
                (query_weight, w_query),
                (key_weight, w_key),
                (value_weight, w_value),
                (output_weight, w_output),
                (inner_weight, w_inner),
                (outer_weight, w_outer),
            )
        )
    ]
    for copy in loads:
        copy.start()
    stores = []

    def store(source, target):
        copy = pltpu.make_async_copy(source, target, out_sems.at[len(stores)])
        copy.start()
        stores.append(copy)

    def line(ref):
        return ref[...].reshape(1, ref.shape[0])

    key_rows = activated.at[:, 0:width]
    values_t = activated.at[0:width, width : width + rows]

    def prob_slot(pair, unit):
        start = pl.multiple_of((lax.rem(pair, 3) * 2 + unit // 2) * slots, slots)
        lane = unit % 2 * slots
        return activated_t.at[pl.ds(start, slots), lane : lane + slots]

    slot_ids = lax.broadcasted_iota(jnp.int32, (slots, 128), 0)
    lane_ids = lax.broadcasted_iota(jnp.int32, (slots, 128), 1)
    for sentence in range(sentences):
        mask_block[sentence] = jnp.where(
            jnp.logical_and(slot_ids >= lengths[sentence], lane_ids == 0), -1e30, 0.0
        ).astype(low)

    for copy in loads[:4]:
        copy.wait()
    span = 512
    pieces = [slice(start, start + span) for start in range(0, rows, span)]
    bias = line(query_bias)
    for at in pieces:
        queries_t[:, at] = ((dot(tokens[at, :], w_query[...]) + bias) * 0.125).astype(low).T
    for at in pieces:
        result = dot(tokens[at, :], w_key[...]).astype(low)
        key_rows[at, :] = result
        keys_t[:, at] = result.T
    bias = line(value_bias)
    for at in pieces:
        result = (dot(tokens[at, :], w_value[...]) + bias).astype(low)
        values[at, :] = result
        values_t[:, at] = result.T
    for at in pieces:
        tokens_t[:, at] = tokens[at, :].T
    store(queries_t, queries_t_out)
    store(keys_t, keys_t_out)
    store(values, values_out)
    store(tokens_t, tokens_t_out)

    pick_row = jnp.where(
        lax.broadcasted_iota(jnp.int32, (128, slots), 0) == 0, 1.0, 0.0
    ).astype(low)
    empty = jnp.zeros((HD, slots), low)

    units = [(sentence, half) for sentence in range(sentences) for half in range(2)]

    def prob_copies(pair):
        return [
            pltpu.make_async_copy(
                prob_slot(pair, unit),
                probs_out.at[sentence * HEADS + pair * 2 + half],
                prob_sems.at[lax.rem(pair, 3), unit],
            )
            for unit, (sentence, half) in enumerate(units)
        ]

    def head_pair(exact, pair, carry):
        start = pl.multiple_of(pair * 128, 128)

        @pl.when(pair >= 3)
        def _():
            for copy in prob_copies(pair):
                copy.wait()

        def spans(unit):
            sentence = units[unit][0]
            return slice(sentence * slots, (sentence + 1) * slots)

        def get_scores(unit):
            sentence, half = units[unit]
            left = jnp.concatenate(
                [key_rows[spans(unit), pl.ds(start, 128)], mask_block[sentence]], axis=1
            )
            own = queries_t[pl.ds(pl.multiple_of(start + half * HD, HD), HD), spans(unit)]
            parts = [own, empty] if half == 0 else [empty, own]
            return dot(left, jnp.concatenate(parts + [pick_row], axis=0))

        def get_probs(unit, scores):
            sentence, half = units[unit]
            if exact:
                summit = jnp.max(scores, axis=0, keepdims=True)
            totals = jnp.zeros((8, slots), full)
            slot = prob_slot(pair, unit)
            step = 64
            parts = []
            for place in range(0, slots, step):
                piece = scores[place : place + step, :]
                piece = jnp.exp(piece - summit if exact else piece)
                totals = totals + jnp.sum(piece.reshape(step // 8, 8, slots), axis=0)
                piece = piece.astype(low)
                slot[place : place + step, :] = piece
                parts.append(piece)
            inverse = 1.0 / jnp.sum(totals, axis=0, keepdims=True)
            inverse_totals[sentence * HEADS + pair * 2 + half] = inverse
            return jnp.concatenate(parts, axis=0), inverse

        def mix(unit, raised, inverse):
            row = pl.multiple_of(start + units[unit][1] * HD, HD)
            mixed = dot(values_t[pl.ds(row, HD), spans(unit)], raised) * inverse
            mixture_t[pl.ds(row, HD), spans(unit)] = mixed.astype(low)

        count = len(units)
        scored, raised = {}, {}
        for turn in range(count + 2):
            if turn < count:
                scored[turn] = get_scores(turn)
            if 0 <= turn - 1 < count:
                raised[turn - 1] = get_probs(turn - 1, scored.pop(turn - 1))
            if turn >= 2:
                mix(turn - 2, *raised.pop(turn - 2))
        for copy in prob_copies(pair):
            copy.start()
        return carry

    head_ids = lax.broadcasted_iota(jnp.int32, (16, width), 0)
    column_ids = lax.broadcasted_iota(jnp.int32, (16, width), 1)
    selector = jnp.where(head_ids == lax.div(column_ids, HD), 1.0, 0.0).astype(low)

    def largest(ref):
        return jnp.max(dot(selector, ref[...] * ref[...]), axis=1, keepdims=True)

    bound = jnp.max(largest(queries_t) * largest(keys_t))

    @pl.when(bound < 1600.0)
    def _():
        lax.fori_loop(0, HEADS // 2, functools.partial(head_pair, False), 0)

    @pl.when(jnp.logical_not(bound < 1600.0))
    def _():
        lax.fori_loop(0, HEADS // 2, functools.partial(head_pair, True), 0)

    store(mixture_t, mixture_t_out)
    store(inverse_totals, inverse_totals_out)

    loads[4].wait()
    bias, gain, shift = line(output_bias), line(first_gain), line(first_shift)
    span, step = 256, 32
    for start in range(0, rows, span):
        attended = dot(mixture_t[:, start : start + span], w_output[...], 0, 0)
        for place in range(0, span, step):
            at = slice(start + place, start + place + step)
            normed, inverse = standardized(
                tokens[at, :].astype(full) + attended[place : place + step] + bias
            )
            first_normed[at, :] = normed
            first_inverse[at, :] = jnp.broadcast_to(inverse, (step, 128))
            hidden_low[at, :] = (normed * gain + shift).astype(low)
        at = slice(start, start + span)
        hidden_t[:, at] = hidden_low[at, :].T
    store(first_normed, first_normed_out)
    store(first_inverse, first_inverse_out)
    store(hidden_t, hidden_t_out)

    loads[5].wait()
    for pair in range(HEADS // 2 - 3, HEADS // 2):
        for copy in prob_copies(pair):
            copy.wait()

    def feed_copies(index):
        start = pl.multiple_of(index * wide, wide)
        return (
            pltpu.make_async_copy(
                activated_t.at[pl.ds(start, wide)],
                activated_t_out.at[pl.ds(start, wide)],
                feed_sems.at[index, 0],
            ),
            pltpu.make_async_copy(
                slopes.at[index], slopes_out.at[index], feed_sems.at[index, 1]
            ),
        )

    def feed(index, carry):
        start = pl.multiple_of(index * wide, wide)
        weight = w_inner[:, pl.ds(start, wide)]
        offset = inner_bias[:, pl.ds(start, wide)]
        block, step = 128, 16

        def gelu_block(place, pre):
            at = slice(place, place + block)
            parts = []
            for piece in range(0, block, step):
                value, slope = gelu_pair(pre[piece : piece + step] + offset)
                slopes[index, place + piece : place + piece + step, :] = slope.astype(low)
                parts.append(value.astype(low))
            value = jnp.concatenate(parts, axis=0)
            activated[at, pl.ds(start, wide)] = value
            activated_t[pl.ds(start, wide), at] = value.T

        before = None
        for place in range(0, rows, block):
            pre = dot(hidden_low[place : place + block, :], weight)
            if before is not None:
                gelu_block(place - block, before)
            before = pre
        gelu_block(rows - block, before)
        for copy in feed_copies(index):
            copy.start()
        return carry

    lax.fori_loop(0, inner // wide, feed, 0)

    loads[6].wait()
    bias, gain_2, shift_2 = line(outer_bias), line(second_gain), line(second_shift)
    live_sums = [jnp.zeros((8, width), full) for _ in range(sentences)]
    for start in range(0, rows, span):
        branch = dot(activated[start : start + span, :], w_outer[...])
        sentence = start // slots
        length = lengths[sentence]
        for place in range(0, span, step):
            at = slice(start + place, start + place + step)
            hidden = first_normed[at, :] * gain + shift
            normed, inverse = standardized(hidden + branch[place : place + step] + bias)
            second_normed[at, :] = normed
            layer_output[at, :] = (normed * gain_2 + shift_2).astype(low)
            slot_row = lax.broadcasted_iota(jnp.int32, (step, 128), 0) + (
                start + place - sentence * slots
            )
            live = jnp.where(slot_row < length, 1.0, 0.0)
            live_sums[sentence] = live_sums[sentence] + jnp.sum(
                (normed * widen(live, width)).reshape(step // 8, 8, width), axis=0
            )
            second_inverse[at, :] = inverse * live * (1.0 / length.astype(full))
        at = slice(start, start + span)
        store(second_normed.at[at], second_normed_out.at[at])
        store(layer_output.at[at], layer_output_out.at[at])
        store(second_inverse.at[at], second_inverse_out.at[at])
    for sentence in range(sentences):
        mean_normed = jnp.sum(live_sums[sentence], axis=0, keepdims=True) / lengths[
            sentence
        ].astype(full)
        live_mean[sentence] = jnp.broadcast_to(mean_normed, (8, width))
        vector = (mean_normed * gain_2 + shift_2).astype(low).astype(full)
        pooled[sentence] = jnp.broadcast_to(vector, (8, width))
    for index in range(inner // wide):
        for copy in feed_copies(index):
            copy.wait()
    for copy in stores:
        copy.wait()


def forward(lengths, tokens, vectors, inner_bias, weights):
    sentences = lengths.shape[0]
    rows, width = tokens.shape
    slots = rows // sentences
    inner = weights[4].shape[1]
    wide = 1024
    hbm = pl.BlockSpec(memory_space=pl.ANY)
    vmem = pl.BlockSpec(memory_space=pltpu.VMEM)
    shape = jax.ShapeDtypeStruct
    kept = [
        ((rows, width), low),
        ((width, rows), low),
        ((width, rows), low),
        ((rows, width), low),
        ((width, rows), low),
        ((width, rows), low),
        ((sentences * HEADS, 1, slots), full),
        ((rows, width), full),
        ((rows, 128), full),
        ((rows, width), low),
        ((width, rows), low),
        ((rows, width), full),
        ((rows, 128), full),
        ((rows, inner), low),
        ((inner, rows), low),
        ((inner // wide, rows, wide), low),
    ]
    outs = [shape(*k) for k in kept]
    per_sentence = shape((sentences, 8, width), full)
    probs = shape((sentences * HEADS, slots, slots), low)
    return pl.pallas_call(
        functools.partial(forward_kernel, sentences),
        in_specs=[pl.BlockSpec(memory_space=pltpu.SMEM)] + [vmem] * 9 + [hbm] * 7,
        out_specs=[hbm, vmem, vmem] + [hbm] * 14,
        out_shape=[outs[0], per_sentence, per_sentence]
        + outs[1:6]
        + [probs]
        + outs[6:9]
        + outs[10:13]
        + outs[14:],
        scratch_shapes=[pltpu.VMEM((rows, width), low)]
        + [pltpu.VMEM(w.shape, low) for w in weights]
        + [pltpu.VMEM(*k) for k in kept]
        + [
            pltpu.VMEM((sentences, slots, 128), low),
            pltpu.SemaphoreType.DMA((7,)),
            pltpu.SemaphoreType.DMA((32,)),
            pltpu.SemaphoreType.DMA((3, 2 * sentences)),
            pltpu.SemaphoreType.DMA((inner // wide, 2)),
        ],
        compiler_params=pltpu.CompilerParams(vmem_limit_bytes=63 * MIB),
        name="encode",
    )(lengths, *vectors[:5], inner_bias, *vectors[5:], tokens, *weights)


SETS = ("A0", "A1", "A2", "B0", "B1", "B2", "C0", "C1", "C2", "C3")

SCHEDULE = {
    "e0": (("A0", 0),),
    "g0": (("A1", 0),),
    "e1": (("A2", 0),),
    "g1": (("A0", 1),),
    "w1": (("B0", 0),),
    "w2": (("A1", 1), ("B1", 0),),
    "h0": (("B2", 0), ("A0", 2), ("A2", 1),),
    "h1": (("B0", 1),),
    "h3": (("A1", 2),),
    "o": (("B1", 1),),
    "m": (("B2", 1), ("C0", 0),),
    "s1": (("A0", 3), ("A2", 2),),
    "s2": (("B0", 2),),
    "s3": (("A1", 3),),
    "c0": (("B1", 2),),
    "s5": (("C1", 0),),
    "s6": (("C0", 1), ("B2", 2),),
    "c1": (("A2", 3), ("B0", 3),),
    "s9": (("C2", 0),),
    "s10": (("C1", 1), ("C0", 2),),
    "c2": (("B1", 3), ("C2", 1),),
    "t1": (("C3", 0), ("C1", 2),),
    "t2": (("B2", 3), ("C2", 2),),
    "t4": (("C3", 1), ("C0", 3),),
    "end": (("C1", 3), ("C3", 2), ("C2", 3), ("C3", 3),),
}


class Summation:
    def __init__(self, name, send, held, out, sems, me, links):
        self.send, self.held, self.out = send, held, out
        self.place = SETS.index(name)
        self.odd = self.place % 2
        self.send_sems, self.recv_sems = sems
        self.me, self.links = me, links
        self.third = held[0].shape[-2] // 3

    def side(self, link, away):
        bit = self.links[link][0]
        return 1 - bit if away else bit

    def halves(self, stage, away):
        h = self.third

        def side(link):
            return self.side(link, away)

        if stage == 0:
            return [(self.send.at[:, :, :, :, side("core")], "core")]
        r = self.held[stage - 1]
        if stage == 1:
            return [
                (r.at[:, :, :, side("x"), pl.ds(0, h)], "x"),
                (r.at[:, :, side("y"), :, pl.ds(h, h)], "y"),
                (r.at[:, side("z0"), :, :, pl.ds(2 * h, h)], "z0"),
            ]
        last = (r.at[2, :, side("y")], "y") if self.odd else (r.at[2, :, :, side("x")], "x")
        return [(r.at[0, :, :, side("y")], "y"), (r.at[1, :, :, side("x")], "x"), last]

    def quarter(self, parts, far, near):
        link = "z0" if parts == 0 else "x" if self.odd else "y"
        at = pl.ds(0, 2) if parts == 0 else pl.ds(2, 1)
        source = self.held[2].at[at, self.side("z1", far), self.side(link, near)]
        return at, source, self.me + far * self.links["z1"][1] + near * self.links[link][1]

    def copies(self, stage):
        moves = []
        if stage < 3:
            target = self.held[stage]
            for part, (source, link) in enumerate(self.halves(stage, 1)):
                goal = target if stage == 0 else target.at[part]
                moves.append((source, goal, self.me + self.links[link][1]))
        else:
            for parts in range(2):
                for slot, (far, near) in enumerate(((0, 1), (1, 0), (1, 1))):
                    at, source, device = self.quarter(parts, far, near)
                    moves.append((source, self.held[3].at[at, slot], device))
        return [self.copy(stage, *move) for move in moves]

    def copy(self, stage, source, goal, device):
        return pltpu.make_async_remote_copy(
            src_ref=source,
            dst_ref=goal,
            send_sem=self.send_sems.at[self.place, stage],
            recv_sem=self.recv_sems.at[self.place, stage],
            device_id=(device,),
            device_id_type=pl.DeviceIdType.MESH,
        )

    def start(self, stage=0):
        for copy in self.copies(stage):
            copy.start()

    def step(self, stage):
        held = self.held[stage]
        whole = self.copy(stage, held, held, self.me + self.links["core"][1])
        whole.wait_send()
        whole.wait_recv()
        if stage < 3:
            for part, (kept, _) in enumerate(self.halves(stage, 0)):
                if stage == 0:
                    held[...] = held[...] + kept[...]
                else:
                    held[part] = held[part] + kept[...]
            self.start(stage + 1)
        else:
            h = self.third
            for part in range(3):
                total = self.quarter(part // 2, 0, 0)[1][part % 2].astype(full)
                for slot in range(3):
                    total = total + self.held[3][part, slot].astype(full)
                self.out[part * h : part * h + h, :] = total


def contrast(points, groups):
    count = points.shape[0]
    inverse = lax.rsqrt(jnp.sum(points * points, axis=1, keepdims=True) + unit_epsilon)
    unit = points * inverse
    similar = cosine_scale * lax.dot_general(
        unit,
        unit,
        (((1,), (1,)), ((), ())),
        precision=lax.Precision.HIGHEST,
        preferred_element_type=full,
    )
    rows = lax.broadcasted_iota(jnp.int32, (count, count), 0)
    columns = lax.broadcasted_iota(jnp.int32, (count, count), 1)
    itself = rows == columns
    logits = jnp.where(itself, -1e30, similar)
    summit = jnp.max(logits, axis=1, keepdims=True)
    raised = jnp.exp(logits - summit)
    totals = jnp.sum(raised, axis=1, keepdims=True)
    chances = raised / totals
    log_total = summit + jnp.log(totals)
    across = jnp.broadcast_to(groups, (count, count))
    matched = jnp.where(
        jnp.logical_and(across == across.T, jnp.logical_not(itself)), 1.0, 0.0
    )
    weights = matched / jnp.maximum(jnp.sum(matched, axis=1, keepdims=True), 1.0)
    row_mass = jnp.sum(weights, axis=1, keepdims=True)
    loss_rows = row_mass * log_total - jnp.sum(weights * similar, axis=1, keepdims=True)
    loss = jnp.sum(loss_rows, axis=0, keepdims=True)
    coupling = row_mass * chances - weights
    unit_grad = cosine_scale * lax.dot_general(
        coupling + coupling.T,
        unit,
        (((1,), (0,)), ((), ())),
        precision=lax.Precision.HIGHEST,
        preferred_element_type=full,
    )
    grad = inverse * (unit_grad - unit * jnp.sum(unit * unit_grad, axis=1, keepdims=True))
    return loss, grad


def backward_kernel(
    devices,
    sentences,
    pooled,
    live_mean,
    first_gain,
    second_gain,
    groups,
    activated_t_in,
    slopes_in,
    second_normed_in,
    second_inverse_in,
    hidden_t_in,
    first_normed_in,
    first_inverse_in,
    mixture_t_in,
    queries_t_in,
    keys_t_in,
    values_in,
    tokens_t_in,
    probs_in,
    inverse_totals_in,
    query_weight,
    key_weight,
    value_weight,
    output_weight,
    inner_weight,
    outer_weight,
    packed_out,
    loss_out,
    outer_out,
    inner_out,
    square_out,
    sums_out,
    act_t,
    inner_grad,
    w_rows,
    w_columns,
    normed,
    grads,
    branch,
    hidden_t,
    inverses,
    inverse_totals,
    own,
    gathered,
    outer_send,
    outer_0,
    outer_1,
    outer_2,
    outer_3,
    inner_send,
    inner_0,
    inner_1,
    inner_2,
    inner_3,
    square_1,
    square_2,
    square_3,
    sum_held,
    sum_recv,
    late_held,
    late_recv,
    load_sems,
    prob_sems,
    gather_sems,
    set_send,
    set_recv,
    sum_sems,
    credit,
):
    me = lax.axis_index("dp")
    rows, width = normed.shape
    slots = rows // sentences
    parts, _, wide = inner_grad.shape
    heads = width // HD
    own_rows = width // devices

    def link(mask):
        bit = lax.rem(lax.div(me, mask), 2)
        return bit, mask * (1 - 2 * bit)

    links = {"core": link(1), "x": link(2), "y": link(4), "z0": link(8), "z1": link(16)}
    load_count = iter(range(44))

    def load(source, target):
        copy = pltpu.make_async_copy(source, target, load_sems.at[next(load_count)])
        copy.start()
        return copy

    get_normed = load(second_normed_in, normed)
    get_second = load(second_inverse_in, inverses)
    get_act = load(activated_t_in, act_t)
    get_outer = load(outer_weight, w_rows)
    get_slopes = [load(slopes_in.at[part], inner_grad.at[part]) for part in range(parts)]
    get_hidden = load(hidden_t_in, hidden_t)
    get_inner = load(inner_weight, w_columns)
    get_totals = load(inverse_totals_in, inverse_totals)

    barrier = pltpu.get_barrier_semaphore()

    def greet(step, carry):
        other = lax.rem(me + step, devices)
        pl.semaphore_signal(
            barrier, inc=1, device_id=(other,), device_id_type=pl.DeviceIdType.MESH
        )
        return carry

    lax.fori_loop(1, devices, greet, 0)
    blocks = width // 128
    cut = [
        pooled[sentence, 0:1, block * 128 : (block + 1) * 128]
        for block in range(blocks)
        for sentence in range(sentences)
    ]
    cut.append(jnp.zeros((own.shape[0] - len(cut), 128), full))
    own[...] = jnp.concatenate(cut, axis=0).astype(low)
    gathered[me] = own[...]
    pl.semaphore_wait(barrier, devices - 1)

    def gather_copy(step):
        return pltpu.make_async_remote_copy(
            src_ref=own,
            dst_ref=gathered.at[me],
            send_sem=gather_sems.at[0],
            recv_sem=gather_sems.at[1],
            device_id=(lax.rem(me + step, devices),),
            device_id_type=pl.DeviceIdType.MESH,
        )

    def gather_start(step, carry):
        gather_copy(step).start()
        return carry

    lax.fori_loop(1, devices, gather_start, 0)
    others = gathered.at[pl.ds(0, devices - 1)]
    whole = pltpu.make_async_remote_copy(
        src_ref=others,
        dst_ref=others,
        send_sem=gather_sems.at[0],
        recv_sem=gather_sems.at[1],
        device_id=(lax.rem(me + 1, devices),),
        device_id_type=pl.DeviceIdType.MESH,
    )
    whole.wait_send()
    whole.wait_recv()
    everyone = gathered[...].reshape(devices * own.shape[0], 128)
    shape = (devices * sentences, devices * own.shape[0])
    row_ids = lax.broadcasted_iota(jnp.int32, shape, 0)
    source = lax.div(row_ids, sentences) * own.shape[0] + lax.rem(row_ids, sentences)
    column_ids = lax.broadcasted_iota(jnp.int32, shape, 1)
    points = jnp.concatenate(
        [
            dot(
                jnp.where(column_ids == source + block * sentences, 1.0, 0.0).astype(low), everyone
            )
            for block in range(blocks)
        ],
        axis=1,
    )
    loss, pooled_grad = contrast(
        points, groups[...].astype(full).reshape(1, groups.shape[0])
    )
    loss_out[...] = jnp.broadcast_to(loss, loss_out.shape)
    row_ids = lax.broadcasted_iota(jnp.int32, (devices * sentences, width), 0)
    own_grads = [
        jnp.sum(
            jnp.where(row_ids == me * sentences + sentence, pooled_grad, 0.0),
            axis=0,
            keepdims=True,
        )
        for sentence in range(sentences)
    ]
    vector_sums = sum_held.at[0]
    vector_sums[...] = jnp.zeros_like(vector_sums)
    vector_sums[1:2, :] = sum(
        own_grads[sentence] * live_mean[sentence, 0:1, :] for sentence in range(sentences)
    )
    vector_sums[2:3, :] = sum(own_grads)

    sets = {}

    def add_set(name, send, held, out):
        sets[name] = Summation(name, send, held, out, (set_send, set_recv), me, links)

    def columns(ref, start, size):
        return ref.at[(slice(None),) * (len(ref.shape) - 1) + (pl.ds(start, size),)]

    third = width // 3
    for part in range(3):
        lanes = (part * third, third)
        add_set(
            f"A{part}",
            columns(outer_send, *lanes),
            [columns(r, *lanes) for r in (outer_0, outer_1, outer_2, outer_3)],
            columns(outer_out, *lanes),
        )
        half = wide // 2
        lanes = (part * half, half)
        add_set(
            f"B{part}",
            columns(inner_send, *lanes),
            [columns(r, *lanes) for r in (inner_0, inner_1, inner_2, inner_3)],
            columns(inner_out, *lanes),
        )
    piece_rows, piece_columns = outer_send.shape[-2] // 2, width // 2
    square_sends = [
        outer_send.at[
            :,
            :,
            :,
            :,
            :,
            pl.ds(place % 2 * piece_rows, piece_rows),
            pl.ds(place // 2 * piece_columns, piece_columns),
        ]
        for place in range(4)
    ]
    for place in range(4):
        first = outer_0.at[
            :,
            :,
            :,
            :,
            pl.ds(place % 2 * piece_rows, piece_rows),
            pl.ds(place // 2 * piece_columns, piece_columns),
        ]
        add_set(
            f"C{place}",
            square_sends[place],
            [first] + [r.at[place] for r in (square_1, square_2, square_3)],
            square_out.at[place],
        )
    second_done, done = [], []

    def step_set(name, stage):
        sets[name].step(stage)
        if stage == 3:
            done.append(name)
        if name[0] == "A" and stage == 1:
            second_done.append(name)
            if len(second_done) == 3:
                pl.semaphore_signal(
                    credit,
                    inc=1,
                    device_id=(me + links["core"][1],),
                    device_id_type=pl.DeviceIdType.MESH,
                )

    def tick(point):
        for name, stage in SCHEDULE.get(point, ()):
            step_set(name, stage)

    def piece_at(device):
        return device // 16, device // 8 % 2, device // 4 % 2, device // 2 % 2, device % 2

    get_normed.wait()
    get_second.wait()
    bias_sum = jnp.zeros((8, width), full)
    step = 32
    for sentence in range(sentences):
        scaled = own_grads[sentence] * second_gain[...].reshape(1, width)
        shifted = scaled - jnp.mean(scaled, axis=1, keepdims=True)

        def second_back(index, total):
            at = pl.ds(pl.multiple_of(sentence * slots + index * step, step), step)
            unit = normed[at, :]
            mass = jnp.mean(unit * scaled, axis=1, keepdims=True)
            grad = widen(inverses[at, :], width) * (shifted - unit * mass)
            grads[at, :] = grad
            rounded = grad.astype(low)
            branch[at, :] = rounded
            return total + jnp.sum(
                rounded.astype(full).reshape(step // 8, 8, width), axis=0
            )

        bias_sum = lax.fori_loop(0, slots // step, second_back, bias_sum)
    vector_sums[0:1, :] = jnp.sum(bias_sum, axis=0, keepdims=True)
    get_normed_2 = load(first_normed_in, normed)
    get_first = load(first_inverse_in, inverses)

    get_act.wait()
    piece = outer_send.shape[-2]
    for part in range(3):
        right = branch[:, part * third : (part + 1) * third]
        for block in range(4):
            result = dot(act_t[block * 8 * piece : (block + 1) * 8 * piece, :], right).astype(low)
            for place in range(8):
                sets[f"A{part}"].send[piece_at(block * 8 + place)] = result[
                    place * piece : (place + 1) * piece, :
                ]
        sets[f"A{part}"].start()
        tick(f"a{part}")

    get_values = load(values_in, act_t.at[0:rows, 0:width])
    steps = heads // 2 * sentences

    def prob_slot(index, half):
        start = pl.multiple_of(rows + lax.rem(index, 4) * slots, slots)
        return act_t.at[pl.ds(start, slots), half * slots : (half + 1) * slots]

    def prob_copies(index):
        first = lax.rem(index, sentences) * heads + lax.div(index, sentences) * 2
        return [
            pltpu.make_async_copy(
                probs_in.at[first + half],
                prob_slot(index, half),
                prob_sems.at[lax.rem(index, 4), half],
            )
            for half in range(2)
        ]

    for index in range(3):
        for copy in prob_copies(index):
            copy.start()

    get_outer.wait()
    get_hidden.wait()
    block, step = wide // 2, 32

    def slope_dot(index):
        return dot(branch[...], w_rows[index * block : (index + 1) * block, :], 1, 1)

    def slope_block(index, result):
        part, lanes = index // 2, slice(index % 2 * block, (index % 2 + 1) * block)
        total = jnp.zeros((8, block), full)
        for place in range(0, rows, step):
            at = slice(place, place + step)
            value = (result[at] * inner_grad[part, at, lanes].astype(full)).astype(low)
            inner_grad[part, at, lanes] = value
            total = total + jnp.sum(value.astype(full).reshape(step // 8, 8, block), axis=0)
        total = jnp.sum(total, axis=0, keepdims=True)
        for piece in range(0, block, 256):
            flat = index * block + piece
            row, lane = 8 + flat // width, flat % width
            vector_sums[row : row + 1, lane : lane + 256] = total[:, piece : piece + 256]

    before = slope_dot(0)
    for index in range(2 * parts):
        part = index // 2
        result = slope_dot(index + 1) if index + 1 < 2 * parts else None
        if index % 2 == 0:
            get_slopes[part].wait()
        slope_block(index, before)
        before = result
        if index % 2 == 0:
            tick(f"e{part}")
            continue
        tick(f"g{part}")
        for piece in range(2):
            result = dot(
                hidden_t[piece * (width // 2) : (piece + 1) * (width // 2), :], inner_grad[part]
            )
            for place in range(devices // 2):
                value = result[place * own_rows : (place + 1) * own_rows]
                sets[f"B{part}"].send[piece_at(piece * (devices // 2) + place)] = jnp.concatenate(
                    [value[:, : wide // 2], value[:, wide // 2 :]], axis=0
                ).astype(low)
        sets[f"B{part}"].start()
        tick(f"w{part}")
    mixture_t = hidden_t
    get_mixture = load(mixture_t_in, mixture_t)
    square_loads = [
        load(source, w_rows.at[pl.ds(place * width, width)])
        for place, source in enumerate((output_weight, query_weight, key_weight, value_weight))
    ]

    get_inner.wait()
    get_normed_2.wait()
    get_first.wait()
    span, step = rows // 4, 32
    gain = first_gain[...].reshape(1, width)

    def hidden_dot(start):
        total = None
        for part in range(parts):
            term = dot(
                inner_grad[part, start : start + span, :],
                w_columns[:, part * wide : (part + 1) * wide],
                1,
                1,
            )
            total = term if total is None else total + term
        return total

    def first_back(start, total, gain_sum, shift_sum, bias_sum):
        for place in range(0, span, step):
            at = slice(start + place, start + place + step)
            upstream = grads[at, :] + total[place : place + step]
            unit = normed[at, :]
            gain_sum = gain_sum + jnp.sum((upstream * unit).reshape(step // 8, 8, width), axis=0)
            shift_sum = shift_sum + jnp.sum(upstream.reshape(step // 8, 8, width), axis=0)
            scaled = upstream * gain
            center = scaled - jnp.mean(scaled, axis=1, keepdims=True)
            grad = widen(inverses[at, :], width) * (
                center - unit * jnp.mean(scaled * unit, axis=1, keepdims=True)
            )
            grads[at, :] = grad
            rounded = grad.astype(low)
            branch[at, :] = rounded
            bias_sum = bias_sum + jnp.sum(
                rounded.astype(full).reshape(step // 8, 8, width), axis=0
            )
        return gain_sum, shift_sum, bias_sum

    zero = jnp.zeros((8, width), full)
    state = (zero, zero, zero)
    before = hidden_dot(0)
    for index in range(4):
        result = hidden_dot((index + 1) * span) if index < 3 else None
        state = first_back(index * span, before, *state)
        before = result
        tick(f"h{index}")
    for place, total in zip((3, 4, 5), state):
        vector_sums[place : place + 1, :] = jnp.sum(total, axis=0, keepdims=True)

    get_queries = load(queries_t_in, w_columns.at[:, 0:rows])
    get_keys = load(keys_t_in, w_columns.at[:, rows : 2 * rows])
    tokens_t = inner_grad.at[1, 0:width, :]
    get_tokens = load(tokens_t_in, tokens_t)

    def square_pieces(place, index, result):
        lanes = pl.ds(index * 128, 128)
        for device in range(devices):
            at = slice(device * own_rows, (device + 1) * own_rows)
            z1, z0, y, x, core = piece_at(device)
            square_sends[place].at[z1, z0, y, x, core][:, lanes] = jnp.concatenate(
                [result[at, 0:128], result[at, 128:256]], axis=0
            ).astype(low)

    get_mixture.wait()
    for index in range(3):
        square_pieces(0, index, dot(mixture_t[...], branch[:, index * 256 : (index + 1) * 256]))
    pl.semaphore_wait(credit, 1)
    sets["C0"].start()
    tick("o")

    def start_sums(group, stage):
        for copy in sum_copies(group, stage)[1:]:
            copy.start()

    def sum_copies(group, stage):
        held, arrived, sems = group
        core, x, y, z0, z1 = (links[name][1] for name in ("core", "x", "y", "z0", "z1"))
        moves = ((core,), (x, y, x + y), (z0, z1, z0 + z1))[stage]
        base = (0, 1, 4)[stage]

        def copy(source, goal, move):
            return pltpu.make_async_remote_copy(
                src_ref=source,
                dst_ref=goal,
                send_sem=sems.at[stage, 0],
                recv_sem=sems.at[stage, 1],
                device_id=(me + move,),
                device_id_type=pl.DeviceIdType.MESH,
            )

        whole = arrived.at[pl.ds(base, len(moves))]
        return [copy(whole, whole, core)] + [
            copy(held.at[stage], arrived.at[base + index], move)
            for index, move in enumerate(moves)
        ]

    def sum_step(group, stage):
        held, arrived, _ = group
        copies = sum_copies(group, stage)
        copies[0].wait_send()
        copies[0].wait_recv()
        total = held[stage]
        for index in range(len(copies) - 1):
            total = total + arrived[(0, 1, 4)[stage] + index]
        if stage < 2:
            held[stage + 1] = total
            start_sums(group, stage + 1)
        elif group is early_sums:
            sums_out[...] = total
        else:
            sums_out[6:7, :] = total

    early_sums = (sum_held, sum_recv, sum_sems.at[0])
    late_sums = (late_held, late_recv, sum_sems.at[1])

    square_loads[0].wait()
    bias_row = vector_sums[5:6, :]
    upper = bias_row.astype(low)
    lower = (bias_row - upper.astype(full)).astype(low)
    split = jnp.concatenate([upper, lower, jnp.zeros((14, width), low)], axis=0)
    split = dot(split, w_rows[0:width, :], 1, 1)
    vector_sums[7:8, :] = split[0:1, :] + split[1:2, :]
    start_sums(early_sums, 0)
    get_totals.wait()
    upstream_t = inner_grad.at[0, 0:width, :]
    for sentence in range(sentences):
        spans = slice(sentence * slots, (sentence + 1) * slots)
        result = dot(w_rows[0:width, :], branch[spans, :], 1, 1)
        for head in range(heads):
            at = slice(head * HD, (head + 1) * HD)
            place = sentence * heads + head
            value = result[at] * inverse_totals[place, 0:1, :]
            mass = jnp.sum(value * mixture_t[at, spans].astype(full), axis=0, keepdims=True)
            inverse_totals[place] = mass
            upstream_t[at, spans] = value.astype(low)
    tick("m")

    get_queries.wait()
    get_keys.wait()
    get_values.wait()
    get_tokens.wait()
    empty = jnp.zeros((HD, slots), low)
    value_grads, key_grads = act_t.at[0:rows, 0:width], branch
    toward_refs = [normed.at[at : at + slots, 0:slots] for at in (0, slots)]
    score_refs = [inner_grad.at[2, at : at + slots, 0:slots] for at in (0, slots)]

    def projection_grads(group):
        at = slice(group * 256, (group + 1) * 256)
        left = tokens_t[...]
        square_pieces(1 + group, 0, dot(left, w_columns[at, 0:rows], 1, 1) * 0.125)
        square_pieces(1 + group, 1, dot(left, key_grads[:, at]))
        square_pieces(1 + group, 2, dot(left, value_grads[:, at]))
        sets[f"C{1 + group}"].start()

    def head_pair(index, carry):
        pair, sentence = lax.div(index, sentences), lax.rem(index, sentences)
        start = pl.multiple_of(pair * 128, 128)
        spans = pl.ds(pl.multiple_of(sentence * slots, slots), slots)
        key_spans = pl.ds(pl.multiple_of(rows + sentence * slots, slots), slots)
        for copy in prob_copies(index):
            copy.wait()

        @pl.when(index + 3 < steps)
        def _():
            for copy in prob_copies(index + 3):
                copy.start()

        def row(half):
            return pl.ds(pl.multiple_of(start + half * HD, HD), HD)

        def masked(half, value):
            return jnp.concatenate([value, empty] if half == 0 else [empty, value], axis=0)

        def toward(half):
            upstream = masked(half, upstream_t[row(half), spans])
            toward_refs[half][...] = dot(value_grads[spans, pl.ds(start, 128)], upstream)
            return dot(prob_slot(index, half)[...], upstream.T)

        def scores(half):
            mass = inverse_totals[sentence * heads + pair * 2 + half, 0:1, :]
            prob = prob_slot(index, half)
            result = toward_refs[half]
            for piece in range(0, slots, 64):
                at = slice(piece, piece + 64)
                score_refs[half][at, :] = (
                    prob[at, :].astype(full) * (result[at, :] - mass)
                ).astype(low)

        def finish(half):
            score = score_refs[half][...]
            query = w_columns[row(half), spans]
            key = w_columns[row(half), key_spans]
            key_grad = dot(score, masked(half, query).T)
            w_columns[row(half), spans] = dot(key, score).astype(low)
            return key_grad

        value_grad = toward(0)
        value_grad = value_grad + toward(1)
        scores(0)
        key_grad = finish(0)
        scores(1)
        key_grad = key_grad + finish(1)
        key_grads[spans, pl.ds(start, 128)] = key_grad.astype(low)
        value_grads[spans, pl.ds(start, 128)] = value_grad.astype(low)
        per_group = steps // 3
        for when in range(steps):
            last = when % per_group == per_group - 1
            vector_stage = {5: 0, 11: 1}.get(when)
            if not last and vector_stage is None and f"s{when}" not in SCHEDULE:
                continue

            def after(when=when, last=last, vector_stage=vector_stage):
                tick(f"s{when}")
                if vector_stage is not None:
                    sum_step(early_sums, vector_stage)
                if last:
                    projection_grads(when // per_group)
                    tick(f"c{when // per_group}")

            pl.when(index == when)(after)
        return carry

    lax.fori_loop(0, steps, head_pair, 0)

    late_held[0] = 0.125 * dot(jnp.ones((8, rows), low), w_columns[:, 0:rows], 1, 1)[0:1, :]
    start_sums(late_sums, 0)

    for copy in square_loads[1:]:
        copy.wait()

    outs = []
    finished = []

    def pack(source, start, lane=0):
        size, lanes = source.shape
        outs.append(
            load(source, packed_out.at[pl.ds(rows + start, size), pl.ds(lane, lanes)])
        )

    def pack_finished():
        for name in sets:
            if name in done and name not in finished:
                finished.append(name)
                place = int(name[1])
                if name[0] == "A":
                    pack(columns(outer_out, place * third, third), 0, place * third)
                elif name[0] == "B":
                    half = wide // 2
                    for piece in range(0, half, 256):
                        lane = place * half + piece
                        pack(
                            columns(inner_out, lane, 256),
                            outer_out.shape[0] + lane // width * inner_out.shape[0],
                            lane % width,
                        )
                else:
                    size = square_out.shape[1]
                    pack(square_out.at[place], square_at + place // 2 * size, place % 2 * (width // 2))

    sums_at = outer_out.shape[0] + 2 * inner_out.shape[0]
    square_at = sums_at + sums_out.shape[0] + loss_out.shape[0]
    pack(loss_out, sums_at + sums_out.shape[0])
    turn = 0
    span = rows // 2
    for index, start in enumerate(range(0, rows, span)):
        at = slice(start, start + span)
        total = grads[at, :] + 0.125 * dot(w_columns[:, at], w_rows[width : 2 * width, :], 0, 1)
        for place, terms in ((2, key_grads), (3, value_grads)):
            tick(f"t{turn}")
            if turn == 3:
                sum_step(early_sums, 2)
            if turn in (1, 4):
                sum_step(late_sums, turn // 3)
            turn += 1
            total = total + dot(
                terms[at, :], w_rows[place * width : (place + 1) * width, :], 1, 1
            )
        grads[at, :] = total
        outs.append(load(grads.at[at], packed_out.at[at]))
        tick(f"t{turn}")
        turn += 1
        pack_finished()
    for name, stage in SCHEDULE["end"]:
        if (name, stage) == SCHEDULE["end"][-1]:
            sum_step(late_sums, 2)
            pack(sums_out, sums_at)
        step_set(name, stage)
        pack_finished()
    for copy in outs:
        copy.wait()


def finish_kernel(
    devices,
    packed,
    loss_out,
    token_grad_out,
    query_out,
    query_bias,
    key_out,
    value_out,
    value_bias,
    output_out,
    output_bias,
    first_gain,
    first_shift,
    inner_out,
    inner_bias,
    outer_out,
    outer_bias,
    second_gain,
    second_shift,
    square_held,
    sums_held,
    sems,
):
    me = lax.axis_index("dp")
    rows, width = token_grad_out.shape
    own = query_out.shape[0]
    copies = []

    def move(source, target):
        copy = pltpu.make_async_copy(source, target, sems.at[len(copies)])
        copy.start()
        copies.append(copy)
        return copy

    outer_at = rows
    inner_at = outer_at + outer_out.shape[0]
    sums_at = inner_at + 4 * own
    square_at = sums_at + 24
    get_sums = move(packed.at[pl.ds(sums_at, 24)], sums_held)
    get_square = move(packed.at[pl.ds(square_at, 4 * own)], square_held)
    for start in range(0, rows, rows // 4):
        at = pl.ds(start, rows // 4)
        move(packed.at[at], token_grad_out.at[at])
    move(packed.at[pl.ds(outer_at, outer_out.shape[0])], outer_out)
    part = inner_out.shape[1] // 6
    for index in range(6):
        lane = index // 2 * part
        for piece in range(0, part, 256):
            first = lane + piece
            start = inner_at + first // width * 2 * own + index % 2 * own
            move(
                packed.at[pl.ds(start, own), pl.ds(first % width, 256)],
                inner_out.at[:, pl.ds(index * part + piece, 256)],
            )
    source = lax.broadcasted_iota(jnp.int32, (width, 128), 0)
    lane = lax.broadcasted_iota(jnp.int32, (width, 128), 1)

    def pick(values, start):
        chosen = jnp.where(source == lane + start, 1.0, 0.0)
        return lax.dot_general(
            values,
            chosen,
            (((1,), (0,)), ((), ())),
            precision=lax.Precision.HIGHEST,
            preferred_element_type=full,
        )

    get_sums.wait()
    picked = pick(sums_held[0:8, :], me * own)
    for place, ref in enumerate(
        (
            outer_bias,
            second_gain,
            second_shift,
            first_gain,
            first_shift,
            output_bias,
            query_bias,
            value_bias,
        )
    ):
        ref[...] = picked[place : place + 1, 0 : ref.shape[1]]
    wide = inner_bias.shape[1]
    per_row = width // wide
    row_ids = lax.broadcasted_iota(jnp.int32, (8, width), 0)
    chosen = jnp.sum(
        jnp.where(row_ids == lax.div(me, per_row), sums_held[8:16, :], 0.0),
        axis=0,
        keepdims=True,
    )
    inner_bias[...] = pick(jnp.broadcast_to(chosen, (8, width)), lax.rem(me, per_row) * wide)[
        0:1, 0:wide
    ]
    get_square.wait()
    half = width // 2

    def square(place, lower):
        start = place // 2 * 2 * own + lower * own
        return square_held[start : start + own, place % 2 * half : (place % 2 + 1) * half]

    def place_columns(target, column, place, index):
        lanes = slice(index * 128, (index + 1) * 128)
        for lower in range(2):
            at = column + lower * 128
            target[:, at : at + 128] = square(place, lower)[:, lanes]

    for index in range(3):
        place_columns(output_out, index * 256, 0, index)
        for place, target in enumerate((query_out, key_out, value_out)):
            place_columns(target, index * 256, 1 + index, place)
    loss_out[...] = sums_held[16:17, 0:1]
    for copy in copies[2:]:
        copy.wait()


def linked_device(
    devices,
    tokens,
    lengths,
    groups,
    query_weight,
    query_bias,
    key_weight,
    value_weight,
    value_bias,
    output_weight,
    output_bias,
    first_gain,
    first_shift,
    inner_weight,
    inner_bias,
    outer_weight,
    outer_bias,
    second_gain,
    second_shift,
):
    sentences = lengths.shape[0]
    rows, width = tokens.shape
    slots = rows // sentences
    inner = inner_weight.shape[1]
    vectors = (
        query_bias,
        value_bias,
        output_bias,
        first_gain,
        first_shift,
        outer_bias,
        second_gain,
        second_shift,
    )
    weights = (query_weight, key_weight, value_weight, output_weight, inner_weight, outer_weight)
    (
        layer_output,
        pooled,
        live_mean,
        queries_t,
        keys_t,
        values,
        mixture_t,
        tokens_t,
        probs,
        inverse_totals,
        first_normed,
        first_inverse,
        hidden_t,
        second_normed,
        second_inverse,
        activated_t,
        slopes,
    ) = forward(lengths, tokens, vectors, inner_bias[None], weights)
    hbm = pl.BlockSpec(memory_space=pl.ANY)
    vmem = pl.BlockSpec(memory_space=pltpu.VMEM)
    shape = jax.ShapeDtypeStruct
    piece_outer = (inner // devices, width)
    piece_inner = (2 * width // devices, inner // 2)
    piece_square = (2 * width // devices, width // 2)

    def levels(piece, lead=()):
        third = (piece[0] // 3, piece[1])
        shapes = [(2,) * 5 + piece, (2,) * 4 + piece]
        shapes += [(3,) + (2,) * k + third for k in (3, 2)] + [(3, 3) + third]
        return [pltpu.VMEM(lead + s, low) for s in shapes]

    sets = len(SETS)
    extra = piece_outer[0] + 2 * piece_inner[0] + 16 + 8 + 2 * piece_square[0]
    packed = pl.pallas_call(
        functools.partial(backward_kernel, devices, sentences),
        in_specs=[vmem] * 5 + [hbm] * 20,
        out_specs=hbm,
        out_shape=shape((rows + extra, width), full),
        scratch_shapes=[
            pltpu.VMEM((8, width), full),
            pltpu.VMEM(piece_outer, full),
            pltpu.VMEM(piece_inner, full),
            pltpu.VMEM((4,) + piece_square, full),
            pltpu.VMEM((16, width), full),
            pltpu.VMEM(activated_t.shape, low),
            pltpu.VMEM(slopes.shape, low),
            pltpu.VMEM((inner, width), low),
            pltpu.VMEM((width, inner), low),
            pltpu.VMEM((rows, width), full),
            pltpu.VMEM((rows, width), full),
            pltpu.VMEM((rows, width), low),
            pltpu.VMEM((width, rows), low),
            pltpu.VMEM((rows, 128), full),
            pltpu.VMEM(inverse_totals.shape, full),
            pltpu.VMEM((16, 128), low),
            pltpu.VMEM((devices, 16, 128), low),
        ]
        + levels(piece_outer)
        + levels(piece_inner)
        + levels(piece_square, (4,))[2:]
        + [
            pltpu.VMEM((3, 16, width), full),
            pltpu.VMEM((7, 16, width), full),
            pltpu.VMEM((3, 1, width), full),
            pltpu.VMEM((7, 1, width), full),
            pltpu.SemaphoreType.DMA((44,)),
            pltpu.SemaphoreType.DMA((4, 2)),
            pltpu.SemaphoreType.DMA((2,)),
            pltpu.SemaphoreType.DMA((sets, 4)),
            pltpu.SemaphoreType.DMA((sets, 4)),
            pltpu.SemaphoreType.DMA((2, 3, 2)),
            pltpu.SemaphoreType.REGULAR,
        ],
        compiler_params=pltpu.CompilerParams(
            collective_id=0, has_side_effects=True, vmem_limit_bytes=63 * MIB
        ),
        name="decode",
    )(
        pooled,
        live_mean,
        first_gain,
        second_gain,
        groups,
        activated_t,
        slopes,
        second_normed,
        second_inverse,
        hidden_t,
        first_normed,
        first_inverse,
        mixture_t,
        queries_t,
        keys_t,
        values,
        tokens_t,
        probs,
        inverse_totals,
        *weights,
    )
    own = width // devices
    finals = pl.pallas_call(
        functools.partial(finish_kernel, devices),
        out_shape=[
            shape((1, 1), full),
            shape((rows, width), full),
            shape((own, width), full),
            shape((1, own), full),
            shape((own, width), full),
            shape((own, width), full),
            shape((1, own), full),
            shape((own, width), full),
            shape((1, own), full),
            shape((1, own), full),
            shape((1, own), full),
            shape((own, inner), full),
            shape((1, inner // devices), full),
            shape((inner // devices, width), full),
            shape((1, own), full),
            shape((1, own), full),
            shape((1, own), full),
        ],
        in_specs=[hbm],
        out_specs=[vmem, hbm] + [vmem] * 15,
        scratch_shapes=[
            pltpu.VMEM((2 * piece_square[0], width), full),
            pltpu.VMEM((24, width), full),
            pltpu.SemaphoreType.DMA((20,)),
        ],
        compiler_params=pltpu.CompilerParams(vmem_limit_bytes=32 * MIB),
        name="finish",
    )(packed)
    finals = [f.reshape(f.shape[1:]) if f.shape[0] == 1 else f for f in finals]
    return (finals[0].reshape(()), layer_output, *finals[1:])


highest = lax.Precision.HIGHEST


def project(operand, weight):
    return jnp.dot(operand, weight, preferred_element_type=jnp.float32)


def transpose_left(left_rows, right_rows):
    return lax.dot_general(
        left_rows, right_rows, (((0,), (0,)), ((), ())), preferred_element_type=jnp.float32
    )


def transpose_right(operand, weight):
    return lax.dot_general(
        operand, weight, (((1,), (1,)), ((), ())), preferred_element_type=jnp.float32
    )


def standardize(residual):
    center = residual - jnp.mean(residual, axis=-1, keepdims=True)
    inverse = lax.rsqrt(jnp.mean(center * center, axis=-1, keepdims=True) + layer_epsilon)
    return (center * inverse, inverse)


def standardize_back(upstream, normed, inverse, scaling):
    scaled = upstream * scaling
    return inverse * (
        scaled
        - jnp.mean(scaled, axis=-1, keepdims=True)
        - normed * jnp.mean(scaled * normed, axis=-1, keepdims=True)
    )


def gelu_slope(inner_pre):
    cumulative = 0.5 * (1.0 + lax.erf(inner_pre * (1.0 / math.sqrt(2.0))))
    density = jnp.exp(-0.5 * inner_pre * inner_pre) * (1.0 / math.sqrt(2.0 * math.pi))
    return cumulative + inner_pre * density


def masked_scores(queries, key_rows, key_live):
    scores = jnp.einsum("qhd,khd->hqk", queries, key_rows, preferred_element_type=jnp.float32)
    return jnp.where(key_live[None, None, :], scores, -1e30)


def attend(pieces):
    queries, key_rows, value_rows, key_live = pieces
    scores = masked_scores(queries, key_rows, key_live)
    summit = jnp.max(scores, axis=-1, keepdims=True)
    raised = jnp.exp(scores - summit)
    totals = jnp.sum(raised, axis=-1, keepdims=True)
    weights = (raised / totals).astype(jnp.bfloat16)
    mixture = jnp.einsum("hqk,khd->qhd", weights, value_rows, preferred_element_type=jnp.float32)
    return (mixture.astype(jnp.bfloat16), (summit + jnp.log(totals))[..., 0])


def attend_back(pieces):
    queries, key_rows, value_rows, key_live, log_total, upstream = pieces
    scores = masked_scores(queries, key_rows, key_live)
    chances = jnp.exp(scores - log_total[..., None])
    toward = jnp.einsum("qhd,khd->hqk", upstream, value_rows, preferred_element_type=jnp.float32)
    score_grad = (chances * (toward - jnp.sum(chances * toward, axis=-1, keepdims=True))).astype(
        jnp.bfloat16
    )
    value_grad = jnp.einsum(
        "hqk,qhd->khd", chances.astype(jnp.bfloat16), upstream, preferred_element_type=jnp.float32
    )
    query_grad = jnp.einsum(
        "hqk,khd->qhd", score_grad, key_rows, preferred_element_type=jnp.float32
    )
    key_grad = jnp.einsum("hqk,qhd->khd", score_grad, queries, preferred_element_type=jnp.float32)
    return (
        query_grad.astype(jnp.bfloat16),
        key_grad.astype(jnp.bfloat16),
        value_grad.astype(jnp.bfloat16),
    )


def contrast_rows(row_unit, unit_rows, row_groups, groups, row_start):
    similar = cosine_scale * lax.dot_general(
        row_unit, unit_rows, (((1,), (1,)), ((), ())), precision=highest
    )
    row_ids = row_start + jnp.arange(row_unit.shape[0])
    column_ids = jnp.arange(unit_rows.shape[0])
    itself = row_ids[:, None] == column_ids[None, :]
    logits = jnp.where(itself, -1e30, similar)
    summit = jnp.max(logits, axis=-1, keepdims=True)
    raised = jnp.exp(logits - summit)
    totals = jnp.sum(raised, axis=-1, keepdims=True)
    chances = raised / totals
    log_total = summit + jnp.log(totals)
    matched = jnp.logical_and(
        row_groups[:, None] == groups[None, :], jnp.logical_not(itself)
    ).astype(jnp.float32)
    weights = matched / jnp.maximum(jnp.sum(matched, axis=-1, keepdims=True), 1.0)
    row_mass = jnp.sum(weights, axis=-1, keepdims=True)
    loss_rows = row_mass[:, 0] * log_total[:, 0] - jnp.sum(weights * similar, axis=-1)
    return (jnp.sum(loss_rows), row_mass * chances - weights)


def per_device(
    tokens,
    lengths,
    groups,
    query_weight,
    query_bias,
    key_weight,
    value_weight,
    value_bias,
    output_weight,
    output_bias,
    first_gain,
    first_shift,
    inner_weight,
    inner_bias,
    outer_weight,
    outer_bias,
    second_gain,
    second_shift,
):
    seq_count = lengths.shape[0]
    slot_count = tokens.shape[0] // seq_count
    model_width = tokens.shape[1]
    heads_shape = (seq_count, slot_count, HEADS, HD)
    queries = ((project(tokens, query_weight) + query_bias) * 0.125).astype(jnp.bfloat16)
    key_rows = project(tokens, key_weight).astype(jnp.bfloat16)
    value_rows = (project(tokens, value_weight) + value_bias).astype(jnp.bfloat16)
    key_live = jnp.arange(slot_count)[None, :] < lengths[:, None]
    head_queries = queries.reshape(heads_shape)
    head_keys = key_rows.reshape(heads_shape)
    head_values = value_rows.reshape(heads_shape)
    mixture, log_total = lax.map(attend, (head_queries, head_keys, head_values, key_live))
    mixture = mixture.reshape(tokens.shape)
    first_normed, first_inverse = standardize(
        tokens.astype(jnp.float32) + project(mixture, output_weight) + output_bias
    )
    hidden = first_normed * first_gain + first_shift
    hidden_low = hidden.astype(jnp.bfloat16)
    inner_pre = project(hidden_low, inner_weight) + inner_bias
    activated = jax.nn.gelu(inner_pre, approximate=False).astype(jnp.bfloat16)
    second_normed, second_inverse = standardize(
        hidden + project(activated, outer_weight) + outer_bias
    )
    output = second_normed * second_gain + second_shift
    live_rows = key_live.astype(jnp.float32)[:, :, None]
    counts = lengths.astype(jnp.float32)[:, None]
    pooled = (
        jnp.sum(output.reshape(seq_count, slot_count, model_width) * live_rows, axis=1) / counts
    ).astype(jnp.bfloat16)
    everyone = lax.all_gather(pooled, "dp", axis=0, tiled=True).astype(jnp.float32)
    inverse_all = lax.rsqrt(jnp.sum(everyone * everyone, axis=-1, keepdims=True) + unit_epsilon)
    unit_rows = everyone * inverse_all
    first_row = lax.axis_index("dp") * seq_count
    own_unit = lax.dynamic_slice_in_dim(unit_rows, first_row, seq_count, 0)
    own_inverse = lax.dynamic_slice_in_dim(inverse_all, first_row, seq_count, 0)
    own_groups = lax.dynamic_slice_in_dim(groups, first_row, seq_count, 0)
    part_loss, coupling = contrast_rows(own_unit, unit_rows, own_groups, groups, first_row)
    loss_value = lax.psum(part_loss, "dp")
    spread = cosine_scale * lax.dot_general(
        coupling, own_unit, (((0,), (0,)), ((), ())), precision=highest
    )
    unit_grad = cosine_scale * jnp.dot(coupling, unit_rows, precision=highest) + lax.psum_scatter(
        spread, "dp", scatter_dimension=0, tiled=True
    )
    pooled_grad = own_inverse * (
        unit_grad - own_unit * jnp.sum(own_unit * unit_grad, axis=-1, keepdims=True)
    )
    grad_output = (pooled_grad[:, None, :] / counts[:, :, None] * live_rows).reshape(tokens.shape)
    second_gain_grad = jnp.sum(grad_output * second_normed, axis=0)
    second_shift_grad = jnp.sum(grad_output, axis=0)
    grad_second = standardize_back(grad_output, second_normed, second_inverse, second_gain)
    branch_grad = grad_second.astype(jnp.bfloat16)
    outer_bias_grad = jnp.sum(branch_grad, axis=0, dtype=jnp.float32)
    outer_weight_grad = transpose_left(activated, branch_grad)
    inner_grad = (transpose_right(branch_grad, outer_weight) * gelu_slope(inner_pre)).astype(
        jnp.bfloat16
    )
    inner_bias_grad = jnp.sum(inner_grad, axis=0, dtype=jnp.float32)
    inner_weight_grad = transpose_left(hidden_low, inner_grad)
    hidden_grad = grad_second + transpose_right(inner_grad, inner_weight)
    first_gain_grad = jnp.sum(hidden_grad * first_normed, axis=0)
    first_shift_grad = jnp.sum(hidden_grad, axis=0)
    grad_first = standardize_back(hidden_grad, first_normed, first_inverse, first_gain)
    attended_grad = grad_first.astype(jnp.bfloat16)
    output_bias_grad = jnp.sum(attended_grad, axis=0, dtype=jnp.float32)
    output_weight_grad = transpose_left(mixture, attended_grad)
    mixture_grad = transpose_right(attended_grad, output_weight).astype(jnp.bfloat16)
    query_grad, key_grad, value_grad = lax.map(
        attend_back,
        (
            head_queries,
            head_keys,
            head_values,
            key_live,
            log_total,
            mixture_grad.reshape(heads_shape),
        ),
    )
    query_grad = query_grad.reshape(tokens.shape)
    key_grad = key_grad.reshape(tokens.shape)
    value_grad = value_grad.reshape(tokens.shape)
    query_weight_grad = 0.125 * transpose_left(tokens, query_grad)
    query_bias_grad = 0.125 * jnp.sum(query_grad, axis=0, dtype=jnp.float32)
    key_weight_grad = transpose_left(tokens, key_grad)
    value_weight_grad = transpose_left(tokens, value_grad)
    value_bias_grad = jnp.sum(value_grad, axis=0, dtype=jnp.float32)
    token_grad = (
        grad_first
        + 0.125 * transpose_right(query_grad, query_weight)
        + transpose_right(key_grad, key_weight)
        + transpose_right(value_grad, value_weight)
    )
    summed = tuple(
        (
            lax.psum_scatter(query_weight_grad, "dp", scatter_dimension=0, tiled=True),
            lax.psum_scatter(query_bias_grad, "dp", scatter_dimension=0, tiled=True),
            lax.psum_scatter(key_weight_grad, "dp", scatter_dimension=0, tiled=True),
            lax.psum_scatter(value_weight_grad, "dp", scatter_dimension=0, tiled=True),
            lax.psum_scatter(value_bias_grad, "dp", scatter_dimension=0, tiled=True),
            lax.psum_scatter(output_weight_grad, "dp", scatter_dimension=0, tiled=True),
            lax.psum_scatter(output_bias_grad, "dp", scatter_dimension=0, tiled=True),
            lax.psum_scatter(first_gain_grad, "dp", scatter_dimension=0, tiled=True),
            lax.psum_scatter(first_shift_grad, "dp", scatter_dimension=0, tiled=True),
            lax.psum_scatter(inner_weight_grad, "dp", scatter_dimension=0, tiled=True),
            lax.psum_scatter(inner_bias_grad, "dp", scatter_dimension=0, tiled=True),
            lax.psum_scatter(outer_weight_grad, "dp", scatter_dimension=0, tiled=True),
            lax.psum_scatter(outer_bias_grad, "dp", scatter_dimension=0, tiled=True),
            lax.psum_scatter(second_gain_grad, "dp", scatter_dimension=0, tiled=True),
            lax.psum_scatter(second_shift_grad, "dp", scatter_dimension=0, tiled=True),
        )
    )
    return (loss_value, output.astype(jnp.bfloat16), token_grad) + summed


def solution(mesh):
    placed = (
        P("dp", None),
        P("dp"),
        P(),
        P(),
        P(),
        P(),
        P(),
        P(),
        P(),
        P(),
        P(),
        P(),
        P(),
        P(),
        P(),
        P(),
        P(),
        P(),
    )
    devices = mesh.shape["dp"]
    body = functools.partial(linked_device, devices) if devices == 32 else per_device
    return jax.shard_map(
        body,
        mesh=mesh,
        in_specs=placed,
        out_specs=(
            P(),
            P("dp", None),
            P("dp", None),
            P("dp", None),
            P("dp"),
            P("dp", None),
            P("dp", None),
            P("dp"),
            P("dp", None),
            P("dp"),
            P("dp"),
            P("dp"),
            P("dp", None),
            P("dp"),
            P("dp", None),
            P("dp"),
            P("dp"),
            P("dp"),
        ),
        check_vma=False,
    )
```
